32 devices in a mesh: dp: 4 (over z), fsdp: 8 (over y, x, core).
Axes of the slice: x: 2, y: 2, z: 4, core: 2. Of those that a mesh axis runs over, the one named last changes fastest.
Arguments:
- tokens: bfloat16 [4096, 2304], P(('dp', 'fsdp')), may hold values from -6 to 6
- query_codes: bfloat16 [2304, 2048], P(('dp', 'fsdp')), may hold values from -128 to 127, as said below
- key_codes: bfloat16 [2304, 1024], P(('dp', 'fsdp')), may hold values from -128 to 127, as said below
- value_codes: bfloat16 [2304, 1024], P(('dp', 'fsdp')), may hold values from -128 to 127, as said below
- output_codes: bfloat16 [2048, 2304], P(('dp', 'fsdp')), may hold values from -128 to 127, as said below
- gate_codes: bfloat16 [2304, 9216], P(('dp', 'fsdp')), may hold values from -128 to 127, as said below
- up_codes: bfloat16 [2304, 9216], P(('dp', 'fsdp')), may hold values from -128 to 127, as said below
- down_codes: bfloat16 [9216, 2304], P(('dp', 'fsdp')), may hold values from -128 to 127, as said below
- query_scale: float32 [2048], P(('dp', 'fsdp')), may hold values from 0.00014 to 0.00056
- key_scale: float32 [1024], P(('dp', 'fsdp')), may hold values from 0.00014 to 0.00056
- value_scale: float32 [1024], P(('dp', 'fsdp')), may hold values from 0.00014 to 0.00056
- output_scale: float32 [2304], P(('dp', 'fsdp')), may hold values from 0.00015 to 0.0006
- gate_scale: float32 [9216], P(('dp', 'fsdp')), may hold values from 0.00014 to 0.00056
- up_scale: float32 [9216], P(('dp', 'fsdp')), may hold values from 0.00014 to 0.00056
- down_scale: float32 [2304], P(('dp', 'fsdp')), may hold values from 7e-05 to 0.00028
- pre_attn_gain: float32 [2304], replicated, may hold values from 0.25 to 1.75
- post_attn_gain: float32 [2304], replicated, may hold values from 0.25 to 1.75
- pre_ffw_gain: float32 [2304], replicated, may hold values from 0.25 to 1.75
- post_ffw_gain: float32 [2304], replicated, may hold values from 0.25 to 1.75
- slot_width: int32 [4, 3], P('dp'), may hold values from 0 to 2, as said below
- slot_live: int32 [4, 3], P('dp'), may hold values from 0 to 1, as said below
- cotangent: bfloat16 [3, 4096, 2304], P(None, ('dp', 'fsdp')), may hold values from -6 to 6
Outputs:
- mixed: bfloat16 [3, 4096, 2304], P(None, ('dp', 'fsdp'))
- input_grad: float32 [4096, 2304], P(('dp', 'fsdp'))
- query_grad: float32 [2304, 2048], P(('dp', 'fsdp'))
- key_grad: float32 [2304, 1024], P(('dp', 'fsdp'))
- value_grad: float32 [2304, 1024], P(('dp', 'fsdp'))
- output_grad: float32 [2048, 2304], P(('dp', 'fsdp'))
- gate_grad: float32 [2304, 9216], P(('dp', 'fsdp'))
- up_grad: float32 [2304, 9216], P(('dp', 'fsdp'))
- down_grad: float32 [9216, 2304], P(('dp', 'fsdp'))
- query_scale_grad: float32 [2048], P(('dp', 'fsdp'))
- key_scale_grad: float32 [1024], P(('dp', 'fsdp'))
- value_scale_grad: float32 [1024], P(('dp', 'fsdp'))
- output_scale_grad: float32 [2304], P(('dp', 'fsdp'))
- gate_scale_grad: float32 [9216], P(('dp', 'fsdp'))
- up_scale_grad: float32 [9216], P(('dp', 'fsdp'))
- down_scale_grad: float32 [2304], P(('dp', 'fsdp'))
- pre_attn_gain_grad: float32 [2304], P(('dp', 'fsdp'))
- post_attn_gain_grad: float32 [2304], P(('dp', 'fsdp'))
- pre_ffw_gain_grad: float32 [2304], P(('dp', 'fsdp'))
- post_ffw_gain_grad: float32 [2304], P(('dp', 'fsdp'))
The draws below stay inside these ranges and needn't reach their ends.
Inputs may be any that keep to these rules, and one draw needn't show every extreme that they name: `query_codes`: whole numbers. `key_codes`: whole numbers. `value_codes`: whole numbers. `output_codes`: whole numbers. `gate_codes`: whole numbers. `up_codes`: whole numbers. `down_codes`: whole numbers. `slot_width`: each row is an ordering of 0, 1 and 2. `slot_live`: each row is a run of ones followed by zeros with at least one one; some row has three ones and some other row exactly one.
All inputs are finite; a program needn't handle non-finite values.
Results may differ from the reference program's by a relative error of at most 0.017.
Values may be sent and summed in bfloat16 or wider, within the bound.
No kernel may reach another device: no remote copies, remote signals or barrier semaphores. Data moves between devices by JAX's collectives and lax.ppermute only.
A program may use at most 1.0625 GiB of HBM per device.

```python
import math
import jax
import jax.numpy as jnp
from jax import lax

D = 2304
FF = 9216
HEADS = 8
KV_HEADS = 4
HD = 256
SLOTS = 3
SEQS = 4
LENGTH = 1024
TOKENS = 4096
QW = 2048
KW = 1024


def code_table(key, rows, columns):
    drawn = jax.random.uniform(key, (rows, columns), jnp.float32, -128.0, 128.0)
    return jnp.clip(jnp.floor(drawn), -128.0, 127.0)


def draw_query_codes(key, part):
    key = jax.random.fold_in(key, 21)
    return code_table(key, D, QW).astype(jnp.bfloat16)


def draw_key_codes(key, part):
    key = jax.random.fold_in(key, 22)
    return code_table(key, D, KW).astype(jnp.bfloat16)


def draw_value_codes(key, part):
    key = jax.random.fold_in(key, 23)
    return code_table(key, D, KW).astype(jnp.bfloat16)


def draw_output_codes(key, part):
    key = jax.random.fold_in(key, 24)
    return code_table(key, QW, D).astype(jnp.bfloat16)


def draw_gate_codes(key, part):
    key = jax.random.fold_in(key, 25)
    return code_table(key, D, FF).astype(jnp.bfloat16)


def draw_up_codes(key, part):
    key = jax.random.fold_in(key, 26)
    return code_table(key, D, FF).astype(jnp.bfloat16)


def draw_down_codes(key, part):
    key = jax.random.fold_in(key, 27)
    return code_table(key, FF, D).astype(jnp.bfloat16)


def slot_plan(key):
    row_keys = jax.random.split(jax.random.fold_in(key, 11), SEQS)
    orders = jax.vmap(lambda sub_key: jax.random.permutation(sub_key, 3))(row_keys)
    counts = jax.random.randint(jax.random.fold_in(key, 12), (SEQS,), 1, 4)
    full_row = jax.random.randint(jax.random.fold_in(key, 13), (), 0, SEQS)
    single_row = (full_row + jax.random.randint(jax.random.fold_in(key, 14), (), 1, SEQS)) % SEQS
    row_ids = jnp.arange(SEQS)
    counts = jnp.where(row_ids == full_row, 3, counts)
    counts = jnp.where(row_ids == single_row, 1, counts)
    return (orders.astype(jnp.int32), counts.astype(jnp.int32))


def draw_slot_width(key, part):
    orders, counts = slot_plan(key)
    return orders


def draw_slot_live(key, part):
    orders, counts = slot_plan(key)
    return (jnp.arange(SLOTS)[None, :] < counts[:, None]).astype(jnp.int32)


def block_scale(rng, dims, cuts, smallest, top_value):
    factor_of, own = 1.0, jax.random.fold_in(rng, 6)
    for dim, shards_of in cuts:
        steps = jnp.exp(jax.random.uniform(jax.random.fold_in(own, dim), (shards_of,), jnp.float32, smallest / len(cuts), top_value / len(cuts)))
        factor_of = factor_of * jnp.repeat(steps, dims[dim] // shards_of).reshape([-1 if axis == dim else 1 for axis in range(len(dims))])
    return factor_of


def centred(rng, dims, deviation, reach, pieces=(), kind=jnp.bfloat16):
    values = deviation * jax.random.normal(rng, dims, jnp.float32)
    if pieces:
        values = values * block_scale(rng, dims, pieces, -0.22, 0.18)
    return jnp.clip(values, -reach, reach).astype(kind)


def setup_inputs(seed: int = 0) -> dict:
    keys = jax.random.split(jax.random.key(seed), 23)
    return {
        "tokens": centred(keys[0], (TOKENS, D), 1.0, 6.0, ((0, 32),)),
        "query_codes": draw_query_codes(jax.random.fold_in(keys[22], 71), 0),
        "key_codes": draw_key_codes(jax.random.fold_in(keys[22], 71), 0),
        "value_codes": draw_value_codes(jax.random.fold_in(keys[22], 71), 0),
        "output_codes": draw_output_codes(jax.random.fold_in(keys[22], 71), 0),
        "gate_codes": draw_gate_codes(jax.random.fold_in(keys[22], 71), 0),
        "up_codes": draw_up_codes(jax.random.fold_in(keys[22], 71), 0),
        "down_codes": draw_down_codes(jax.random.fold_in(keys[22], 71), 0),
        "query_scale": jnp.clip(jnp.exp(math.log(0.00056) - 1.3862944 * jax.random.uniform(keys[8], (QW,), jnp.float32) ** block_scale(keys[8], (QW,), ((0, 32),), -0.2, 0.2)), 0.00014, 0.00056),
        "key_scale": jnp.clip(jnp.exp(math.log(0.00056) - 1.3862944 * jax.random.uniform(keys[9], (KW,), jnp.float32) ** block_scale(keys[9], (KW,), ((0, 32),), -0.2, 0.2)), 0.00014, 0.00056),
        "value_scale": jnp.clip(jnp.exp(math.log(0.00056) - 1.3862944 * jax.random.uniform(keys[10], (KW,), jnp.float32) ** block_scale(keys[10], (KW,), ((0, 32),), -0.2, 0.2)), 0.00014, 0.00056),
        "output_scale": jnp.clip(jnp.exp(math.log(0.0006) - 1.3862944 * jax.random.uniform(keys[11], (D,), jnp.float32) ** block_scale(keys[11], (D,), ((0, 32),), -0.2, 0.2)), 0.00015, 0.0006),
        "gate_scale": jnp.clip(jnp.exp(math.log(0.00056) - 1.3862944 * jax.random.uniform(keys[12], (FF,), jnp.float32) ** block_scale(keys[12], (FF,), ((0, 32),), -0.2, 0.2)), 0.00014, 0.00056),
        "up_scale": jnp.clip(jnp.exp(math.log(0.00056) - 1.3862944 * jax.random.uniform(keys[13], (FF,), jnp.float32) ** block_scale(keys[13], (FF,), ((0, 32),), -0.2, 0.2)), 0.00014, 0.00056),
        "down_scale": jnp.clip(jnp.exp(math.log(0.00028) - 1.3862944 * jax.random.uniform(keys[14], (D,), jnp.float32) ** block_scale(keys[14], (D,), ((0, 32),), -0.2, 0.2)), 7.000000186963007e-05, 0.00028),
        "pre_attn_gain": jnp.clip(1.0 + 0.15 * jax.random.normal(keys[15], (D,), jnp.float32), 0.25, 1.75),
        "post_attn_gain": jnp.clip(1.0 + 0.15 * jax.random.normal(keys[16], (D,), jnp.float32), 0.25, 1.75),
        "pre_ffw_gain": jnp.clip(1.0 + 0.15 * jax.random.normal(keys[17], (D,), jnp.float32), 0.25, 1.75),
        "post_ffw_gain": jnp.clip(1.0 + 0.15 * jax.random.normal(keys[18], (D,), jnp.float32), 0.25, 1.75),
        "slot_width": draw_slot_width(jax.random.fold_in(keys[22], 71), 0),
        "slot_live": draw_slot_live(jax.random.fold_in(keys[22], 71), 0),
        "cotangent": centred(keys[21], (SLOTS, TOKENS, D), 1.0, 6.0, ((1, 32),)),
    }


@jax.custom_vjp
def low(v):
    return lax.optimization_barrier(v.astype(jnp.bfloat16)).astype(jnp.float32)

@jax.custom_vjp
def low_back(v):
    return v

def low_keep(v):
    return (low(v), None)

def low_pass(kept, grad):
    return (grad,)

def back_keep(v):
    return (v, None)

def back_low(kept, grad):
    return (low(grad),)
low.defvjp(low_keep, low_pass)
low_back.defvjp(back_keep, back_low)
EPSILON = 1e-06
SOFT_CAP = 50.0
HIGHEST = lax.Precision.HIGHEST

def levels(code_values, width_index):
    step_size = jnp.where(width_index == 0, 1.0, jnp.where(width_index == 1, 16.0, 64.0)).astype(jnp.float32)
    return jnp.floor(code_values / step_size) * step_size + 0.5 * step_size

def rms_norm(values, gain_vector):
    return values * lax.rsqrt(lax.optimization_barrier(jnp.mean(values * values, axis=-1, keepdims=True)) + EPSILON) * gain_vector

def rotate(values, positions, heads):
    half_dim = HD // 2
    inv_rates = 10000.0 ** (-jnp.arange(half_dim, dtype=jnp.float32) / half_dim)
    angles = positions.astype(jnp.float32)[:, None] * inv_rates[None, :]
    cosine = jnp.cos(angles)[:, None, :]
    sine_part = jnp.sin(angles)[:, None, :]
    shaped = values.reshape(values.shape[0], heads, HD)
    first_half = shaped[:, :, :half_dim]
    second = shaped[:, :, half_dim:]
    turned = jnp.concatenate([first_half * cosine - second * sine_part, second * cosine + first_half * sine_part], axis=-1)
    return turned.reshape(values.shape)

def attend(queries, key_rows, values):
    length = queries.shape[0]
    group_size = HEADS // KV_HEADS
    query_heads = queries.reshape(length, KV_HEADS, group_size, HD)
    key_heads = key_rows.reshape(length, KV_HEADS, HD)
    value_heads = values.reshape(length, KV_HEADS, HD)
    scores = low_back(jnp.einsum('tgeh,lgh->getl', query_heads, key_heads, precision=HIGHEST))
    capped = SOFT_CAP * jnp.tanh(scores / SOFT_CAP)
    causal = jnp.arange(length)[:, None] >= jnp.arange(length)[None, :]
    masked = jnp.where(causal, capped, -1e+30)
    row_max = lax.optimization_barrier(jnp.max(masked, axis=-1, keepdims=True))
    exp_scores = jnp.exp(masked - row_max)
    row_total = lax.optimization_barrier(jnp.sum(exp_scores, axis=-1, keepdims=True))
    probabilities = low(exp_scores / row_total)
    attended = jnp.einsum('getl,lgh->tgeh', probabilities, value_heads, precision=HIGHEST)
    return attended.reshape(length, HEADS * HD)

def block_layer(inputs, matrices, scales, gain_list):
    length = inputs.shape[0]
    positions = jnp.arange(length)

    def project(activations, matrix_index):
        return low_back(jnp.dot(activations, matrices[matrix_index], precision=HIGHEST)) * scales[matrix_index]
    normed = low(rms_norm(inputs, gain_list[0]))
    queries = low(rotate(project(normed, 0), positions, HEADS) * HD ** (-0.5))
    key_rows = low(rotate(project(normed, 1), positions, KV_HEADS))
    values = low(project(normed, 2))
    attended = low_back(low(attend(queries, key_rows, values)))
    middle = inputs + rms_norm(project(attended, 3), gain_list[1])
    normed_two = low(rms_norm(middle, gain_list[2]))
    hidden = low(jax.nn.gelu(project(normed_two, 4), approximate=True) * project(normed_two, 5))
    return middle + rms_norm(project(hidden, 6), gain_list[3])

def reference(tokens, query_codes, key_codes, value_codes, output_codes, gate_codes, up_codes, down_codes, query_scale, key_scale, value_scale, output_scale, gate_scale, up_scale, down_scale, pre_attn_gain, post_attn_gain, pre_ffw_gain, post_ffw_gain, slot_width, slot_live, cotangent):
    code_mats = tuple((codes.astype(jnp.float32) for codes in (query_codes, key_codes, value_codes, output_codes, gate_codes, up_codes, down_codes)))
    scales = (query_scale, key_scale, value_scale, output_scale, gate_scale, up_scale, down_scale)
    gain_list = (pre_attn_gain, post_attn_gain, pre_ffw_gain, post_ffw_gain)
    inputs = tokens.astype(jnp.float32).reshape(SEQS, LENGTH, D)
    offsets = tuple((jnp.zeros(code_matrix.shape, jnp.float32) for code_matrix in code_mats))
    chosen = ((slot_width[:, :, None] == jnp.arange(3)[None, None, :]) & (slot_live[:, :, None] == 1)).astype(jnp.float32)

    def forward(inputs, offsets, scales, gain_list):
        results = []
        for width_index in range(3):
            matrices = tuple((levels(code_matrix, width_index) + offset for code_matrix, offset in zip(code_mats, offsets)))

            def run_one(sequence, matrices=matrices):
                return block_layer(sequence, matrices, scales, gain_list)
            results.append(lax.map(jax.checkpoint(run_one), inputs))
        stacked = jnp.stack(results, axis=0)
        mixed_rows = jnp.einsum('skw,wsld->ksld', chosen, stacked, precision=HIGHEST)
        return mixed_rows.reshape(SLOTS, TOKENS, D)
    mixed_rows, pull_back = jax.vjp(forward, inputs, offsets, scales, gain_list)
    input_grad, offset_grads, scale_grads, gain_grads = pull_back(cotangent.astype(jnp.float32))
    weight_grads = tuple((offset_grad / scale_vector[None, :] for offset_grad, scale_vector in zip(offset_grads, scales)))
    return (mixed_rows.astype(jnp.bfloat16), input_grad.reshape(TOKENS, D), weight_grads[0], weight_grads[1], weight_grads[2], weight_grads[3], weight_grads[4], weight_grads[5], weight_grads[6], scale_grads[0], scale_grads[1], scale_grads[2], scale_grads[3], scale_grads[4], scale_grads[5], scale_grads[6], gain_grads[0], gain_grads[1], gain_grads[2], gain_grads[3])
```

```python
import functools

import jax
import jax.numpy as jnp
from jax import lax
from jax.experimental import pallas as pl
from jax.experimental.pallas import tpu as pltpu
from jax.sharding import PartitionSpec as P

HEADS = 8
KV_HEADS = 4
HD = 256
HALF = HD // 2
SLOTS = 3
EPSILON = 1e-06
SOFT_CAP = 50.0
BF = jnp.bfloat16
F32 = jnp.float32
ALL = ("dp", "fsdp")
STEPS = (1.0, 16.0, 64.0)
VMEM_LIMIT = 48 * 1024 * 1024


def dequantized(codes, width):
    step = STEPS[width]
    if width == 0:
        return codes + BF(0.5)
    return jnp.floor(codes * BF(1.0 / step)) * BF(step) + BF(step / 2)


def rms_norm(values, gain_vector):
    return (
        values
        * lax.rsqrt(jnp.mean(values * values, axis=-1, keepdims=True) + EPSILON)
        * gain_vector
    )


def rotate(values, cosine, sine_part):
    first_half = values[..., :HALF]
    second = values[..., HALF:]
    return jnp.concatenate(
        [first_half * cosine - second * sine_part, second * cosine + first_half * sine_part],
        axis=-1,
    )


def dot(left, right):
    return jnp.dot(left, right, preferred_element_type=F32)


def dot_nt(left, right):
    return lax.dot_general(left, right, (((1,), (1,)), ((), ())), preferred_element_type=F32)


def dot_tn(left, right):
    return lax.dot_general(left, right, (((0,), (0,)), ((), ())), preferred_element_type=F32)


def gated(gate_in, up_in):
    return jax.nn.gelu(gate_in, approximate=True) * up_in


def score_block(qpos_ref, kpos_ref, q, k):
    tanh_part = jnp.tanh(dot_nt(q, k) * (1.0 / SOFT_CAP))
    causal = qpos_ref[...] >= kpos_ref[...]
    exp_scores = jnp.where(causal, jnp.exp(SOFT_CAP * tanh_part), 0.0)
    total = jnp.sum(exp_scores, axis=-1, keepdims=True)
    return tanh_part, exp_scores / total


def attend_kernel(qpos_ref, kpos_ref, q_ref, k_ref, v_ref, o_ref):
    rows = qpos_ref.shape[0]
    keys = kpos_ref.shape[1]
    k = k_ref[...].reshape(keys, HD)
    v = v_ref[...].reshape(keys, HD)
    _, probs = score_block(qpos_ref, kpos_ref, q_ref[...].reshape(rows, HD), k)
    o_ref[...] = dot(probs.astype(BF), v).astype(BF).reshape(o_ref.shape)


def attend_back_kernel(
    qpos_ref, kpos_ref, q_ref, k_ref, v_ref, do_ref, dq_ref, dk_ref, dv_ref
):
    rows = qpos_ref.shape[0]
    keys = kpos_ref.shape[1]
    q = q_ref[...].reshape(rows, HD)
    k = k_ref[...].reshape(keys, HD)
    v = v_ref[...].reshape(keys, HD)
    do = do_ref[...].reshape(rows, HD)
    tanh_part, probs = score_block(qpos_ref, kpos_ref, q, k)
    prob_grad = dot_nt(do, v)
    row_dot = jnp.sum(probs * prob_grad, axis=-1, keepdims=True)
    score_grad = (probs * (prob_grad - row_dot) * (1.0 - tanh_part * tanh_part)).astype(BF)
    dq_ref[...] = dot(score_grad, k).reshape(dq_ref.shape)
    dk_ref[...] = dot_tn(score_grad, q).reshape(dk_ref.shape)
    dv_ref[...] = dot_tn(probs.astype(BF), do).reshape(dv_ref.shape)


def attention_specs(q, keys):
    widths, _, seqs, rows, _ = q.shape
    groups = keys.shape[1]
    q_spec = pl.BlockSpec((1, 2, 1, rows, HD), lambda w, z: (w, 0, z, 0, 0))
    k_spec = pl.BlockSpec((1, groups, 2, 1, rows, HD), lambda w, z: (w, 0, 0, z, 0, 0))
    qpos_spec = pl.BlockSpec((2 * rows, 1), lambda w, z: (0, 0))
    kpos_spec = pl.BlockSpec((1, groups * 2 * rows), lambda w, z: (0, 0))
    return (widths, seqs), q_spec, k_spec, qpos_spec, kpos_spec


def attention_cost(q, keys, products):
    pairs = q.shape[0] * q.shape[2] * 2 * q.shape[3] * keys.shape[1] * 2 * keys.shape[4]
    return pl.CostEstimate(
        flops=2 * products * pairs * HD, bytes_accessed=2 * q.size + 4 * keys.size, transcendentals=2 * pairs
    )


def attend(qpos, kpos, q, k, v):
    grid, q_spec, k_spec, qpos_spec, kpos_spec = attention_specs(q, k)
    return pl.pallas_call(
        attend_kernel,
        grid=grid,
        in_specs=[qpos_spec, kpos_spec, q_spec, k_spec, k_spec],
        out_specs=q_spec,
        out_shape=jax.ShapeDtypeStruct(q.shape, BF),
        compiler_params=pltpu.CompilerParams(vmem_limit_bytes=VMEM_LIMIT),
        cost_estimate=attention_cost(q, k, 2),
        name="attend",
    )(qpos, kpos, q, k, v)


def attend_back(qpos, kpos, q, k, v, do):
    grid, q_spec, k_spec, qpos_spec, kpos_spec = attention_specs(q, k)
    return pl.pallas_call(
        attend_back_kernel,
        grid=grid,
        in_specs=[qpos_spec, kpos_spec, q_spec, k_spec, k_spec, q_spec],
        out_specs=[q_spec, k_spec, k_spec],
        out_shape=[
            jax.ShapeDtypeStruct(q.shape, F32),
            jax.ShapeDtypeStruct(k.shape, F32),
            jax.ShapeDtypeStruct(k.shape, F32),
        ],
        compiler_params=pltpu.CompilerParams(vmem_limit_bytes=VMEM_LIMIT),
        cost_estimate=attention_cost(q, k, 5),
        name="attend_back",
    )(qpos, kpos, q, k, v, do)


def shards(
    tokens,
    query_codes,
    key_codes,
    value_codes,
    output_codes,
    gate_codes,
    up_codes,
    down_codes,
    query_scale,
    key_scale,
    value_scale,
    output_scale,
    gate_scale,
    up_scale,
    down_scale,
    pre_attn_gain,
    post_attn_gain,
    pre_ffw_gain,
    post_ffw_gain,
    slot_width,
    slot_live,
    cotangent,
):
    planes = lax.axis_size("dp")
    width = lax.axis_size("fsdp")
    devices = planes * width
    zh_count, y_count = planes // 2, width // 4
    dp_rank = lax.axis_index("dp")
    rank = lax.axis_index("fsdp")
    me = dp_rank * width + rank
    zh, zl = dp_rank // 2, dp_rank % 2
    yh, xc = rank // 4, rank % 4
    core = rank % 2
    t_index = zl * 4 + xc
    CORE, X, ZL = 1, 2, width
    zh_masks = [width * 2 * (1 << b) for b in range(zh_count.bit_length() - 1)]
    y_masks = [4 * (1 << b) for b in range(y_count.bit_length() - 1)]

    def swap(values, mask):
        return lax.ppermute(values, ALL, [(i, i ^ mask) for i in range(devices)])

    tok_rows, model = tokens.shape
    group_rows = 8 * tok_rows
    d_rows = query_codes.shape[0]
    o_rows = output_codes.shape[0]
    ff_rows = down_codes.shape[0]
    q_cols = query_codes.shape[1] // 8
    k_cols = key_codes.shape[1] // 8
    ff_cols = ff_rows * zh_count * y_count
    half = model // 2
    widths = range(SLOTS)

    def tp_gather(block):
        first, second = block[:, :half], block[:, half:]
        first_z = swap(first, ZL)
        second_x = swap(second, X)
        first_x = swap(jnp.stack([first, first_z]), X)
        second_z = swap(jnp.stack([second, second_x]), ZL)
        same = jnp.concatenate(
            [
                block,
                jnp.concatenate([first_x[0], second_x], axis=1),
                jnp.concatenate([first_z, second_z[0]], axis=1),
                jnp.concatenate([first_x[1], second_z[1]], axis=1),
            ],
            axis=0,
        )
        return jnp.concatenate([same, swap(same, CORE)], axis=0)

    def tp_scatter(partial):
        low = partial.astype(BF).reshape(2, 2, 2, tok_rows, model)
        pair = (low[0].astype(F32) + swap(low[1], CORE).astype(F32)).astype(BF)
        got_x = swap(pair[:, 1, :, :half], X)
        got_z = swap(pair[1, :, :, half:], ZL)
        first = (pair[:, 0, :, :half].astype(F32) + got_x.astype(F32)).astype(BF)
        second = (pair[0, :, :, half:].astype(F32) + got_z.astype(F32)).astype(BF)
        last_z = swap(first[1], ZL)
        last_x = swap(second[1], X)
        return jnp.concatenate(
            [
                first[0].astype(F32) + last_z.astype(F32),
                second[0].astype(F32) + last_x.astype(F32),
            ],
            axis=1,
        )

    def tp_columns(blocks):
        result = jnp.zeros_like(blocks)
        for m in range(8):
            mask = (m & 3) + (width if m & 4 else 0)
            block = lax.dynamic_index_in_dim(blocks, t_index ^ m, 0, keepdims=False)
            moved = block if m == 0 else swap(block, mask)
            result = lax.dynamic_update_index_in_dim(result, moved, t_index ^ m, 0)
        return result

    def weight_gather(shard, place):
        parts = {0: shard}
        for mask in zh_masks + y_masks:
            for key in list(parts):
                parts[key ^ mask] = swap(parts[key], mask)
        return parts

    def from_parts(parts, key):
        other = me ^ key
        other_dp, other_rank = other // width, other % width
        return other_dp // 2, other_rank // 4

    def gather_rows(shard):
        parts = weight_gather(shard, None)
        rows, cols = shard.shape[1], shard.shape[2]
        result = jnp.zeros((zh_count, 2, y_count, 4 * rows, cols), shard.dtype)
        for key, part in parts.items():
            z, y = from_parts(parts, key)
            result = lax.dynamic_update_slice(
                result, part.reshape(1, 2, 1, 4 * rows, cols), (z, 0, y, 0, 0)
            )
        return result.reshape(devices * rows, cols)

    def gather_blocks(shard):
        parts = weight_gather(shard, None)
        rows, cols = shard.shape
        result = jnp.zeros((zh_count, y_count, rows, cols), shard.dtype)
        for key, part in parts.items():
            z, y = from_parts(parts, key)
            result = lax.dynamic_update_slice(result, part[None, None], (z, y, 0, 0))
        return result

    def weight_scatter(values, z_axis, y_axis):
        for axis, masks, place in ((y_axis, y_masks, yh), (z_axis, zh_masks, zh)):
            for bit in reversed(range(len(masks))):
                keep = values.shape[axis] // 2
                side = (place >> bit) & 1
                gone = lax.dynamic_slice_in_dim(values, (1 - side) * keep, keep, axis)
                kept = lax.dynamic_slice_in_dim(values, side * keep, keep, axis)
                values = (kept.astype(F32) + swap(gone, masks[bit]).astype(F32)).astype(BF)
        return values

    def scatter_rows(grad):
        rows, cols = grad.shape[0] // devices, grad.shape[1]
        values = grad.reshape(zh_count, 2, y_count, 4 * rows, cols)
        return weight_scatter(values, 0, 2).reshape(8, rows, cols)

    small = jnp.concatenate(
        [query_scale, key_scale, value_scale, output_scale, gate_scale, up_scale, down_scale]
    )
    all_small = small[None]
    for bit in range(devices.bit_length() - 1):
        all_small = jnp.concatenate([all_small, swap(all_small, 1 << bit)], axis=0)
    order = jnp.arange(devices, dtype=jnp.int32) ^ me
    all_small = all_small[order]
    cuts = []
    at = 0
    for vector in (
        query_scale,
        key_scale,
        value_scale,
        output_scale,
        gate_scale,
        up_scale,
        down_scale,
    ):
        cuts.append(all_small[:, at : at + vector.shape[0]].reshape(-1))
        at += vector.shape[0]
    q_scale_all, k_scale_all, v_scale_all, o_scale_all, g_scale_all, u_scale_all, d_scale_all = cuts

    head = (xc // 2) * 4 + zl * 2 + core
    kv_half = head

    def own_ff(vector):
        cut = vector.reshape(zh_count, 2, y_count, 4, ff_rows)
        cut = lax.dynamic_slice(cut, (0, zl, 0, xc, 0), (zh_count, 1, y_count, 1, ff_rows))
        return cut.reshape(ff_cols)

    qkv_scale = jnp.concatenate(
        [
            lax.dynamic_slice_in_dim(q_scale_all, head * q_cols, q_cols),
            lax.dynamic_slice_in_dim(k_scale_all, kv_half * k_cols, k_cols),
            lax.dynamic_slice_in_dim(v_scale_all, kv_half * k_cols, k_cols),
        ]
    )
    g_scale = own_ff(g_scale_all)
    u_scale = own_ff(u_scale_all)

    def by_head(codes):
        cut = codes.reshape(codes.shape[0], 2, 2, 2, -1)
        return cut.transpose(2, 1, 3, 0, 4).reshape(8, codes.shape[0], -1)

    def by_head_back(blocks):
        cut = blocks.reshape(2, 2, 2, blocks.shape[1], blocks.shape[2])
        return cut.transpose(3, 1, 0, 2, 4).reshape(blocks.shape[1], -1)

    def by_ff(codes):
        cut = codes.reshape(d_rows, zh_count, 2, y_count, 4, ff_rows)
        return cut.transpose(2, 4, 0, 1, 3, 5).reshape(8, d_rows, ff_cols)

    def by_ff_back(blocks):
        cut = blocks.reshape(2, 4, d_rows, zh_count, y_count, ff_rows)
        return cut.transpose(2, 3, 0, 4, 1, 5).reshape(d_rows, 8 * ff_cols)

    qkv_blocks = jnp.concatenate(
        [by_head(query_codes), by_head(key_codes), by_head(value_codes)], axis=2
    )
    inputs = tokens.astype(F32)
    normed = tp_gather(rms_norm(inputs, pre_attn_gain).astype(BF))
    qkv_codes = gather_rows(tp_columns(qkv_blocks))

    def quarter_swap(blocks):
        result = jnp.zeros_like(blocks)
        for m in range(4):
            block = lax.dynamic_index_in_dim(blocks, xc ^ m, 0, keepdims=False)
            moved = block if m == 0 else swap(block, m)
            result = lax.dynamic_update_index_in_dim(result, moved, xc ^ m, 0)
        return result

    whole_heads = zh_count == 2 and y_count == 2
    if whole_heads:
        parts = gather_blocks(output_codes).reshape(4, o_rows, model)
        out_codes = quarter_swap(parts).reshape(HD, model)
    else:
        every = lax.all_gather(output_codes, ALL, axis=0, tiled=True)
        out_codes = lax.dynamic_slice_in_dim(every, head * HD, HD, 0)

    gate_codes_t = gather_rows(tp_columns(by_ff(gate_codes)))
    up_codes_t = gather_rows(tp_columns(by_ff(up_codes)))
    down_codes_t = gather_blocks(down_codes).reshape(ff_cols, model)

    offsets = jnp.arange(tok_rows, dtype=jnp.int32)
    blocks_at = jnp.stack([jnp.stack([xc ^ (c + 2 * x) for x in range(2)]) for c in range(2)])
    q_positions = ((yh * 4 + blocks_at) * tok_rows)[:, :, None] + offsets
    q_positions = q_positions.reshape(4 * tok_rows)
    seq_rows = 4 * tok_rows
    far = jnp.int32(1 << 30)
    key_positions = []
    for back in range(y_count):
        positions = q_positions - back * seq_rows
        key_positions.append(jnp.where(positions >= 0, positions, far))
    kpos = jnp.concatenate(key_positions)[None, :]
    qpos = q_positions[:, None]
    inv_rates = 10000.0 ** (-jnp.arange(HALF, dtype=F32) / HALF)
    angles = q_positions.astype(F32)[:, None] * inv_rates[None, :]
    cosine = jnp.cos(angles).reshape(2, 1, 2 * tok_rows, HALF)
    sine = jnp.sin(angles).reshape(2, 1, 2 * tok_rows, HALF)
    q_factor = HD ** (-0.5)
    rows_shape = (SLOTS, 2, 2, 2 * tok_rows)

    qkv_w = [dequantized(qkv_codes, w) for w in widths]
    qkv_raw = [dot(normed, qkv_w[w]) for w in widths]
    qkv_lin = jnp.stack([raw * qkv_scale for raw in qkv_raw]).reshape(
        SLOTS, 2, 2, 2 * tok_rows, q_cols + 2 * k_cols
    )
    q = (rotate(qkv_lin[..., :q_cols], cosine, sine) * q_factor).astype(BF)
    kv_own = qkv_lin[..., q_cols:]
    kv_other = swap(kv_own, CORE)[:, ::-1]
    first_core = core == 0

    def both(own, other):
        return jnp.concatenate(
            [jnp.where(first_core, own, other), jnp.where(first_core, other, own)], axis=-1
        )

    k_near = rotate(both(kv_own[..., :k_cols], kv_other[..., :k_cols]), cosine, sine).astype(BF)
    v_near = both(kv_own[..., k_cols:], kv_other[..., k_cols:]).astype(BF)

    def own_half(values):
        return lax.dynamic_slice_in_dim(values, core * k_cols, k_cols, values.ndim - 1)

    kv_near = jnp.concatenate([own_half(k_near), own_half(v_near)], axis=-1)
    k_parts, v_parts = [k_near], [v_near]

    def back_pairs(back):
        return [(i, i + 4 * back) for i in range(devices) if (i % width) + 4 * back < width]

    for back in range(1, y_count):
        mine = lax.ppermute(kv_near, ALL, back_pairs(back))
        other = swap(mine, CORE)[:, ::-1]
        k_parts.append(both(mine[..., :k_cols], other[..., :k_cols]))
        v_parts.append(both(mine[..., k_cols:], other[..., k_cols:]))
    k_all = jnp.stack(k_parts, axis=1)
    v_all = jnp.stack(v_parts, axis=1)
    attended = attend(qpos, kpos, q, k_all, v_all)
    o_flat = attended.reshape(SLOTS, group_rows, HD)

    slot_of = []
    for w in widths:
        slot = jnp.int32(0)
        for s in range(SLOTS):
            slot = jnp.where(slot_width[0, s] == w, s, slot)
        slot_of.append(slot)
    kept = [dict() for w in widths]
    for w in widths:
        k = kept[w]
        k["out_w"] = dequantized(out_codes, w)
        k["out_raw"] = tp_scatter(dot(o_flat[w], k["out_w"]))
        k["attn_out"] = k["out_raw"] * o_scale_all
        k["middle"] = inputs + rms_norm(k["attn_out"], post_attn_gain)
        k["normed_two"] = tp_gather(rms_norm(k["middle"], pre_ffw_gain).astype(BF))
    for w in widths:
        k = kept[w]
        k["gate_w"] = dequantized(gate_codes_t, w)
        k["up_w"] = dequantized(up_codes_t, w)
        k["gate_raw"] = dot(k["normed_two"], k["gate_w"])
        k["up_raw"] = dot(k["normed_two"], k["up_w"])
        k["hidden"] = gated(k["gate_raw"] * g_scale, k["up_raw"] * u_scale).astype(BF)
    for w in widths:
        k = kept[w]
        k["down_w"] = dequantized(down_codes_t, w)
        k["down_raw"] = tp_scatter(dot(k["hidden"], k["down_w"]))

    mixed = jnp.zeros((SLOTS, tok_rows, model), BF)
    out_scale_acc = jnp.zeros((model,), F32)
    down_scale_acc = jnp.zeros((model,), F32)
    gate_scale_acc = jnp.zeros((ff_cols,), F32)
    up_scale_acc = jnp.zeros((ff_cols,), F32)
    gains = [jnp.zeros((model,), F32) for g in range(4)]
    input_total = jnp.zeros(inputs.shape, F32)
    for w in widths:
        k = kept[w]
        live = lax.dynamic_index_in_dim(slot_live[0], slot_of[w], 0, keepdims=False).astype(F32)
        down_lin = k["down_raw"] * d_scale_all
        branch, pull_four = jax.vjp(rms_norm, down_lin, post_ffw_gain)
        result = ((k["middle"] + branch) * live).astype(BF)
        mixed = lax.dynamic_update_index_in_dim(mixed, result, slot_of[w], 0)
        cot = lax.dynamic_index_in_dim(cotangent, slot_of[w], 0, keepdims=False)
        k["grad_out"] = cot.astype(F32) * live
        down_lin_grad, gain_four = pull_four(k["grad_out"])
        gains[3] = gains[3] + gain_four
        down_scale_acc = down_scale_acc + jnp.sum(k["down_raw"] * down_lin_grad, axis=0)
        k["down_round"] = tp_gather((down_lin_grad * d_scale_all).astype(BF))
    down_sum = dot_tn(
        jnp.concatenate([kept[w]["hidden"] for w in widths], axis=0),
        jnp.concatenate([kept[w]["down_round"] for w in widths], axis=0),
    )
    down_sum = weight_scatter(
        (down_sum / d_scale_all).astype(BF).reshape(zh_count, y_count, ff_rows, model), 0, 1
    )
    for w in widths:
        k = kept[w]
        hidden_grad = dot_nt(k["down_round"], k["down_w"])
        _, pull_mix = jax.vjp(gated, k["gate_raw"] * g_scale, k["up_raw"] * u_scale)
        gate_grad, up_grad = pull_mix(hidden_grad)
        gate_scale_acc = gate_scale_acc + jnp.sum(k["gate_raw"] * gate_grad, axis=0)
        up_scale_acc = up_scale_acc + jnp.sum(k["up_raw"] * up_grad, axis=0)
        k["gate_round"] = (gate_grad * g_scale).astype(BF)
        k["up_round"] = (up_grad * u_scale).astype(BF)
        k["two_grad"] = tp_scatter(
            dot_nt(k["gate_round"], k["gate_w"]) + dot_nt(k["up_round"], k["up_w"])
        )
    normed_two_rows = jnp.concatenate([kept[w]["normed_two"] for w in widths], axis=0)
    gate_sum = dot_tn(
        normed_two_rows, jnp.concatenate([kept[w]["gate_round"] for w in widths], axis=0)
    )
    gate_sum = scatter_rows((gate_sum / g_scale).astype(BF))
    up_sum = dot_tn(
        normed_two_rows, jnp.concatenate([kept[w]["up_round"] for w in widths], axis=0)
    )
    up_sum = scatter_rows((up_sum / u_scale).astype(BF))
    for w in widths:
        k = kept[w]
        _, pull_three = jax.vjp(rms_norm, k["middle"], pre_ffw_gain)
        middle_part, gain_three = pull_three(k["two_grad"])
        gains[2] = gains[2] + gain_three
        middle_grad = k["grad_out"] + middle_part
        _, pull_two = jax.vjp(rms_norm, k["attn_out"], post_attn_gain)
        attn_out_grad, gain_two = pull_two(middle_grad)
        gains[1] = gains[1] + gain_two
        out_scale_acc = out_scale_acc + jnp.sum(k["out_raw"] * attn_out_grad, axis=0)
        k["out_round"] = tp_gather((attn_out_grad * o_scale_all).astype(BF))
        k["o_grad"] = dot_nt(k["out_round"], k["out_w"]).astype(BF)
        input_total = input_total + middle_grad
    out_sum = dot_tn(
        o_flat.reshape(SLOTS * group_rows, HD),
        jnp.concatenate([kept[w]["out_round"] for w in widths], axis=0),
    )
    out_sum = (out_sum / o_scale_all).astype(BF)
    if whole_heads:
        out_blocks = quarter_swap(out_sum.reshape(4, o_rows, model))
        out_sum = weight_scatter(out_blocks.reshape(2, 2, o_rows, model), 0, 1)
    else:
        whole = jnp.zeros((HEADS * HD, model), BF)
        whole = lax.dynamic_update_slice_in_dim(whole, out_sum, head * HD, 0)
        out_sum = lax.psum_scatter(whole, ALL, scatter_dimension=0, tiled=True)

    o_grad = jnp.stack([kept[w]["o_grad"] for w in widths]).reshape(q.shape)
    dq, dk, dv = attend_back(qpos, kpos, q, k_all, v_all, o_grad)
    q_grad = rotate(dq * q_factor, cosine, -sine)
    far_cos = jnp.stack([jnp.cos((q_positions - b * seq_rows).astype(F32)[:, None] * inv_rates) for b in range(y_count)])
    far_sin = jnp.stack([jnp.sin((q_positions - b * seq_rows).astype(F32)[:, None] * inv_rates) for b in range(y_count)])
    far_shape = (y_count, 2, 1, 2 * tok_rows, HALF)
    dk = rotate(dk, far_cos.reshape(far_shape), -far_sin.reshape(far_shape))
    other = 1 - core

    def half_of(values, which):
        return lax.dynamic_slice_in_dim(values, which * k_cols, k_cols, values.ndim - 1)

    dkv = jnp.concatenate([half_of(dk, core), half_of(dv, core)], axis=-1)
    dkv_gone = jnp.concatenate([half_of(dk, other), half_of(dv, other)], axis=-1)
    dkv = dkv + swap(dkv_gone, CORE)[:, :, ::-1]
    kv_grad = dkv[:, 0]
    for back in range(1, y_count):
        pairs = [(b, a) for a, b in back_pairs(back)]
        kv_grad = kv_grad + lax.ppermute(dkv[:, back].astype(BF), ALL, pairs).astype(F32)
    qkv_grad = jnp.concatenate([q_grad, kv_grad], axis=-1).reshape(SLOTS, group_rows, -1)
    qkv_round = [(qkv_grad[w] * qkv_scale).astype(BF) for w in widths]
    qkv_scale_acc = sum(jnp.sum(qkv_raw[w] * qkv_grad[w], axis=0) for w in widths)
    qkv_rows = sum(qkv_round[w].astype(F32) for w in widths).astype(BF)
    normed_grad = tp_scatter(sum(dot_nt(qkv_round[w], qkv_w[w]) for w in widths))
    qkv_sum = scatter_rows((dot_tn(normed, qkv_rows) / qkv_scale).astype(BF))
    _, pull_one = jax.vjp(rms_norm, inputs, pre_attn_gain)
    input_part, gains[0] = pull_one(normed_grad)
    input_total = input_total + input_part

    down_grad = down_sum.reshape(ff_rows, model).astype(F32)
    gate_grad = by_ff_back(tp_columns(gate_sum)).astype(F32)
    up_grad = by_ff_back(tp_columns(up_sum)).astype(F32)
    output_grad = out_sum.reshape(o_rows, model).astype(F32)
    qkv_back = tp_columns(qkv_sum)
    query_grad = by_head_back(qkv_back[:, :, :q_cols]).astype(F32)
    key_grad = by_head_back(qkv_back[:, :, q_cols : q_cols + k_cols]).astype(F32)
    value_grad = by_head_back(qkv_back[:, :, q_cols + k_cols :]).astype(F32)

    def placed(part, count):
        whole = jnp.zeros((8 * count,), F32)
        return lax.dynamic_update_slice_in_dim(whole, part, head * count, 0)

    def placed_ff(part):
        whole = jnp.zeros((zh_count, 2, y_count, 4, ff_rows), F32)
        block = part.reshape(zh_count, 1, y_count, 1, ff_rows)
        return lax.dynamic_update_slice(whole, block, (0, zl, 0, xc, 0)).reshape(-1)

    vectors = [
        placed(qkv_scale_acc[:q_cols], q_cols),
        placed(qkv_scale_acc[q_cols : q_cols + k_cols], k_cols),
        placed(qkv_scale_acc[q_cols + k_cols :], k_cols),
        out_scale_acc,
        placed_ff(gate_scale_acc),
        placed_ff(up_scale_acc),
        down_scale_acc,
    ] + gains
    summed = jnp.concatenate([v.reshape(devices, -1) for v in vectors], axis=1)[order]
    for bit in reversed(range(devices.bit_length() - 1)):
        keep = 1 << bit
        summed = summed[:keep] + swap(summed[keep:], keep)
    summed = summed[0]
    vector_grads = []
    at = 0
    for v in vectors:
        size = v.shape[0] // devices
        vector_grads.append(summed[at : at + size])
        at += size

    return (
        mixed,
        input_total,
        query_grad,
        key_grad,
        value_grad,
        output_grad,
        gate_grad,
        up_grad,
        down_grad,
        *vector_grads,
    )


def solution(mesh):
    rows = P(ALL, None)
    vector = P(ALL)
    in_specs = (
        (rows,) * 8
        + (vector,) * 7
        + (P(),) * 4
        + (P("dp", None), P("dp", None), P(None, ALL, None))
    )
    out_specs = (P(None, ALL, None),) + (rows,) * 8 + (vector,) * 11
    return jax.shard_map(shards, mesh=mesh, in_specs=in_specs, out_specs=out_specs, check_vma=False)
```

```python
import functools

import jax
import jax.numpy as jnp
from jax import lax
from jax.experimental import pallas as pl
from jax.experimental.pallas import tpu as pltpu
from jax.sharding import PartitionSpec as P

HEADS = 8
KV_HEADS = 4
HD = 256
HALF = HD // 2
SLOTS = 3
EPSILON = 1e-06
SOFT_CAP = 50.0
BF = jnp.bfloat16
F32 = jnp.float32
ALL = ("dp", "fsdp")
STEPS = (1.0, 16.0, 64.0)
VMEM_LIMIT = 60 * 1024 * 1024


def dequantized(codes, width):
    step = STEPS[width]
    if width == 0:
        return codes + BF(0.5)
    return jnp.floor(codes * BF(1.0 / step)) * BF(step) + BF(step / 2)


def rms_norm(values, gain_vector):
    return (
        values
        * lax.rsqrt(jnp.mean(values * values, axis=-1, keepdims=True) + EPSILON)
        * gain_vector
    )


def rotate(values, cosine, sine_part):
    first_half = values[..., :HALF]
    second = values[..., HALF:]
    return jnp.concatenate(
        [first_half * cosine - second * sine_part, second * cosine + first_half * sine_part],
        axis=-1,
    )


def dot(left, right):
    return jnp.dot(left, right, preferred_element_type=F32)


def dot_nt(left, right):
    return lax.dot_general(left, right, (((1,), (1,)), ((), ())), preferred_element_type=F32)


def dot_tn(left, right):
    return lax.dot_general(left, right, (((0,), (0,)), ((), ())), preferred_element_type=F32)


def gated(gate_in, up_in):
    return jax.nn.gelu(gate_in, approximate=True) * up_in


def score_block(qpos_ref, kpos_ref, q, k):
    tanh_part = jnp.tanh(dot_nt(q, k) * (1.0 / SOFT_CAP))
    causal = qpos_ref[...] >= kpos_ref[...]
    exp_scores = jnp.where(causal, jnp.exp(SOFT_CAP * tanh_part), 0.0)
    total = jnp.sum(exp_scores, axis=-1, keepdims=True)
    return tanh_part, exp_scores / total


def attend_kernel(qpos_ref, kpos_ref, q_ref, k_ref, v_ref, o_ref):
    _, probs = score_block(qpos_ref, kpos_ref, q_ref[0], k_ref[0])
    o_ref[0] = dot(probs.astype(BF), v_ref[0]).astype(BF)


def attend_back_kernel(
    qpos_ref,
    kpos_ref,
    qcos_ref,
    qsin_ref,
    kcos_ref,
    ksin_ref,
    q_ref,
    k_ref,
    v_ref,
    do_ref,
    dq_ref,
    dk_ref,
    dv_ref,
):
    q, k, v, do = q_ref[0], k_ref[0], v_ref[0], do_ref[0]

    @pl.when(pl.program_id(1) == 0)
    def _():
        dk_ref[...] = jnp.zeros_like(dk_ref)
        dv_ref[...] = jnp.zeros_like(dv_ref)

    tanh_part, probs = score_block(qpos_ref, kpos_ref, q, k)
    prob_grad = dot_nt(do, v)
    row_dot = jnp.sum(probs * prob_grad, axis=-1, keepdims=True)
    score_grad = (probs * (prob_grad - row_dot) * (1.0 - tanh_part * tanh_part)).astype(BF)
    dq = dot(score_grad, k) * HD ** (-0.5)
    dq_ref[0] = rotate(dq, qcos_ref[...], -qsin_ref[...])
    dk_ref[0] += dot_tn(score_grad, q)
    dv_ref[0] += dot_tn(probs.astype(BF), do)

    @pl.when(pl.program_id(1) == pl.num_programs(1) - 1)
    def _():
        dk_ref[0] = rotate(dk_ref[0], kcos_ref[...], -ksin_ref[...])


def attention_specs(q, keys, tok_rows):
    widths, rows, _ = q.shape
    chunk = 2 * tok_rows
    q_spec = pl.BlockSpec((1, chunk, HD), lambda w, i: (w, i, 0))
    k_spec = pl.BlockSpec((1, keys.shape[1], HD), lambda w, i: (w, 0, 0))
    qpos_spec = pl.BlockSpec((chunk, 1), lambda w, i: (i, 0))
    kpos_spec = pl.BlockSpec((1, keys.shape[1]), lambda w, i: (0, 0))
    turn_specs = [pl.BlockSpec((chunk, HALF), lambda w, i: (i, 0))] * 2
    turn_specs += [pl.BlockSpec((keys.shape[1], HALF), lambda w, i: (0, 0))] * 2
    return (widths, rows // chunk), q_spec, k_spec, qpos_spec, kpos_spec, turn_specs


def attention_cost(q, keys, products):
    pairs = q.shape[0] * q.shape[1] * keys.shape[1]
    return pl.CostEstimate(
        flops=2 * products * pairs * HD,
        bytes_accessed=2 * q.size + 4 * keys.size,
        transcendentals=2 * pairs,
    )


def attend(qpos, kpos, q, k, v, tok_rows):
    grid, q_spec, k_spec, qpos_spec, kpos_spec, _ = attention_specs(q, k, tok_rows)
    return pl.pallas_call(
        attend_kernel,
        grid=grid,
        in_specs=[qpos_spec, kpos_spec, q_spec, k_spec, k_spec],
        out_specs=q_spec,
        out_shape=jax.ShapeDtypeStruct(q.shape, BF),
        compiler_params=pltpu.CompilerParams(vmem_limit_bytes=VMEM_LIMIT),
        cost_estimate=attention_cost(q, k, 2),
        name="attend",
    )(qpos, kpos, q, k, v)


def attend_back(qpos, kpos, turns, q, k, v, do, tok_rows):
    grid, q_spec, k_spec, qpos_spec, kpos_spec, turn_specs = attention_specs(q, k, tok_rows)
    return pl.pallas_call(
        attend_back_kernel,
        grid=grid,
        in_specs=[qpos_spec, kpos_spec, *turn_specs, q_spec, k_spec, k_spec, q_spec],
        out_specs=[q_spec, k_spec, k_spec],
        out_shape=[
            jax.ShapeDtypeStruct(q.shape, F32),
            jax.ShapeDtypeStruct(k.shape, F32),
            jax.ShapeDtypeStruct(k.shape, F32),
        ],
        compiler_params=pltpu.CompilerParams(vmem_limit_bytes=VMEM_LIMIT),
        cost_estimate=attention_cost(q, k, 5),
        name="attend_back",
    )(qpos, kpos, *turns, q, k, v, do)


def project_kernel(
    a_ref, w_hbm, scale_ref, cos_ref, sin_ref, raw_ref, q_ref, kv_ref, kept_hbm, held, sems, out_sems
):
    @pl.when(pl.program_id(0) == 0)
    def _():
        for w in range(SLOTS):
            load_codes(w, (w_hbm,), (held.at[w],), sems)

    copies = keep_copies((held,), (kept_hbm,), out_sems)
    start_on_first(copies)
    a = a_ref[...]
    cosine, sine = cos_ref[...], sin_ref[...]
    for w in range(SLOTS):
        raw = dot(a, held[w])
        raw_ref[w] = raw.astype(BF)
        lin = raw * scale_ref[...]
        q_ref[w] = (rotate(lin[:, :HD], cosine, sine) * HD ** (-0.5)).astype(BF)
        kv_ref[w] = lin[:, HD:]
    wait_on_last(copies)


def project(a, codes, scale, cosine, sine):
    rows, model = a.shape
    cols = codes.shape[1]
    chunk = min(rows, 256)
    turn = pl.BlockSpec((chunk, HALF), lambda i: (i, 0))

    def out(count):
        return pl.BlockSpec((SLOTS, chunk, count), lambda i: (0, i, 0))

    return pl.pallas_call(
        project_kernel,
        grid=(rows // chunk,),
        in_specs=[
            pl.BlockSpec((chunk, model), lambda i: (i, 0)),
            pl.BlockSpec(memory_space=pl.ANY),
            pl.BlockSpec((1, cols), lambda i: (0, 0)),
            turn,
            turn,
        ],
        out_specs=[out(cols), out(HD), out(cols - HD), pl.BlockSpec(memory_space=pl.ANY)],
        out_shape=[
            jax.ShapeDtypeStruct((SLOTS, rows, cols), BF),
            jax.ShapeDtypeStruct((SLOTS, rows, HD), BF),
            jax.ShapeDtypeStruct((SLOTS, rows, cols - HD), F32),
            jax.ShapeDtypeStruct((SLOTS, model, cols), BF),
        ],
        scratch_shapes=[
            pltpu.VMEM((SLOTS, model, cols), BF),
            pltpu.SemaphoreType.DMA((1,)),
            pltpu.SemaphoreType.DMA((1,)),
        ],
        compiler_params=pltpu.CompilerParams(vmem_limit_bytes=VMEM_LIMIT),
        cost_estimate=pl.CostEstimate(
            flops=2 * SLOTS * rows * model * cols,
            bytes_accessed=2 * rows * model + 2 * model * cols + 8 * SLOTS * rows * cols,
            transcendentals=0,
        ),
        name="project",
    )(a, codes, scale[None], cosine, sine)


def heads_kernel(core_ref, own_ref, other_ref, cos_ref, sin_ref, k_ref, v_ref):
    own, other = own_ref[0], other_ref[0]
    cols = own.shape[1] // 2
    first = core_ref[0, 0] == 0
    low = jnp.where(first, own, other)
    high = jnp.where(first, other, own)
    k = jnp.concatenate([low[:, :cols], high[:, :cols]], axis=1)
    k_ref[0] = rotate(k, cos_ref[...], sin_ref[...]).astype(BF)
    v_ref[0] = jnp.concatenate([low[:, cols:], high[:, cols:]], axis=1).astype(BF)


def whole_heads_of(core, own, other, cosine, sine):
    widths, rows, cols = own.shape
    part = rows // 2
    mine = pl.BlockSpec((1, part, cols), lambda w, c: (w, c, 0))
    turn = pl.BlockSpec((part, HALF), lambda w, c: (c, 0))
    return pl.pallas_call(
        heads_kernel,
        grid=(widths, 2),
        in_specs=[
            pl.BlockSpec(memory_space=pltpu.SMEM),
            mine,
            pl.BlockSpec((1, part, cols), lambda w, c: (w, 1 - c, 0)),
            turn,
            turn,
        ],
        out_specs=[mine, mine],
        out_shape=[jax.ShapeDtypeStruct(own.shape, BF)] * 2,
        compiler_params=pltpu.CompilerParams(vmem_limit_bytes=VMEM_LIMIT),
        cost_estimate=pl.CostEstimate(flops=8 * own.size, bytes_accessed=12 * own.size, transcendentals=0),
        name="heads",
    )(core.reshape(1, 1).astype(jnp.int32), own, other, cosine, sine)


def norm_scale(values):
    return lax.rsqrt(jnp.mean(values * values, axis=-1, keepdims=True) + EPSILON)


def norm_back(values, gain, grad):
    r = norm_scale(values)
    weighted = grad * gain
    unit = values * r
    back = r * (weighted - unit * jnp.mean(weighted * unit, axis=-1, keepdims=True))
    return back, jnp.sum(grad * unit, axis=0, keepdims=True)


def output_partial_kernel(width, o_ref, w_ref, low_ref, high_ref, held):
    @pl.when(pl.program_id(0) == 0)
    def _():
        held[...] = dequantized(w_ref[...], width)

    store_halves(low_ref, high_ref, dot(o_ref[0], held[...]).astype(BF))


def output_partial(width, attended, codes):
    rows = attended.shape[1]
    model = codes.shape[1]
    chunk = min(rows // 2, 256)
    specs, shapes = halves_specs(rows, model, chunk)
    return pl.pallas_call(
        functools.partial(output_partial_kernel, width),
        grid=(rows // chunk,),
        in_specs=[
            pl.BlockSpec((1, chunk, HD), lambda i: (width, i, 0)),
            pl.BlockSpec((HD, model), lambda i: (0, 0)),
        ],
        out_specs=specs,
        out_shape=shapes,
        scratch_shapes=[pltpu.VMEM((HD, model), BF)],
        compiler_params=pltpu.CompilerParams(vmem_limit_bytes=VMEM_LIMIT),
        cost_estimate=pl.CostEstimate(
            flops=2 * rows * HD * model, bytes_accessed=2 * rows * model, transcendentals=0
        ),
        name="output_partial",
    )(attended, codes)


def output_norm_kernel(
    part_ref, from_x_ref, from_y_ref, x_ref, scale_ref, post_ref, pre_ref, raw_ref, middle_ref, two_ref
):
    raw = part_ref[...].astype(F32) + from_x_ref[...].astype(F32) + from_y_ref[...].astype(F32)
    raw_ref[...] = raw
    lin = raw * scale_ref[...]
    middle = x_ref[...].astype(F32) + lin * norm_scale(lin) * post_ref[...]
    middle_ref[...] = middle
    two_ref[...] = (middle * norm_scale(middle) * pre_ref[...]).astype(BF)


def output_norm(parts, x, scale, post_gain, pre_gain):
    rows, model = x.shape
    whole = pl.BlockSpec(memory_space=pltpu.VMEM)
    return pl.pallas_call(
        output_norm_kernel,
        in_specs=[whole] * 7,
        out_specs=[whole] * 3,
        out_shape=[
            jax.ShapeDtypeStruct((rows, model), F32),
            jax.ShapeDtypeStruct((rows, model), F32),
            jax.ShapeDtypeStruct((rows, model), BF),
        ],
        compiler_params=pltpu.CompilerParams(vmem_limit_bytes=VMEM_LIMIT),
        cost_estimate=pl.CostEstimate(flops=20 * rows * model, bytes_accessed=18 * rows * model, transcendentals=0),
        name="output_norm",
    )(*parts, x, scale[None], post_gain[None], pre_gain[None])


def loss_kernel(
    live_ref,
    part_ref,
    from_x_ref,
    from_y_ref,
    middle_ref,
    cot_ref,
    scale_ref,
    gain_ref,
    mixed_ref,
    round_ref,
    gain_sum_ref,
    scale_sum_ref,
):
    live = live_ref[0, 0]
    raw = part_ref[...].astype(F32) + from_x_ref[...].astype(F32) + from_y_ref[...].astype(F32)
    scale, gain = scale_ref[...], gain_ref[...]
    lin = raw * scale
    mixed_ref[...] = ((middle_ref[...] + lin * norm_scale(lin) * gain) * live).astype(BF)
    back, gain_sum_ref[...] = norm_back(lin, gain, cot_ref[...].astype(F32) * live)
    round_ref[...] = (back * scale).astype(BF)
    scale_sum_ref[...] = jnp.sum(raw * back, axis=0, keepdims=True)


def loss_step(live, parts, middle, cot, scale, gain):
    rows, model = middle.shape
    whole = pl.BlockSpec(memory_space=pltpu.VMEM)
    return pl.pallas_call(
        loss_kernel,
        in_specs=[pl.BlockSpec(memory_space=pltpu.SMEM)] + [whole] * 7,
        out_specs=[whole] * 4,
        out_shape=[
            jax.ShapeDtypeStruct((rows, model), BF),
            jax.ShapeDtypeStruct((rows, model), BF),
            jax.ShapeDtypeStruct((1, model), F32),
            jax.ShapeDtypeStruct((1, model), F32),
        ],
        compiler_params=pltpu.CompilerParams(vmem_limit_bytes=VMEM_LIMIT),
        cost_estimate=pl.CostEstimate(flops=20 * rows * model, bytes_accessed=16 * rows * model, transcendentals=0),
        name="loss_step",
    )(live, *parts, middle, cot, scale[None], gain[None])


def output_back_kernel(
    live_ref,
    part_ref,
    from_x_ref,
    from_y_ref,
    middle_ref,
    raw_ref,
    cot_ref,
    scale_ref,
    post_ref,
    pre_ref,
    middle_grad_ref,
    round_ref,
    pre_sum_ref,
    post_sum_ref,
    scale_sum_ref,
):
    two_grad = part_ref[...].astype(F32) + from_x_ref[...].astype(F32) + from_y_ref[...].astype(F32)
    back, pre_sum_ref[...] = norm_back(middle_ref[...], pre_ref[...], two_grad)
    middle_grad = cot_ref[...].astype(F32) * live_ref[0, 0] + back
    middle_grad_ref[...] = middle_grad
    raw, scale = raw_ref[...], scale_ref[...]
    lin_grad, post_sum_ref[...] = norm_back(raw * scale, post_ref[...], middle_grad)
    scale_sum_ref[...] = jnp.sum(raw * lin_grad, axis=0, keepdims=True)
    round_ref[...] = (lin_grad * scale).astype(BF)


def output_back(live, parts, middle, raw, cot, scale, post_gain, pre_gain):
    rows, model = middle.shape
    whole = pl.BlockSpec(memory_space=pltpu.VMEM)
    return pl.pallas_call(
        output_back_kernel,
        in_specs=[pl.BlockSpec(memory_space=pltpu.SMEM)] + [whole] * 9,
        out_specs=[whole] * 5,
        out_shape=[
            jax.ShapeDtypeStruct((rows, model), F32),
            jax.ShapeDtypeStruct((rows, model), BF),
            jax.ShapeDtypeStruct((1, model), F32),
            jax.ShapeDtypeStruct((1, model), F32),
            jax.ShapeDtypeStruct((1, model), F32),
        ],
        compiler_params=pltpu.CompilerParams(vmem_limit_bytes=VMEM_LIMIT),
        cost_estimate=pl.CostEstimate(flops=40 * rows * model, bytes_accessed=24 * rows * model, transcendentals=0),
        name="output_back",
    )(live, *parts, middle, raw, cot, scale[None], post_gain[None], pre_gain[None])


def head_back_kernel(width, count, *refs):
    pieces = refs[:count]
    w_ref, do_ref, joined, rows_held, w_held, piece_sems, out_sems = refs[count:]
    gathered = piece_copies(pieces, rows_held, piece_sems)
    start_on_first(gathered)

    @pl.when(pl.program_id(0) == 0)
    def _():
        w_held[...] = dequantized(w_ref[...], width)
        for copy in gathered:
            copy.wait()

    copies = keep_copies((rows_held,), (joined,), out_sems)
    start_on_first(copies)
    chunk = do_ref.shape[0]
    part = rows_held[pl.ds(pl.multiple_of(pl.program_id(0) * chunk, chunk), chunk)]
    do_ref[...] = dot_nt(part, w_held[...]).astype(BF)
    wait_on_last(copies)


def head_back(width, pieces, codes):
    rows = sum(piece.shape[0] for piece in pieces)
    model = codes.shape[1]
    chunk = min(rows, 256)
    whole = pl.BlockSpec(memory_space=pl.ANY)
    return pl.pallas_call(
        functools.partial(head_back_kernel, width, len(pieces)),
        grid=(rows // chunk,),
        in_specs=[whole] * len(pieces) + [pl.BlockSpec((HD, model), lambda i: (0, 0))],
        out_specs=[pl.BlockSpec((chunk, HD), lambda i: (i, 0)), whole],
        out_shape=[
            jax.ShapeDtypeStruct((rows, HD), BF),
            jax.ShapeDtypeStruct((rows, model), BF),
        ],
        scratch_shapes=[
            pltpu.VMEM((rows, model), BF),
            pltpu.VMEM((HD, model), BF),
            pltpu.SemaphoreType.DMA((len(pieces),)),
            pltpu.SemaphoreType.DMA((1,)),
        ],
        compiler_params=pltpu.CompilerParams(vmem_limit_bytes=VMEM_LIMIT),
        cost_estimate=pl.CostEstimate(
            flops=2 * rows * HD * model, bytes_accessed=4 * rows * model, transcendentals=0
        ),
        name="head_back",
    )(*pieces, codes)


def join_kernel(starts, *refs):
    result = refs[-1]
    step = pl.program_id(0)
    for piece, start in zip(refs[:-1], starts):

        @pl.when(step == start // result.shape[0])
        def _(piece=piece, start=start):
            result[pl.ds(start % result.shape[0], piece.shape[0])] = piece[...]


def join(*pieces):
    starts = [0]
    for piece in pieces:
        starts.append(starts[-1] + piece.shape[0])
    total, cols = starts[-1], pieces[0].shape[1]
    rows = pieces[0].shape[0]
    return pl.pallas_call(
        functools.partial(join_kernel, tuple(starts[:-1])),
        grid=(total // rows,),
        in_specs=[pl.BlockSpec(piece.shape, lambda i: (0, 0)) for piece in pieces],
        out_specs=pl.BlockSpec((rows, cols), lambda i: (i, 0)),
        out_shape=jax.ShapeDtypeStruct((total, cols), pieces[0].dtype),
        compiler_params=pltpu.CompilerParams(vmem_limit_bytes=VMEM_LIMIT),
        cost_estimate=pl.CostEstimate(flops=0, bytes_accessed=4 * total * cols, transcendentals=0),
        name="join",
    )(*pieces)


GELU_A = 0.7978845608028654
GELU_B = 0.044715


def load_codes(width, codes, held, sems):
    copies = [
        pltpu.make_async_copy(source, target, sems.at[i])
        for i, (source, target) in enumerate(zip(codes, held))
    ]
    for copy in copies:
        copy.start()
    for copy, target in zip(copies, held):
        copy.wait()
        rows = target.shape[0]
        step = 128 if rows % 128 == 0 else 16

        def turn(i, carry, target=target, step=step):
            part = pl.ds(pl.multiple_of(i * step, step), step)
            target[part] = dequantized(target[part], width)
            return carry

        lax.fori_loop(0, rows // step, turn, 0)


def halves_specs(rows, model, chunk):
    steps = rows // chunk // 2
    low = pl.BlockSpec((chunk, model), lambda i: (jnp.minimum(i, steps - 1), 0))
    high = pl.BlockSpec((chunk, model), lambda i: (jnp.maximum(i - steps, 0), 0))
    return [low, high], [jax.ShapeDtypeStruct((rows // 2, model), BF)] * 2


def store_halves(low_ref, high_ref, value):
    step, steps = pl.program_id(0), pl.num_programs(0)

    @pl.when(step < steps // 2)
    def _():
        low_ref[...] = value

    @pl.when(step >= steps // 2)
    def _():
        high_ref[...] = value


def keep_copies(held, kept, sems):
    return [
        pltpu.make_async_copy(source, target, sems.at[i])
        for i, (source, target) in enumerate(zip(held, kept))
    ]


def start_on_first(copies):
    @pl.when(pl.program_id(0) == 0)
    def _():
        for copy in copies:
            copy.start()


def wait_on_last(copies):
    @pl.when(pl.program_id(0) == pl.num_programs(0) - 1)
    def _():
        for copy in copies:
            copy.wait()


def piece_copies(pieces, held, sems):
    copies = []
    at = 0
    for i, piece in enumerate(pieces):
        rows = piece.shape[0]
        copies.append(pltpu.make_async_copy(piece, held.at[pl.ds(at, rows)], sems.at[i]))
        at += rows
    return copies


def ffn_in_kernel(width, count, *refs):
    pieces = refs[:count]
    (
        g_hbm,
        u_hbm,
        gs_ref,
        us_ref,
        gate_ref,
        up_ref,
        hidden_ref,
        a_hbm,
        gw_hbm,
        uw_hbm,
        a_held,
        g_held,
        u_held,
        piece_sems,
        sems,
        out_sems,
    ) = refs[count:]
    gathered = piece_copies(pieces, a_held, piece_sems)
    start_on_first(gathered)

    @pl.when(pl.program_id(0) == 0)
    def _():
        load_codes(width, (g_hbm, u_hbm), (g_held, u_held), sems)
        for copy in gathered:
            copy.wait()

    copies = keep_copies((a_held, g_held, u_held), (a_hbm, gw_hbm, uw_hbm), out_sems)
    start_on_first(copies)
    chunk = gate_ref.shape[0]
    a = a_held[pl.ds(pl.multiple_of(pl.program_id(0) * chunk, chunk), chunk)]
    gate = dot(a, g_held[...])
    up = dot(a, u_held[...])
    gate_ref[...] = gate.astype(BF)
    up_ref[...] = up.astype(BF)
    gate = gate * gs_ref[...]
    inner = jnp.tanh(GELU_A * (gate + GELU_B * gate * gate * gate))
    hidden_ref[...] = (0.5 * gate * (1.0 + inner) * (up * us_ref[...])).astype(BF)
    wait_on_last(copies)


def ffn_in(width, pieces, gate_codes, up_codes, g_scale, u_scale):
    rows = sum(piece.shape[0] for piece in pieces)
    model, features = gate_codes.shape
    chunk = min(rows, 256)
    whole = pl.BlockSpec(memory_space=pl.ANY)
    vector = pl.BlockSpec((1, features), lambda i: (0, 0))
    block = pl.BlockSpec((chunk, features), lambda i: (i, 0))
    return pl.pallas_call(
        functools.partial(ffn_in_kernel, width, len(pieces)),
        grid=(rows // chunk,),
        in_specs=[whole] * len(pieces) + [whole, whole, vector, vector],
        out_specs=[block] * 3 + [whole] * 3,
        out_shape=[jax.ShapeDtypeStruct((rows, features), BF)] * 3
        + [jax.ShapeDtypeStruct((rows, model), BF)]
        + [jax.ShapeDtypeStruct((model, features), BF)] * 2,
        scratch_shapes=[
            pltpu.VMEM((rows, model), BF),
            pltpu.VMEM((model, features), BF),
            pltpu.VMEM((model, features), BF),
            pltpu.SemaphoreType.DMA((len(pieces),)),
            pltpu.SemaphoreType.DMA((2,)),
            pltpu.SemaphoreType.DMA((3,)),
        ],
        compiler_params=pltpu.CompilerParams(vmem_limit_bytes=VMEM_LIMIT),
        cost_estimate=pl.CostEstimate(
            flops=4 * rows * model * features,
            bytes_accessed=2 * (rows * model + 2 * model * features + 3 * rows * features),
            transcendentals=rows * features,
        ),
        name="ffn_in",
    )(*pieces, gate_codes, up_codes, g_scale[None], u_scale[None])


def down_grad_kernel(counts, *refs):
    pieces, refs = refs[: sum(counts)], refs[sum(counts) :]
    widths = len(counts)
    h_refs, scale_ref, out_ref = refs[:widths], refs[widths], refs[widths + 1]
    joined, held = refs[widths + 2 : 2 * widths + 2], refs[2 * widths + 2]
    piece_sems, out_sems = refs[2 * widths + 3 :]
    groups = []
    at = 0
    for w, count in enumerate(counts):
        groups.append(piece_copies(pieces[at : at + count], held.at[w], piece_sems.at[w]))
        at += count
    for group in groups:
        start_on_first(group)
    copies = keep_copies([held.at[w] for w in range(widths)], joined, out_sems)
    first = pl.program_id(0) == 0
    product = None
    for w in range(widths):

        @pl.when(first)
        def _(w=w):
            for copy in groups[w]:
                copy.wait()
            copies[w].start()

        part = dot_tn(h_refs[w][...], held[w])
        product = part if product is None else product + part
    out_ref[...] = (product / scale_ref[...]).astype(BF)
    wait_on_last(copies)


def down_gradient(hiddens, piece_lists, scale):
    rows, features = hiddens[0].shape
    model = scale.shape[0]
    widths = len(hiddens)
    counts = tuple(len(pieces) for pieces in piece_lists)
    chunk = 128 if features % 128 == 0 else features
    whole = pl.BlockSpec(memory_space=pl.ANY)
    return pl.pallas_call(
        functools.partial(down_grad_kernel, counts),
        grid=(features // chunk,),
        in_specs=[whole] * sum(counts)
        + [pl.BlockSpec((rows, chunk), lambda i: (0, i))] * widths
        + [pl.BlockSpec((1, model), lambda i: (0, 0))],
        out_specs=[pl.BlockSpec((chunk, model), lambda i: (i, 0))] + [whole] * widths,
        out_shape=[jax.ShapeDtypeStruct((features, model), BF)]
        + [jax.ShapeDtypeStruct((rows, model), BF)] * widths,
        scratch_shapes=[
            pltpu.VMEM((widths, rows, model), BF),
            pltpu.SemaphoreType.DMA((widths, max(counts))),
            pltpu.SemaphoreType.DMA((widths,)),
        ],
        compiler_params=pltpu.CompilerParams(vmem_limit_bytes=VMEM_LIMIT),
        cost_estimate=pl.CostEstimate(
            flops=2 * widths * rows * model * features,
            bytes_accessed=2 * (2 * widths * rows * model + features * (model + widths * rows)),
            transcendentals=0,
        ),
        name="down_grad",
    )(*[piece for pieces in piece_lists for piece in pieces], *hiddens, scale[None])


def ffn_out_kernel(width, h_ref, d_hbm, low_ref, high_ref, dw_hbm, d_held, sems, out_sems):
    @pl.when(pl.program_id(0) == 0)
    def _():
        load_codes(width, (d_hbm,), (d_held,), sems)

    copies = keep_copies((d_held,), (dw_hbm,), out_sems)
    start_on_first(copies)
    store_halves(low_ref, high_ref, dot(h_ref[...], d_held[...]).astype(BF))
    wait_on_last(copies)


def ffn_out(width, hidden, down_codes):
    rows, features = hidden.shape
    model = down_codes.shape[1]
    chunk = min(rows // 2, 256)
    whole = pl.BlockSpec(memory_space=pl.ANY)
    specs, shapes = halves_specs(rows, model, chunk)
    return pl.pallas_call(
        functools.partial(ffn_out_kernel, width),
        grid=(rows // chunk,),
        in_specs=[pl.BlockSpec((chunk, features), lambda i: (i, 0)), whole],
        out_specs=specs + [whole],
        out_shape=shapes + [jax.ShapeDtypeStruct((features, model), BF)],
        scratch_shapes=[
            pltpu.VMEM((features, model), BF),
            pltpu.SemaphoreType.DMA((1,)),
            pltpu.SemaphoreType.DMA((1,)),
        ],
        compiler_params=pltpu.CompilerParams(vmem_limit_bytes=VMEM_LIMIT),
        cost_estimate=pl.CostEstimate(
            flops=2 * rows * model * features,
            bytes_accessed=2 * (rows * model + 2 * model * features + rows * features),
            transcendentals=0,
        ),
        name="ffn_out",
    )(hidden, down_codes)


def ffn_back_kernel(
    dr_ref,
    gate_ref,
    up_ref,
    d_hbm,
    g_hbm,
    u_hbm,
    gs_ref,
    us_ref,
    after_hbm,
    low_ref,
    high_ref,
    gr_ref,
    ur_ref,
    gsum_ref,
    usum_ref,
    d_held,
    g_held,
    u_held,
    sems,
):
    del after_hbm
    first = pl.program_id(0) == 0
    copies = keep_copies((d_hbm, g_hbm, u_hbm), (d_held, g_held, u_held), sems)
    start_on_first(copies)

    @pl.when(first)
    def _():
        gsum_ref[...] = jnp.zeros_like(gsum_ref)
        usum_ref[...] = jnp.zeros_like(usum_ref)
        copies[0].wait()

    hidden_grad = dot_nt(dr_ref[...], d_held[...])
    gate_raw = gate_ref[...].astype(F32)
    up_raw = up_ref[...].astype(F32)
    gate = gate_raw * gs_ref[...]
    up = up_raw * us_ref[...]
    square = gate * gate
    inner = jnp.tanh(GELU_A * (gate + GELU_B * gate * square))
    half_sum = 0.5 * (1.0 + inner)
    slope = half_sum + 0.5 * gate * (1.0 - inner * inner) * (
        GELU_A * (1.0 + 3.0 * GELU_B * square)
    )
    gate_grad = hidden_grad * up * slope
    up_grad = hidden_grad * (gate * half_sum)
    gsum_ref[...] += jnp.sum(gate_raw * gate_grad, axis=0, keepdims=True)
    usum_ref[...] += jnp.sum(up_raw * up_grad, axis=0, keepdims=True)
    gate_round = (gate_grad * gs_ref[...]).astype(BF)
    up_round = (up_grad * us_ref[...]).astype(BF)
    gr_ref[...] = gate_round
    ur_ref[...] = up_round

    @pl.when(first)
    def _():
        copies[1].wait()
        copies[2].wait()

    store_halves(
        low_ref,
        high_ref,
        (dot_nt(gate_round, g_held[...]) + dot_nt(up_round, u_held[...])).astype(BF),
    )


def ffn_back(down_round, gate_raw, up_raw, down_w, gate_w, up_w, g_scale, u_scale, after):
    rows, model = down_round.shape
    features = gate_w.shape[1]
    chunk = min(rows // 2, 256)
    whole = pl.BlockSpec(memory_space=pl.ANY)
    vector = pl.BlockSpec((1, features), lambda i: (0, 0))
    block = pl.BlockSpec((chunk, features), lambda i: (i, 0))
    wide = pl.BlockSpec((chunk, model), lambda i: (i, 0))
    specs, shapes = halves_specs(rows, model, chunk)
    return pl.pallas_call(
        ffn_back_kernel,
        grid=(rows // chunk,),
        in_specs=[wide, block, block, whole, whole, whole, vector, vector, whole],
        out_specs=specs + [block, block, vector, vector],
        out_shape=shapes
        + [
            jax.ShapeDtypeStruct((rows, features), BF),
            jax.ShapeDtypeStruct((rows, features), BF),
            jax.ShapeDtypeStruct((1, features), F32),
            jax.ShapeDtypeStruct((1, features), F32),
        ],
        scratch_shapes=[
            pltpu.VMEM((features, model), BF),
            pltpu.VMEM((model, features), BF),
            pltpu.VMEM((model, features), BF),
            pltpu.SemaphoreType.DMA((3,)),
        ],
        compiler_params=pltpu.CompilerParams(vmem_limit_bytes=VMEM_LIMIT),
        cost_estimate=pl.CostEstimate(
            flops=6 * rows * model * features,
            bytes_accessed=2 * (2 * rows * model + 3 * model * features + 4 * rows * features),
            transcendentals=rows * features,
        ),
        name="ffn_back",
    )(down_round, gate_raw, up_raw, down_w, gate_w, up_w, g_scale[None], u_scale[None], after)


def project_back_kernel(round_ref, w_hbm, low_ref, high_ref, held, sems):
    copies = keep_copies((w_hbm,), (held,), sems)
    start_on_first(copies)

    @pl.when(pl.program_id(0) == 0)
    def _():
        copies[0].wait()

    product = dot_nt(round_ref[0], held[0])
    for w in range(1, SLOTS):
        product = product + dot_nt(round_ref[w], held[w])
    store_halves(low_ref, high_ref, product.astype(BF))


def project_back(rounded, weights):
    _, rows, cols = rounded.shape
    model = weights.shape[1]
    chunk = min(rows // 2, 256)
    specs, shapes = halves_specs(rows, model, chunk)
    return pl.pallas_call(
        project_back_kernel,
        grid=(rows // chunk,),
        in_specs=[
            pl.BlockSpec((SLOTS, chunk, cols), lambda i: (0, i, 0)),
            pl.BlockSpec(memory_space=pl.ANY),
        ],
        out_specs=specs,
        out_shape=shapes,
        scratch_shapes=[pltpu.VMEM((SLOTS, model, cols), BF), pltpu.SemaphoreType.DMA((1,))],
        compiler_params=pltpu.CompilerParams(vmem_limit_bytes=VMEM_LIMIT),
        cost_estimate=pl.CostEstimate(
            flops=2 * SLOTS * rows * model * cols,
            bytes_accessed=2 * (rows * model + SLOTS * cols * (model + rows)),
            transcendentals=0,
        ),
        name="project_back",
    )(rounded, weights)


def shards(
    tokens,
    query_codes,
    key_codes,
    value_codes,
    output_codes,
    gate_codes,
    up_codes,
    down_codes,
    query_scale,
    key_scale,
    value_scale,
    output_scale,
    gate_scale,
    up_scale,
    down_scale,
    pre_attn_gain,
    post_attn_gain,
    pre_ffw_gain,
    post_ffw_gain,
    slot_width,
    slot_live,
    cotangent,
):
    planes = lax.axis_size("dp")
    width = lax.axis_size("fsdp")
    devices = planes * width
    group_count = width // 8
    rank = lax.axis_index("fsdp")
    me = lax.axis_index("dp") * width + rank
    t_index, group = rank % 8, rank // 8
    core = rank % 2
    CORE, X, Y = 1, 2, 4
    groups = None
    if group_count > 1:
        groups = [[g * 8 + j for j in range(8)] for g in range(group_count)]
        across = [[g * 8 + j for g in range(group_count)] for j in range(8)]

    def swap(values, mask):
        return lax.ppermute(values, "fsdp", [(i, i ^ mask) for i in range(width)])

    def swap_all(values, mask):
        return lax.ppermute(values, ALL, [(i, i ^ mask) for i in range(devices)])

    tok_rows, model = tokens.shape
    group_rows = 8 * tok_rows
    d_rows = query_codes.shape[0]
    o_rows = output_codes.shape[0]
    ff_rows = down_codes.shape[0]
    q_cols = query_codes.shape[1] // 8
    k_cols = key_codes.shape[1] // 8
    ff_cols = ff_rows * planes * group_count
    widths = range(SLOTS)

    def tp_pieces(block):
        from_x = swap(block, X)
        from_y = swap(block, Y)
        cut = block.shape[0] // 2
        first = swap(from_y[:cut], X)
        second = swap(from_x[cut:], Y)
        same = [block, from_x, from_y, first, second]
        return same + [swap(piece, CORE) for piece in same]

    def tp_gather(block):
        return join(*tp_pieces(block))

    def after(values, *others):
        return lax.optimization_barrier((values, *others))[0]

    def core_sum(low, high):
        return (low.astype(F32) + swap(high, CORE).astype(F32)).astype(BF)

    def tp_scatter(low, high):
        return plane_sum(core_sum(low, high))

    def plane_sum(pair):
        rows = pair.shape[0] // 4
        cut = rows // 2
        pair = pair.reshape(2, 2, rows, model)
        got_x = swap(pair[1, 1, :cut], X)
        got_y = swap(pair[1, 1, cut:], Y)
        for_x = jnp.concatenate(
            [pair[0, 1, :cut], (pair[0, 1, cut:].astype(F32) + got_y.astype(F32)).astype(BF)]
        )
        for_y = jnp.concatenate(
            [(pair[1, 0, :cut].astype(F32) + got_x.astype(F32)).astype(BF), pair[1, 0, cut:]]
        )
        return pair[0, 0], swap(for_x, X), swap(for_y, Y)

    def total(parts):
        return sum(part.astype(F32) for part in parts)

    def tp_columns(blocks):
        return lax.all_to_all(blocks, "fsdp", 0, 0, tiled=True, axis_index_groups=groups)

    def gather_rows(rows):
        if group_count > 1:
            rows = lax.all_gather(rows, "fsdp", axis=0, tiled=True, axis_index_groups=across)
        return lax.all_gather(rows, "dp", axis=0, tiled=True)

    def scatter_rows(grad):
        rows = lax.psum_scatter(grad, "dp", scatter_dimension=0, tiled=True)
        if group_count > 1:
            rows = lax.psum_scatter(
                rows, "fsdp", scatter_dimension=0, tiled=True, axis_index_groups=across
            )
        return rows

    small = jnp.concatenate(
        [query_scale, key_scale, value_scale, output_scale, gate_scale, up_scale, down_scale]
    )
    all_small = small[None]
    for bit in range(devices.bit_length() - 1):
        all_small = jnp.concatenate([all_small, swap_all(all_small, 1 << bit)], axis=0)
    order = jnp.arange(devices, dtype=jnp.int32) ^ me
    all_small = all_small[order]
    cuts = []
    at = 0
    for vector in (
        query_scale,
        key_scale,
        value_scale,
        output_scale,
        gate_scale,
        up_scale,
        down_scale,
    ):
        cuts.append(all_small[:, at : at + vector.shape[0]].reshape(-1))
        at += vector.shape[0]
    q_scale_all, k_scale_all, v_scale_all, o_scale_all, g_scale_all, u_scale_all, d_scale_all = cuts

    def own_ff(vector):
        cut = vector.reshape(planes * group_count, 8, ff_rows)
        return lax.dynamic_index_in_dim(cut, t_index, 1, keepdims=False).reshape(ff_cols)

    qkv_scale = jnp.concatenate(
        [
            lax.dynamic_slice_in_dim(q_scale_all, t_index * q_cols, q_cols),
            lax.dynamic_slice_in_dim(k_scale_all, t_index * k_cols, k_cols),
            lax.dynamic_slice_in_dim(v_scale_all, t_index * k_cols, k_cols),
        ]
    )
    g_scale = own_ff(g_scale_all)
    u_scale = own_ff(u_scale_all)

    def by_head(codes):
        return codes.reshape(codes.shape[0], 8, -1).transpose(1, 0, 2)

    def by_head_back(blocks):
        return blocks.transpose(1, 0, 2).reshape(blocks.shape[1], -1)

    def by_ff(codes):
        cut = codes.reshape(d_rows, planes * group_count, 8, ff_rows)
        return cut.transpose(2, 0, 1, 3).reshape(8, d_rows, ff_cols)

    def by_ff_back(blocks):
        cut = blocks.reshape(8, d_rows, planes * group_count, ff_rows)
        return cut.transpose(1, 2, 0, 3).reshape(d_rows, 8 * ff_cols)

    def merged(blocks):
        return blocks.reshape(8 * d_rows, blocks.shape[2])

    qkv_blocks = jnp.concatenate(
        [by_head(query_codes), by_head(key_codes), by_head(value_codes)], axis=2
    )
    inputs = tokens.astype(F32)
    qkv_codes = gather_rows(merged(tp_columns(qkv_blocks)))
    normed = tp_gather(rms_norm(inputs, pre_attn_gain).astype(BF))

    whole_heads = group_count == 1 and 8 % planes == 0
    heads_per_plane = max(1, 8 // planes)

    def turn(step):
        pairs = []
        for source in range(8):
            plane = (source + step) % planes
            pairs.append((source, plane * heads_per_plane + source // planes))
        return pairs

    def pieces_to_heads(pieces):
        result = jnp.zeros_like(pieces)
        for step in range(planes):
            piece = lax.dynamic_index_in_dim(pieces, (rank + step) % planes, 0, keepdims=False)
            moved = lax.ppermute(piece, "fsdp", turn(step))
            place = (rank // heads_per_plane - step) % planes
            result = lax.dynamic_update_index_in_dim(result, moved, place, 0)
        return result

    def heads_to_pieces(pieces):
        result = jnp.zeros_like(pieces)
        for step in range(planes):
            place = (rank // heads_per_plane - step) % planes
            piece = lax.dynamic_index_in_dim(pieces, place, 0, keepdims=False)
            moved = lax.ppermute(piece, "fsdp", [(b, a) for a, b in turn(step)])
            result = lax.dynamic_update_index_in_dim(result, moved, (rank + step) % planes, 0)
        return result

    gate_mine = merged(tp_columns(by_ff(after(gate_codes, normed, qkv_scale))))
    normed, gate_mine = lax.optimization_barrier((normed, gate_mine))
    gate_codes_t = gather_rows(gate_mine)
    output_pieces = gather_rows(output_codes)

    blocks_at = jnp.stack([t_index ^ (c + 2 * x + 4 * y) for c in (0, 1) for y in (0, 1) for x in (0, 1)])
    positions = ((group * 8 + blocks_at) * tok_rows)[:, None] + jnp.arange(tok_rows, dtype=jnp.int32)
    positions = positions.reshape(group_rows)
    far = jnp.int32(1 << 30)
    key_positions = []
    for back in range(group_count):
        earlier = positions - back * group_rows
        key_positions.append(jnp.where(earlier >= 0, earlier, far))
    kpos = jnp.concatenate(key_positions)[None, :]
    qpos = positions[:, None]
    inv_rates = 10000.0 ** (-jnp.arange(HALF, dtype=F32) / HALF)
    angles = positions.astype(F32)[:, None] * inv_rates[None, :]
    cosine, sine = jnp.cos(angles), jnp.sin(angles)
    key_angles = jnp.concatenate(
        [(positions - back * group_rows).astype(F32) for back in range(group_count)]
    )[:, None] * inv_rates[None, :]

    qkv_raw, q, kv_own, qkv_w = project(normed, qkv_codes, qkv_scale, cosine, sine)
    k_near, v_near = whole_heads_of(core, kv_own, swap(kv_own, CORE), cosine, sine)

    if whole_heads:
        head_codes = pieces_to_heads(output_pieces.reshape(planes, o_rows, model)).reshape(HD, model)
    else:
        every = lax.all_gather(output_codes, ALL, axis=0, tiled=True)
        head_codes = lax.dynamic_slice_in_dim(every, t_index * HD, HD, 0)

    def turned(values):
        middle_row = group_rows // 2
        return jnp.concatenate([values[..., middle_row:, :], values[..., :middle_row, :]], axis=-2)

    def back_pairs(back):
        return [(i, i + 8 * back) for i in range(width) if i + 8 * back < width]

    k_parts, v_parts = [k_near], [v_near]
    for back in range(1, group_count):
        k_parts.append(lax.ppermute(k_near, "fsdp", back_pairs(back)))
        v_parts.append(lax.ppermute(v_near, "fsdp", back_pairs(back)))
    k_all = jnp.concatenate(k_parts, axis=1)
    v_all = jnp.concatenate(v_parts, axis=1)
    attended = attend(qpos, kpos, q, k_all, v_all, tok_rows)

    up_codes_t = gather_rows(merged(tp_columns(by_ff(after(up_codes, k_near)))))
    down_codes_t = gather_rows(down_codes)

    slot_of, live_of, cot_of = [], [], []
    for w in widths:
        slot = jnp.int32(0)
        for s in range(SLOTS):
            slot = jnp.where(slot_width[0, s] == w, s, slot)
        slot_of.append(slot)
        live = lax.dynamic_index_in_dim(slot_live[0], slot, 0, keepdims=False)
        live_of.append(live.astype(F32).reshape(1, 1))
        cot_of.append(lax.dynamic_index_in_dim(cotangent, slot, 0, keepdims=False))
    kept = [dict() for w in widths]
    for w in widths:
        k = kept[w]
        blocks = attended if w == 0 else after(attended, kept[w - 1]["low"])
        k["low"], high = output_partial(w, blocks, head_codes)
        k["out_raw"], k["middle"], two = output_norm(
            tp_scatter(k["low"], high), tokens, o_scale_all, post_attn_gain, pre_ffw_gain
        )
        k["two_pieces"] = tp_pieces(two)
    for w in widths:
        k = kept[w]
        (
            k["gate_raw"],
            k["up_raw"],
            k["hidden"],
            k["normed_two"],
            k["gate_w"],
            k["up_w"],
        ) = ffn_in(w, k["two_pieces"], gate_codes_t, up_codes_t, g_scale, u_scale)

    hiddens = lax.optimization_barrier(tuple(kept[w]["hidden"] for w in widths))
    for w in widths:
        k = kept[w]
        k["hidden"] = hiddens[w] if w == 0 else after(hiddens[w], kept[w - 1]["down_w"])
        if w == 2:
            k["hidden"], kept[0]["pair"] = lax.optimization_barrier((k["hidden"], kept[0]["pair"]))
        low, high, k["down_w"] = ffn_out(w, k["hidden"], down_codes_t)
        k["pair"] = core_sum(low, high)
    for w in widths:
        kept[w]["down_parts"] = plane_sum(kept[w]["pair"])

    mixed = jnp.zeros((SLOTS, tok_rows, model), BF)
    for w in widths:
        k = kept[w]
        cot = cot_of[w] if w == 0 else after(cot_of[w], kept[w - 1]["gain_four"])
        result, rounded, k["gain_four"], k["down_scale_sum"] = loss_step(
            live_of[w], k["down_parts"], k["middle"], cot, d_scale_all, post_ffw_gain
        )
        mixed = lax.dynamic_update_index_in_dim(mixed, result, slot_of[w], 0)
        k["down_pieces"] = tp_pieces(rounded)
    down_total, *down_rounds = down_gradient(
        [kept[w]["hidden"] for w in widths], [kept[w]["down_pieces"] for w in widths], d_scale_all
    )
    down_sum = scatter_rows(down_total)
    for w in widths:
        k = kept[w]
        low, high, k["gate_round"], k["up_round"], k["gate_sum"], k["up_sum"] = ffn_back(
            down_rounds[w],
            k["gate_raw"],
            k["up_raw"],
            k["down_w"],
            k["gate_w"],
            k["up_w"],
            g_scale,
            u_scale,
            down_total if w == 0 else kept[w - 1]["gate_sum"],
        )
        k["two_parts"] = tp_scatter(low, high)
    normed_two_rows = jnp.concatenate([kept[w]["normed_two"] for w in widths], axis=0)
    gate_rounds = [kept[w]["gate_round"] for w in widths]
    *gate_rounds, down_sum = lax.optimization_barrier((*gate_rounds, down_sum))
    gate_total = dot_tn(normed_two_rows, jnp.concatenate(gate_rounds, axis=0))
    gate_sum = scatter_rows((gate_total / g_scale).astype(BF))
    for w in widths:
        k = kept[w]
        cot = cot_of[w] if w == 0 else after(cot_of[w], kept[w - 1]["gain_two"])
        k["middle_grad"], rounded, k["gain_three"], k["gain_two"], k["out_scale_sum"] = output_back(
            live_of[w],
            k["two_parts"],
            k["middle"],
            k["out_raw"],
            cot,
            o_scale_all,
            post_attn_gain,
            pre_ffw_gain,
        )
        k["out_pieces"] = tp_pieces(rounded)
    up_rounds = [kept[w]["up_round"] for w in widths]
    *up_rounds, _ = lax.optimization_barrier((*up_rounds, kept[2]["gain_two"]))
    up_total = dot_tn(normed_two_rows, jnp.concatenate(up_rounds, axis=0))
    up_total, gate_sum = lax.optimization_barrier(((up_total / u_scale).astype(BF), gate_sum))
    up_sum = scatter_rows(up_total)
    for w in widths:
        k = kept[w]
        codes = head_codes if w == 0 else after(head_codes, kept[w - 1]["o_grad"])
        k["o_grad"], k["out_round"] = head_back(w, k["out_pieces"], codes)

    o_grad = jnp.stack([kept[w]["o_grad"] for w in widths])
    turns = (cosine, sine, jnp.cos(key_angles), jnp.sin(key_angles))
    out_total = dot_tn(
        attended.reshape(SLOTS * group_rows, HD),
        jnp.concatenate([kept[w]["out_round"] for w in widths], axis=0),
    )
    out_total = (out_total / o_scale_all).astype(BF)
    if whole_heads:
        out_pieces = heads_to_pieces(out_total.reshape(planes, o_rows, model))
        out_pieces = out_pieces.reshape(planes * o_rows, model)
    else:
        whole = jnp.zeros((HEADS * HD, model), BF)
        out_pieces = lax.dynamic_update_slice_in_dim(whole, out_total, t_index * HD, 0)
    q_grad, dk, dv = attend_back(qpos, kpos, turns, q, k_all, v_all, o_grad, tok_rows)
    other = 1 - core

    def half_of(values, which):
        return lax.dynamic_slice_in_dim(values, which * k_cols, k_cols, values.ndim - 1)

    kv_grad = None
    for back in range(group_count):
        part = slice(back * group_rows, (back + 1) * group_rows)
        dkv = jnp.concatenate([half_of(dk[:, part], core), half_of(dv[:, part], core)], axis=-1)
        gone = jnp.concatenate([half_of(dk[:, part], other), half_of(dv[:, part], other)], axis=-1)
        dkv = dkv + turned(swap(gone, CORE))
        if back == 0:
            kv_grad = dkv
        else:
            pairs = [(b, a) for a, b in back_pairs(back)]
            kv_grad = kv_grad + lax.ppermute(dkv, "fsdp", pairs)
    qkv_grad = jnp.concatenate([q_grad, kv_grad], axis=-1)
    qkv_round = (qkv_grad * qkv_scale).astype(BF)
    qkv_scale_acc = jnp.sum(qkv_raw.astype(F32) * qkv_grad, axis=(0, 1))
    qkv_rows = jnp.sum(qkv_round.astype(F32), axis=0).astype(BF)
    qkv_total = (dot_tn(normed, qkv_rows) / qkv_scale).astype(BF)
    qkv_total, out_pieces = lax.optimization_barrier((qkv_total, out_pieces))
    qkv_sum = scatter_rows(qkv_total)
    if whole_heads:
        out_sum = scatter_rows(out_pieces)
    else:
        out_sum = lax.psum_scatter(out_pieces, ALL, scatter_dimension=0, tiled=True)
    normed_parts = tp_scatter(*project_back(qkv_round, qkv_w))
    gate_grad = by_ff_back(tp_columns(gate_sum.reshape(8, d_rows, ff_cols))).astype(F32)
    up_grad = by_ff_back(tp_columns(up_sum.reshape(8, d_rows, ff_cols))).astype(F32)
    down_grad = down_sum.reshape(ff_rows, model).astype(F32)
    normed_parts, qkv_sum, gate_grad, up_grad, down_grad = lax.optimization_barrier(
        (normed_parts, qkv_sum, gate_grad, up_grad, down_grad)
    )
    normed_grad = total(normed_parts)
    _, pull_one = jax.vjp(rms_norm, inputs, pre_attn_gain)
    input_part, gain_one = pull_one(normed_grad)
    input_total = input_part + sum(kept[w]["middle_grad"] for w in widths)

    output_grad = out_sum.reshape(o_rows, model).astype(F32)
    qkv_back = tp_columns(qkv_sum.reshape(8, d_rows, q_cols + 2 * k_cols))
    query_grad = by_head_back(qkv_back[:, :, :q_cols]).astype(F32)
    key_grad = by_head_back(qkv_back[:, :, q_cols : q_cols + k_cols]).astype(F32)
    value_grad = by_head_back(qkv_back[:, :, q_cols + k_cols :]).astype(F32)

    def placed(part, count):
        whole = jnp.zeros((8 * count,), F32)
        return lax.dynamic_update_slice_in_dim(whole, part, t_index * count, 0)

    def placed_ff(part):
        whole = jnp.zeros((planes * group_count, 8, ff_rows), F32)
        block = part.reshape(planes * group_count, 1, ff_rows)
        return lax.dynamic_update_slice(whole, block, (0, t_index, 0)).reshape(-1)

    def over_widths(name):
        return sum(kept[w][name][0] for w in widths)

    vectors = [
        placed(qkv_scale_acc[:q_cols], q_cols),
        placed(qkv_scale_acc[q_cols : q_cols + k_cols], k_cols),
        placed(qkv_scale_acc[q_cols + k_cols :], k_cols),
        over_widths("out_scale_sum"),
        placed_ff(over_widths("gate_sum")),
        placed_ff(over_widths("up_sum")),
        over_widths("down_scale_sum"),
        gain_one,
        over_widths("gain_two"),
        over_widths("gain_three"),
        over_widths("gain_four"),
    ]
    summed = jnp.concatenate([v.reshape(devices, -1) for v in vectors], axis=1)[order]
    for bit in reversed(range(devices.bit_length() - 1)):
        keep = 1 << bit
        summed = summed[:keep] + swap_all(summed[keep:], keep)
    summed = summed[0]
    vector_grads = []
    at = 0
    for v in vectors:
        size = v.shape[0] // devices
        vector_grads.append(summed[at : at + size])
        at += size

    return (
        mixed,
        input_total,
        query_grad,
        key_grad,
        value_grad,
        output_grad,
        gate_grad,
        up_grad,
        down_grad,
        *vector_grads,
    )


def solution(mesh):
    rows = P(ALL, None)
    vector = P(ALL)
    in_specs = (
        (rows,) * 8
        + (vector,) * 7
        + (P(),) * 4
        + (P("dp", None), P("dp", None), P(None, ALL, None))
    )
    out_specs = (P(None, ALL, None),) + (rows,) * 8 + (vector,) * 11
    return jax.shard_map(shards, mesh=mesh, in_specs=in_specs, out_specs=out_specs, check_vma=False)
```

```python
import functools

import jax
import jax.numpy as jnp
from jax import lax
from jax.experimental import pallas as pl
from jax.experimental.pallas import tpu as pltpu
from jax.sharding import PartitionSpec as P

HEADS = 8
KV_HEADS = 4
HD = 256
HALF = HD // 2
SLOTS = 3
EPSILON = 1e-06
SOFT_CAP = 50.0
BF = jnp.bfloat16
F32 = jnp.float32
ALL = ("dp", "fsdp")
STEPS = (1.0, 16.0, 64.0)
VMEM_LIMIT = 60 * 1024 * 1024


def dequantized(codes, width):
    step = STEPS[width]
    if width == 0:
        return codes + BF(0.5)
    return jnp.floor(codes * BF(1.0 / step)) * BF(step) + BF(step / 2)


def rms_norm(values, gain_vector):
    return (
        values
        * lax.rsqrt(jnp.mean(values * values, axis=-1, keepdims=True) + EPSILON)
        * gain_vector
    )


def rotate(values, cosine, sine_part):
    first_half = values[..., :HALF]
    second = values[..., HALF:]
    return jnp.concatenate(
        [first_half * cosine - second * sine_part, second * cosine + first_half * sine_part],
        axis=-1,
    )


def dot(left, right):
    return jnp.dot(left, right, preferred_element_type=F32)


def dot_nt(left, right):
    return lax.dot_general(left, right, (((1,), (1,)), ((), ())), preferred_element_type=F32)


def dot_tn(left, right):
    return lax.dot_general(left, right, (((0,), (0,)), ((), ())), preferred_element_type=F32)


def gated(gate_in, up_in):
    return jax.nn.gelu(gate_in, approximate=True) * up_in


def score_block(qpos_ref, kpos_ref, q, k):
    tanh_part = jnp.tanh(dot_nt(q, k) * (1.0 / SOFT_CAP))
    causal = qpos_ref[...] >= kpos_ref[...]
    exp_scores = jnp.where(causal, jnp.exp(SOFT_CAP * tanh_part), 0.0)
    total = jnp.sum(exp_scores, axis=-1, keepdims=True)
    return tanh_part, exp_scores / total


def attend_kernel(qpos_ref, kpos_ref, q_ref, k_ref, v_ref, o_ref):
    _, probs = score_block(qpos_ref, kpos_ref, q_ref[0], k_ref[0])
    o_ref[0] = dot(probs.astype(BF), v_ref[0]).astype(BF)


def attend_back_kernel(
    qpos_ref,
    kpos_ref,
    qcos_ref,
    qsin_ref,
    kcos_ref,
    ksin_ref,
    q_ref,
    k_ref,
    v_ref,
    do_ref,
    dq_ref,
    dk_ref,
    dv_ref,
):
    q, k, v, do = q_ref[0], k_ref[0], v_ref[0], do_ref[0]

    @pl.when(pl.program_id(1) == 0)
    def _():
        dk_ref[...] = jnp.zeros_like(dk_ref)
        dv_ref[...] = jnp.zeros_like(dv_ref)

    tanh_part, probs = score_block(qpos_ref, kpos_ref, q, k)
    prob_grad = dot_nt(do, v)
    row_dot = jnp.sum(probs * prob_grad, axis=-1, keepdims=True)
    score_grad = (probs * (prob_grad - row_dot) * (1.0 - tanh_part * tanh_part)).astype(BF)
    dq = dot(score_grad, k) * HD ** (-0.5)
    dq_ref[0] = rotate(dq, qcos_ref[...], -qsin_ref[...])
    dk_ref[0] += dot_tn(score_grad, q)
    dv_ref[0] += dot_tn(probs.astype(BF), do)

    @pl.when(pl.program_id(1) == pl.num_programs(1) - 1)
    def _():
        dk_ref[0] = rotate(dk_ref[0], kcos_ref[...], -ksin_ref[...])


def attention_specs(q, keys, tok_rows):
    widths, rows, _ = q.shape
    chunk = 2 * tok_rows
    q_spec = pl.BlockSpec((1, chunk, HD), lambda w, i: (w, i, 0))
    k_spec = pl.BlockSpec((1, keys.shape[1], HD), lambda w, i: (w, 0, 0))
    qpos_spec = pl.BlockSpec((chunk, 1), lambda w, i: (i, 0))
    kpos_spec = pl.BlockSpec((1, keys.shape[1]), lambda w, i: (0, 0))
    turn_specs = [pl.BlockSpec((chunk, HALF), lambda w, i: (i, 0))] * 2
    turn_specs += [pl.BlockSpec((keys.shape[1], HALF), lambda w, i: (0, 0))] * 2
    return (widths, rows // chunk), q_spec, k_spec, qpos_spec, kpos_spec, turn_specs


def attention_cost(q, keys, products):
    pairs = q.shape[0] * q.shape[1] * keys.shape[1]
    return pl.CostEstimate(
        flops=2 * products * pairs * HD,
        bytes_accessed=2 * q.size + 4 * keys.size,
        transcendentals=2 * pairs,
    )


def attend(qpos, kpos, q, k, v, tok_rows):
    grid, q_spec, k_spec, qpos_spec, kpos_spec, _ = attention_specs(q, k, tok_rows)
    return pl.pallas_call(
        attend_kernel,
        grid=grid,
        in_specs=[qpos_spec, kpos_spec, q_spec, k_spec, k_spec],
        out_specs=q_spec,
        out_shape=jax.ShapeDtypeStruct(q.shape, BF),
        compiler_params=pltpu.CompilerParams(vmem_limit_bytes=VMEM_LIMIT),
        cost_estimate=attention_cost(q, k, 2),
        name="attend",
    )(qpos, kpos, q, k, v)


def attend_back(qpos, kpos, turns, q, k, v, do, tok_rows):
    grid, q_spec, k_spec, qpos_spec, kpos_spec, turn_specs = attention_specs(q, k, tok_rows)
    return pl.pallas_call(
        attend_back_kernel,
        grid=grid,
        in_specs=[qpos_spec, kpos_spec, *turn_specs, q_spec, k_spec, k_spec, q_spec],
        out_specs=[q_spec, k_spec, k_spec],
        out_shape=[
            jax.ShapeDtypeStruct(q.shape, F32),
            jax.ShapeDtypeStruct(k.shape, F32),
            jax.ShapeDtypeStruct(k.shape, F32),
        ],
        compiler_params=pltpu.CompilerParams(vmem_limit_bytes=VMEM_LIMIT),
        cost_estimate=attention_cost(q, k, 5),
        name="attend_back",
    )(qpos, kpos, *turns, q, k, v, do)


def project_kernel(
    a_ref, w_hbm, scale_ref, cos_ref, sin_ref, raw_ref, q_ref, kv_ref, kept_hbm, held, sems, out_sems
):
    @pl.when(pl.program_id(0) == 0)
    def _():
        for w in range(SLOTS):
            load_codes(w, (w_hbm,), (held.at[w],), sems)

    copies = keep_copies((held,), (kept_hbm,), out_sems)
    start_on_first(copies)
    a = a_ref[...]
    cosine, sine = cos_ref[...], sin_ref[...]
    for w in range(SLOTS):
        raw = dot(a, held[w])
        raw_ref[w] = raw.astype(BF)
        lin = raw * scale_ref[...]
        q_ref[w] = (rotate(lin[:, :HD], cosine, sine) * HD ** (-0.5)).astype(BF)
        kv_ref[w] = lin[:, HD:]
    wait_on_last(copies)


def project(a, codes, scale, cosine, sine):
    rows, model = a.shape
    cols = codes.shape[1]
    chunk = min(rows, 256)
    turn = pl.BlockSpec((chunk, HALF), lambda i: (i, 0))

    def out(count):
        return pl.BlockSpec((SLOTS, chunk, count), lambda i: (0, i, 0))

    return pl.pallas_call(
        project_kernel,
        grid=(rows // chunk,),
        in_specs=[
            pl.BlockSpec((chunk, model), lambda i: (i, 0)),
            pl.BlockSpec(memory_space=pl.ANY),
            pl.BlockSpec((1, cols), lambda i: (0, 0)),
            turn,
            turn,
        ],
        out_specs=[out(cols), out(HD), out(cols - HD), pl.BlockSpec(memory_space=pl.ANY)],
        out_shape=[
            jax.ShapeDtypeStruct((SLOTS, rows, cols), BF),
            jax.ShapeDtypeStruct((SLOTS, rows, HD), BF),
            jax.ShapeDtypeStruct((SLOTS, rows, cols - HD), F32),
            jax.ShapeDtypeStruct((SLOTS, model, cols), BF),
        ],
        scratch_shapes=[
            pltpu.VMEM((SLOTS, model, cols), BF),
            pltpu.SemaphoreType.DMA((1,)),
            pltpu.SemaphoreType.DMA((1,)),
        ],
        compiler_params=pltpu.CompilerParams(vmem_limit_bytes=VMEM_LIMIT),
        cost_estimate=pl.CostEstimate(
            flops=2 * SLOTS * rows * model * cols,
            bytes_accessed=2 * rows * model + 2 * model * cols + 8 * SLOTS * rows * cols,
            transcendentals=0,
        ),
        name="project",
    )(a, codes, scale[None], cosine, sine)


def heads_kernel(core_ref, own_ref, other_ref, cos_ref, sin_ref, k_ref, v_ref):
    own, other = own_ref[0], other_ref[0]
    cols = own.shape[1] // 2
    first = core_ref[0, 0] == 0
    low = jnp.where(first, own, other)
    high = jnp.where(first, other, own)
    k = jnp.concatenate([low[:, :cols], high[:, :cols]], axis=1)
    k_ref[0] = rotate(k, cos_ref[...], sin_ref[...]).astype(BF)
    v_ref[0] = jnp.concatenate([low[:, cols:], high[:, cols:]], axis=1).astype(BF)


def whole_heads_of(core, own, other, cosine, sine):
    widths, rows, cols = own.shape
    part = rows // 2
    mine = pl.BlockSpec((1, part, cols), lambda w, c: (w, c, 0))
    turn = pl.BlockSpec((part, HALF), lambda w, c: (c, 0))
    return pl.pallas_call(
        heads_kernel,
        grid=(widths, 2),
        in_specs=[
            pl.BlockSpec(memory_space=pltpu.SMEM),
            mine,
            pl.BlockSpec((1, part, cols), lambda w, c: (w, 1 - c, 0)),
            turn,
            turn,
        ],
        out_specs=[mine, mine],
        out_shape=[jax.ShapeDtypeStruct(own.shape, BF)] * 2,
        compiler_params=pltpu.CompilerParams(vmem_limit_bytes=VMEM_LIMIT),
        cost_estimate=pl.CostEstimate(flops=8 * own.size, bytes_accessed=12 * own.size, transcendentals=0),
        name="heads",
    )(core.reshape(1, 1).astype(jnp.int32), own, other, cosine, sine)


def norm_scale(values):
    return lax.rsqrt(jnp.mean(values * values, axis=-1, keepdims=True) + EPSILON)


def norm_back(values, gain, grad):
    r = norm_scale(values)
    weighted = grad * gain
    unit = values * r
    back = r * (weighted - unit * jnp.mean(weighted * unit, axis=-1, keepdims=True))
    return back, jnp.sum(grad * unit, axis=0, keepdims=True)


def output_partial_kernel(width, o_ref, w_ref, low_ref, high_ref, held):
    @pl.when(pl.program_id(0) == 0)
    def _():
        held[...] = dequantized(w_ref[...], width)

    store_halves(low_ref, high_ref, dot(o_ref[0], held[...]).astype(BF))


def output_partial(width, attended, codes):
    rows = attended.shape[1]
    model = codes.shape[1]
    chunk = min(rows // 2, 256)
    specs, shapes = halves_specs(rows, model, chunk)
    return pl.pallas_call(
        functools.partial(output_partial_kernel, width),
        grid=(rows // chunk,),
        in_specs=[
            pl.BlockSpec((1, chunk, HD), lambda i: (width, i, 0)),
            pl.BlockSpec((HD, model), lambda i: (0, 0)),
        ],
        out_specs=specs,
        out_shape=shapes,
        scratch_shapes=[pltpu.VMEM((HD, model), BF)],
        compiler_params=pltpu.CompilerParams(vmem_limit_bytes=VMEM_LIMIT),
        cost_estimate=pl.CostEstimate(
            flops=2 * rows * HD * model, bytes_accessed=2 * rows * model, transcendentals=0
        ),
        name="output_partial",
    )(attended, codes)


def output_norm_kernel(
    part_ref, from_x_ref, from_y_ref, x_ref, scale_ref, post_ref, pre_ref, raw_ref, middle_ref, two_ref
):
    raw = part_ref[...].astype(F32) + from_x_ref[...].astype(F32) + from_y_ref[...].astype(F32)
    raw_ref[...] = raw
    lin = raw * scale_ref[...]
    middle = x_ref[...].astype(F32) + lin * norm_scale(lin) * post_ref[...]
    middle_ref[...] = middle
    two_ref[...] = (middle * norm_scale(middle) * pre_ref[...]).astype(BF)


def output_norm(parts, x, scale, post_gain, pre_gain):
    rows, model = x.shape
    whole = pl.BlockSpec(memory_space=pltpu.VMEM)
    return pl.pallas_call(
        output_norm_kernel,
        in_specs=[whole] * 7,
        out_specs=[whole] * 3,
        out_shape=[
            jax.ShapeDtypeStruct((rows, model), F32),
            jax.ShapeDtypeStruct((rows, model), F32),
            jax.ShapeDtypeStruct((rows, model), BF),
        ],
        compiler_params=pltpu.CompilerParams(vmem_limit_bytes=VMEM_LIMIT),
        cost_estimate=pl.CostEstimate(flops=20 * rows * model, bytes_accessed=18 * rows * model, transcendentals=0),
        name="output_norm",
    )(*parts, x, scale[None], post_gain[None], pre_gain[None])


def loss_kernel(
    live_ref,
    part_ref,
    from_x_ref,
    from_y_ref,
    middle_ref,
    cot_ref,
    scale_ref,
    gain_ref,
    mixed_ref,
    round_ref,
    gain_sum_ref,
    scale_sum_ref,
):
    live = live_ref[0, 0]
    raw = part_ref[...].astype(F32) + from_x_ref[...].astype(F32) + from_y_ref[...].astype(F32)
    scale, gain = scale_ref[...], gain_ref[...]
    lin = raw * scale
    mixed_ref[...] = ((middle_ref[...] + lin * norm_scale(lin) * gain) * live).astype(BF)
    back, gain_sum_ref[...] = norm_back(lin, gain, cot_ref[...].astype(F32) * live)
    round_ref[...] = (back * scale).astype(BF)
    scale_sum_ref[...] = jnp.sum(raw * back, axis=0, keepdims=True)


def loss_step(live, parts, middle, cot, scale, gain):
    rows, model = middle.shape
    whole = pl.BlockSpec(memory_space=pltpu.VMEM)
    return pl.pallas_call(
        loss_kernel,
        in_specs=[pl.BlockSpec(memory_space=pltpu.SMEM)] + [whole] * 7,
        out_specs=[whole] * 4,
        out_shape=[
            jax.ShapeDtypeStruct((rows, model), BF),
            jax.ShapeDtypeStruct((rows, model), BF),
            jax.ShapeDtypeStruct((1, model), F32),
            jax.ShapeDtypeStruct((1, model), F32),
        ],
        compiler_params=pltpu.CompilerParams(vmem_limit_bytes=VMEM_LIMIT),
        cost_estimate=pl.CostEstimate(flops=20 * rows * model, bytes_accessed=16 * rows * model, transcendentals=0),
        name="loss_step",
    )(live, *parts, middle, cot, scale[None], gain[None])


def output_back_kernel(
    live_ref,
    part_ref,
    from_x_ref,
    from_y_ref,
    middle_ref,
    raw_ref,
    cot_ref,
    scale_ref,
    post_ref,
    pre_ref,
    middle_grad_ref,
    round_ref,
    pre_sum_ref,
    post_sum_ref,
    scale_sum_ref,
):
    two_grad = part_ref[...].astype(F32) + from_x_ref[...].astype(F32) + from_y_ref[...].astype(F32)
    back, pre_sum_ref[...] = norm_back(middle_ref[...], pre_ref[...], two_grad)
    middle_grad = cot_ref[...].astype(F32) * live_ref[0, 0] + back
    middle_grad_ref[...] = middle_grad
    raw, scale = raw_ref[...], scale_ref[...]
    lin_grad, post_sum_ref[...] = norm_back(raw * scale, post_ref[...], middle_grad)
    scale_sum_ref[...] = jnp.sum(raw * lin_grad, axis=0, keepdims=True)
    round_ref[...] = (lin_grad * scale).astype(BF)


def output_back(live, parts, middle, raw, cot, scale, post_gain, pre_gain):
    rows, model = middle.shape
    whole = pl.BlockSpec(memory_space=pltpu.VMEM)
    return pl.pallas_call(
        output_back_kernel,
        in_specs=[pl.BlockSpec(memory_space=pltpu.SMEM)] + [whole] * 9,
        out_specs=[whole] * 5,
        out_shape=[
            jax.ShapeDtypeStruct((rows, model), F32),
            jax.ShapeDtypeStruct((rows, model), BF),
            jax.ShapeDtypeStruct((1, model), F32),
            jax.ShapeDtypeStruct((1, model), F32),
            jax.ShapeDtypeStruct((1, model), F32),
        ],
        compiler_params=pltpu.CompilerParams(vmem_limit_bytes=VMEM_LIMIT),
        cost_estimate=pl.CostEstimate(flops=40 * rows * model, bytes_accessed=24 * rows * model, transcendentals=0),
        name="output_back",
    )(live, *parts, middle, raw, cot, scale[None], post_gain[None], pre_gain[None])


def head_back_kernel(width, count, *refs):
    pieces = refs[:count]
    w_ref, do_ref, joined, rows_held, w_held, piece_sems, out_sems = refs[count:]
    gathered = piece_copies(pieces, rows_held, piece_sems)
    start_on_first(gathered)

    @pl.when(pl.program_id(0) == 0)
    def _():
        w_held[...] = dequantized(w_ref[...], width)
        for copy in gathered:
            copy.wait()

    copies = keep_copies((rows_held,), (joined,), out_sems)
    start_on_first(copies)
    chunk = do_ref.shape[0]
    part = rows_held[pl.ds(pl.multiple_of(pl.program_id(0) * chunk, chunk), chunk)]
    do_ref[...] = dot_nt(part, w_held[...]).astype(BF)
    wait_on_last(copies)


def head_back(width, pieces, codes):
    rows = sum(piece.shape[0] for piece in pieces)
    model = codes.shape[1]
    chunk = min(rows, 256)
    whole = pl.BlockSpec(memory_space=pl.ANY)
    return pl.pallas_call(
        functools.partial(head_back_kernel, width, len(pieces)),
        grid=(rows // chunk,),
        in_specs=[whole] * len(pieces) + [pl.BlockSpec((HD, model), lambda i: (0, 0))],
        out_specs=[pl.BlockSpec((chunk, HD), lambda i: (i, 0)), whole],
        out_shape=[
            jax.ShapeDtypeStruct((rows, HD), BF),
            jax.ShapeDtypeStruct((rows, model), BF),
        ],
        scratch_shapes=[
            pltpu.VMEM((rows, model), BF),
            pltpu.VMEM((HD, model), BF),
            pltpu.SemaphoreType.DMA((len(pieces),)),
            pltpu.SemaphoreType.DMA((1,)),
        ],
        compiler_params=pltpu.CompilerParams(vmem_limit_bytes=VMEM_LIMIT),
        cost_estimate=pl.CostEstimate(
            flops=2 * rows * HD * model, bytes_accessed=4 * rows * model, transcendentals=0
        ),
        name="head_back",
    )(*pieces, codes)


def join_kernel(starts, *refs):
    result = refs[-1]
    step = pl.program_id(0)
    for piece, start in zip(refs[:-1], starts):

        @pl.when(step == start // result.shape[0])
        def _(piece=piece, start=start):
            result[pl.ds(start % result.shape[0], piece.shape[0])] = piece[...]


def join(*pieces):
    starts = [0]
    for piece in pieces:
        starts.append(starts[-1] + piece.shape[0])
    total, cols = starts[-1], pieces[0].shape[1]
    rows = pieces[0].shape[0]
    return pl.pallas_call(
        functools.partial(join_kernel, tuple(starts[:-1])),
        grid=(total // rows,),
        in_specs=[pl.BlockSpec(piece.shape, lambda i: (0, 0)) for piece in pieces],
        out_specs=pl.BlockSpec((rows, cols), lambda i: (i, 0)),
        out_shape=jax.ShapeDtypeStruct((total, cols), pieces[0].dtype),
        compiler_params=pltpu.CompilerParams(vmem_limit_bytes=VMEM_LIMIT),
        cost_estimate=pl.CostEstimate(flops=0, bytes_accessed=4 * total * cols, transcendentals=0),
        name="join",
    )(*pieces)


GELU_A = 0.7978845608028654
GELU_B = 0.044715


def load_codes(width, codes, held, sems):
    copies = [
        pltpu.make_async_copy(source, target, sems.at[i])
        for i, (source, target) in enumerate(zip(codes, held))
    ]
    for copy in copies:
        copy.start()
    for copy, target in zip(copies, held):
        copy.wait()
        rows = target.shape[0]
        step = 128 if rows % 128 == 0 else 16

        def turn(i, carry, target=target, step=step):
            part = pl.ds(pl.multiple_of(i * step, step), step)
            target[part] = dequantized(target[part], width)
            return carry

        lax.fori_loop(0, rows // step, turn, 0)


def halves_specs(rows, model, chunk):
    steps = rows // chunk // 2
    low = pl.BlockSpec((chunk, model), lambda i: (jnp.minimum(i, steps - 1), 0))
    high = pl.BlockSpec((chunk, model), lambda i: (jnp.maximum(i - steps, 0), 0))
    return [low, high], [jax.ShapeDtypeStruct((rows // 2, model), BF)] * 2


def store_halves(low_ref, high_ref, value):
    step, steps = pl.program_id(0), pl.num_programs(0)

    @pl.when(step < steps // 2)
    def _():
        low_ref[...] = value

    @pl.when(step >= steps // 2)
    def _():
        high_ref[...] = value


def keep_copies(held, kept, sems):
    return [
        pltpu.make_async_copy(source, target, sems.at[i])
        for i, (source, target) in enumerate(zip(held, kept))
    ]


def start_on_first(copies):
    @pl.when(pl.program_id(0) == 0)
    def _():
        for copy in copies:
            copy.start()


def wait_on_last(copies):
    @pl.when(pl.program_id(0) == pl.num_programs(0) - 1)
    def _():
        for copy in copies:
            copy.wait()


def piece_copies(pieces, held, sems):
    copies = []
    at = 0
    for i, piece in enumerate(pieces):
        rows = piece.shape[0]
        copies.append(pltpu.make_async_copy(piece, held.at[pl.ds(at, rows)], sems.at[i]))
        at += rows
    return copies


def ffn_in_kernel(width, count, *refs):
    pieces = refs[:count]
    (
        g_hbm,
        u_hbm,
        gs_ref,
        us_ref,
        gate_ref,
        up_ref,
        hidden_ref,
        a_hbm,
        gw_hbm,
        uw_hbm,
        a_held,
        g_held,
        u_held,
        piece_sems,
        sems,
        out_sems,
    ) = refs[count:]
    gathered = piece_copies(pieces, a_held, piece_sems)
    start_on_first(gathered)

    @pl.when(pl.program_id(0) == 0)
    def _():
        load_codes(width, (g_hbm, u_hbm), (g_held, u_held), sems)
        for copy in gathered:
            copy.wait()

    copies = keep_copies((a_held, g_held, u_held), (a_hbm, gw_hbm, uw_hbm), out_sems)
    start_on_first(copies)
    chunk = gate_ref.shape[0]
    a = a_held[pl.ds(pl.multiple_of(pl.program_id(0) * chunk, chunk), chunk)]
    gate = dot(a, g_held[...])
    up = dot(a, u_held[...])
    gate_ref[...] = gate.astype(BF)
    up_ref[...] = up.astype(BF)
    gate = gate * gs_ref[...]
    inner = jnp.tanh(GELU_A * (gate + GELU_B * gate * gate * gate))
    hidden_ref[...] = (0.5 * gate * (1.0 + inner) * (up * us_ref[...])).astype(BF)
    wait_on_last(copies)


def ffn_in(width, pieces, gate_codes, up_codes, g_scale, u_scale):
    rows = sum(piece.shape[0] for piece in pieces)
    model, features = gate_codes.shape
    chunk = min(rows, 256)
    whole = pl.BlockSpec(memory_space=pl.ANY)
    vector = pl.BlockSpec((1, features), lambda i: (0, 0))
    block = pl.BlockSpec((chunk, features), lambda i: (i, 0))
    return pl.pallas_call(
        functools.partial(ffn_in_kernel, width, len(pieces)),
        grid=(rows // chunk,),
        in_specs=[whole] * len(pieces) + [whole, whole, vector, vector],
        out_specs=[block] * 3 + [whole] * 3,
        out_shape=[jax.ShapeDtypeStruct((rows, features), BF)] * 3
        + [jax.ShapeDtypeStruct((rows, model), BF)]
        + [jax.ShapeDtypeStruct((model, features), BF)] * 2,
        scratch_shapes=[
            pltpu.VMEM((rows, model), BF),
            pltpu.VMEM((model, features), BF),
            pltpu.VMEM((model, features), BF),
            pltpu.SemaphoreType.DMA((len(pieces),)),
            pltpu.SemaphoreType.DMA((2,)),
            pltpu.SemaphoreType.DMA((3,)),
        ],
        compiler_params=pltpu.CompilerParams(vmem_limit_bytes=VMEM_LIMIT),
        cost_estimate=pl.CostEstimate(
            flops=4 * rows * model * features,
            bytes_accessed=2 * (rows * model + 2 * model * features + 3 * rows * features),
            transcendentals=rows * features,
        ),
        name="ffn_in",
    )(*pieces, gate_codes, up_codes, g_scale[None], u_scale[None])


def down_grad_kernel(counts, *refs):
    pieces, refs = refs[: sum(counts)], refs[sum(counts) :]
    widths = len(counts)
    h_refs, scale_ref, out_ref = refs[:widths], refs[widths], refs[widths + 1]
    joined, held = refs[widths + 2 : 2 * widths + 2], refs[2 * widths + 2]
    piece_sems, out_sems = refs[2 * widths + 3 :]
    groups = []
    at = 0
    for w, count in enumerate(counts):
        groups.append(piece_copies(pieces[at : at + count], held.at[w], piece_sems.at[w]))
        at += count
    for group in groups:
        start_on_first(group)
    copies = keep_copies([held.at[w] for w in range(widths)], joined, out_sems)
    first = pl.program_id(0) == 0
    product = None
    for w in range(widths):

        @pl.when(first)
        def _(w=w):
            for copy in groups[w]:
                copy.wait()
            copies[w].start()

        part = dot_tn(h_refs[w][...], held[w])
        product = part if product is None else product + part
    out_ref[...] = (product / scale_ref[...]).astype(BF)
    wait_on_last(copies)


def down_gradient(hiddens, piece_lists, scale):
    rows, features = hiddens[0].shape
    model = scale.shape[0]
    widths = len(hiddens)
    counts = tuple(len(pieces) for pieces in piece_lists)
    chunk = 128 if features % 128 == 0 else features
    whole = pl.BlockSpec(memory_space=pl.ANY)
    return pl.pallas_call(
        functools.partial(down_grad_kernel, counts),
        grid=(features // chunk,),
        in_specs=[whole] * sum(counts)
        + [pl.BlockSpec((rows, chunk), lambda i: (0, i))] * widths
        + [pl.BlockSpec((1, model), lambda i: (0, 0))],
        out_specs=[pl.BlockSpec((chunk, model), lambda i: (i, 0))] + [whole] * widths,
        out_shape=[jax.ShapeDtypeStruct((features, model), BF)]
        + [jax.ShapeDtypeStruct((rows, model), BF)] * widths,
        scratch_shapes=[
            pltpu.VMEM((widths, rows, model), BF),
            pltpu.SemaphoreType.DMA((widths, max(counts))),
            pltpu.SemaphoreType.DMA((widths,)),
        ],
        compiler_params=pltpu.CompilerParams(vmem_limit_bytes=VMEM_LIMIT),
        cost_estimate=pl.CostEstimate(
            flops=2 * widths * rows * model * features,
            bytes_accessed=2 * (2 * widths * rows * model + features * (model + widths * rows)),
            transcendentals=0,
        ),
        name="down_grad",
    )(*[piece for pieces in piece_lists for piece in pieces], *hiddens, scale[None])


def ffn_out_kernel(width, h_ref, d_hbm, low_ref, high_ref, dw_hbm, d_held, sems, out_sems):
    @pl.when(pl.program_id(0) == 0)
    def _():
        load_codes(width, (d_hbm,), (d_held,), sems)

    copies = keep_copies((d_held,), (dw_hbm,), out_sems)
    start_on_first(copies)
    store_halves(low_ref, high_ref, dot(h_ref[...], d_held[...]).astype(BF))
    wait_on_last(copies)


def ffn_out(width, hidden, down_codes):
    rows, features = hidden.shape
    model = down_codes.shape[1]
    chunk = min(rows // 2, 256)
    whole = pl.BlockSpec(memory_space=pl.ANY)
    specs, shapes = halves_specs(rows, model, chunk)
    return pl.pallas_call(
        functools.partial(ffn_out_kernel, width),
        grid=(rows // chunk,),
        in_specs=[pl.BlockSpec((chunk, features), lambda i: (i, 0)), whole],
        out_specs=specs + [whole],
        out_shape=shapes + [jax.ShapeDtypeStruct((features, model), BF)],
        scratch_shapes=[
            pltpu.VMEM((features, model), BF),
            pltpu.SemaphoreType.DMA((1,)),
            pltpu.SemaphoreType.DMA((1,)),
        ],
        compiler_params=pltpu.CompilerParams(vmem_limit_bytes=VMEM_LIMIT),
        cost_estimate=pl.CostEstimate(
            flops=2 * rows * model * features,
            bytes_accessed=2 * (rows * model + 2 * model * features + rows * features),
            transcendentals=0,
        ),
        name="ffn_out",
    )(hidden, down_codes)


def ffn_back_kernel(
    dr_ref,
    gate_ref,
    up_ref,
    d_hbm,
    g_hbm,
    u_hbm,
    gs_ref,
    us_ref,
    after_hbm,
    low_ref,
    high_ref,
    gr_ref,
    ur_ref,
    gsum_ref,
    usum_ref,
    d_held,
    g_held,
    u_held,
    sems,
):
    del after_hbm
    first = pl.program_id(0) == 0
    copies = keep_copies((d_hbm, g_hbm, u_hbm), (d_held, g_held, u_held), sems)
    start_on_first(copies)

    @pl.when(first)
    def _():
        gsum_ref[...] = jnp.zeros_like(gsum_ref)
        usum_ref[...] = jnp.zeros_like(usum_ref)
        copies[0].wait()

    hidden_grad = dot_nt(dr_ref[...], d_held[...])
    gate_raw = gate_ref[...].astype(F32)
    up_raw = up_ref[...].astype(F32)
    gate = gate_raw * gs_ref[...]
    up = up_raw * us_ref[...]
    square = gate * gate
    inner = jnp.tanh(GELU_A * (gate + GELU_B * gate * square))
    half_sum = 0.5 * (1.0 + inner)
    slope = half_sum + 0.5 * gate * (1.0 - inner * inner) * (
        GELU_A * (1.0 + 3.0 * GELU_B * square)
    )
    gate_grad = hidden_grad * up * slope
    up_grad = hidden_grad * (gate * half_sum)
    gsum_ref[...] += jnp.sum(gate_raw * gate_grad, axis=0, keepdims=True)
    usum_ref[...] += jnp.sum(up_raw * up_grad, axis=0, keepdims=True)
    gate_round = (gate_grad * gs_ref[...]).astype(BF)
    up_round = (up_grad * us_ref[...]).astype(BF)
    gr_ref[...] = gate_round
    ur_ref[...] = up_round

    @pl.when(first)
    def _():
        copies[1].wait()
        copies[2].wait()

    store_halves(
        low_ref,
        high_ref,
        (dot_nt(gate_round, g_held[...]) + dot_nt(up_round, u_held[...])).astype(BF),
    )


def ffn_back(down_round, gate_raw, up_raw, down_w, gate_w, up_w, g_scale, u_scale, after):
    rows, model = down_round.shape
    features = gate_w.shape[1]
    chunk = min(rows // 2, 256)
    whole = pl.BlockSpec(memory_space=pl.ANY)
    vector = pl.BlockSpec((1, features), lambda i: (0, 0))
    block = pl.BlockSpec((chunk, features), lambda i: (i, 0))
    wide = pl.BlockSpec((chunk, model), lambda i: (i, 0))
    specs, shapes = halves_specs(rows, model, chunk)
    return pl.pallas_call(
        ffn_back_kernel,
        grid=(rows // chunk,),
        in_specs=[wide, block, block, whole, whole, whole, vector, vector, whole],
        out_specs=specs + [block, block, vector, vector],
        out_shape=shapes
        + [
            jax.ShapeDtypeStruct((rows, features), BF),
            jax.ShapeDtypeStruct((rows, features), BF),
            jax.ShapeDtypeStruct((1, features), F32),
            jax.ShapeDtypeStruct((1, features), F32),
        ],
        scratch_shapes=[
            pltpu.VMEM((features, model), BF),
            pltpu.VMEM((model, features), BF),
            pltpu.VMEM((model, features), BF),
            pltpu.SemaphoreType.DMA((3,)),
        ],
        compiler_params=pltpu.CompilerParams(vmem_limit_bytes=VMEM_LIMIT),
        cost_estimate=pl.CostEstimate(
            flops=6 * rows * model * features,
            bytes_accessed=2 * (2 * rows * model + 3 * model * features + 4 * rows * features),
            transcendentals=rows * features,
        ),
        name="ffn_back",
    )(down_round, gate_raw, up_raw, down_w, gate_w, up_w, g_scale[None], u_scale[None], after)


def project_back_kernel(round_ref, w_hbm, low_ref, high_ref, held, sems):
    copies = keep_copies((w_hbm,), (held,), sems)
    start_on_first(copies)

    @pl.when(pl.program_id(0) == 0)
    def _():
        copies[0].wait()

    product = dot_nt(round_ref[0], held[0])
    for w in range(1, SLOTS):
        product = product + dot_nt(round_ref[w], held[w])
    store_halves(low_ref, high_ref, product.astype(BF))


def project_back(rounded, weights):
    _, rows, cols = rounded.shape
    model = weights.shape[1]
    chunk = min(rows // 2, 256)
    specs, shapes = halves_specs(rows, model, chunk)
    return pl.pallas_call(
        project_back_kernel,
        grid=(rows // chunk,),
        in_specs=[
            pl.BlockSpec((SLOTS, chunk, cols), lambda i: (0, i, 0)),
            pl.BlockSpec(memory_space=pl.ANY),
        ],
        out_specs=specs,
        out_shape=shapes,
        scratch_shapes=[pltpu.VMEM((SLOTS, model, cols), BF), pltpu.SemaphoreType.DMA((1,))],
        compiler_params=pltpu.CompilerParams(vmem_limit_bytes=VMEM_LIMIT),
        cost_estimate=pl.CostEstimate(
            flops=2 * SLOTS * rows * model * cols,
            bytes_accessed=2 * (rows * model + SLOTS * cols * (model + rows)),
            transcendentals=0,
        ),
        name="project_back",
    )(rounded, weights)


def shards(
    tokens,
    query_codes,
    key_codes,
    value_codes,
    output_codes,
    gate_codes,
    up_codes,
    down_codes,
    query_scale,
    key_scale,
    value_scale,
    output_scale,
    gate_scale,
    up_scale,
    down_scale,
    pre_attn_gain,
    post_attn_gain,
    pre_ffw_gain,
    post_ffw_gain,
    slot_width,
    slot_live,
    cotangent,
):
    planes = lax.axis_size("dp")
    width = lax.axis_size("fsdp")
    devices = planes * width
    group_count = width // 8
    rank = lax.axis_index("fsdp")
    me = lax.axis_index("dp") * width + rank
    t_index, group = rank % 8, rank // 8
    core = rank % 2
    CORE, X, Y = 1, 2, 4
    groups = None
    if group_count > 1:
        groups = [[g * 8 + j for j in range(8)] for g in range(group_count)]
        across = [[g * 8 + j for g in range(group_count)] for j in range(8)]

    def swap(values, mask):
        return lax.ppermute(values, "fsdp", [(i, i ^ mask) for i in range(width)])

    def swap_all(values, mask):
        return lax.ppermute(values, ALL, [(i, i ^ mask) for i in range(devices)])

    tok_rows, model = tokens.shape
    group_rows = 8 * tok_rows
    d_rows = query_codes.shape[0]
    o_rows = output_codes.shape[0]
    ff_rows = down_codes.shape[0]
    q_cols = query_codes.shape[1] // 8
    k_cols = key_codes.shape[1] // 8
    ff_cols = ff_rows * planes * group_count
    widths = range(SLOTS)

    def tp_pieces(block):
        from_x = swap(block, X)
        from_y = swap(block, Y)
        cut = block.shape[0] // 2
        first = swap(from_y[:cut], X)
        second = swap(from_x[cut:], Y)
        same = [block, from_x, from_y, first, second]
        return same + [swap(piece, CORE) for piece in same]

    def tp_gather(block):
        return join(*tp_pieces(block))

    def after(values, *others):
        return lax.optimization_barrier((values, *others))[0]

    def core_sum(low, high):
        return (low.astype(F32) + swap(high, CORE).astype(F32)).astype(BF)

    def tp_scatter(low, high):
        return plane_sum(core_sum(low, high))

    def plane_sum(pair):
        rows = pair.shape[0] // 4
        cut = rows // 2
        pair = pair.reshape(2, 2, rows, model)
        got_x = swap(pair[1, 1, :cut], X)
        got_y = swap(pair[1, 1, cut:], Y)
        for_x = jnp.concatenate(
            [pair[0, 1, :cut], (pair[0, 1, cut:].astype(F32) + got_y.astype(F32)).astype(BF)]
        )
        for_y = jnp.concatenate(
            [(pair[1, 0, :cut].astype(F32) + got_x.astype(F32)).astype(BF), pair[1, 0, cut:]]
        )
        return pair[0, 0], swap(for_x, X), swap(for_y, Y)

    def total(parts):
        return sum(part.astype(F32) for part in parts)

    def tp_columns(blocks):
        return lax.all_to_all(blocks, "fsdp", 0, 0, tiled=True, axis_index_groups=groups)

    def gather_rows(rows):
        if group_count > 1:
            rows = lax.all_gather(rows, "fsdp", axis=0, tiled=True, axis_index_groups=across)
        return lax.all_gather(rows, "dp", axis=0, tiled=True)

    def scatter_rows(grad):
        rows = lax.psum_scatter(grad, "dp", scatter_dimension=0, tiled=True)
        if group_count > 1:
            rows = lax.psum_scatter(
                rows, "fsdp", scatter_dimension=0, tiled=True, axis_index_groups=across
            )
        return rows

    small = jnp.concatenate(
        [query_scale, key_scale, value_scale, output_scale, gate_scale, up_scale, down_scale]
    )
    all_small = small[None]
    for bit in range(devices.bit_length() - 1):
        all_small = jnp.concatenate([all_small, swap_all(all_small, 1 << bit)], axis=0)
    order = jnp.arange(devices, dtype=jnp.int32) ^ me
    all_small = all_small[order]
    cuts = []
    at = 0
    for vector in (
        query_scale,
        key_scale,
        value_scale,
        output_scale,
        gate_scale,
        up_scale,
        down_scale,
    ):
        cuts.append(all_small[:, at : at + vector.shape[0]].reshape(-1))
        at += vector.shape[0]
    q_scale_all, k_scale_all, v_scale_all, o_scale_all, g_scale_all, u_scale_all, d_scale_all = cuts

    def own_ff(vector):
        cut = vector.reshape(planes * group_count, 8, ff_rows)
        return lax.dynamic_index_in_dim(cut, t_index, 1, keepdims=False).reshape(ff_cols)

    qkv_scale = jnp.concatenate(
        [
            lax.dynamic_slice_in_dim(q_scale_all, t_index * q_cols, q_cols),
            lax.dynamic_slice_in_dim(k_scale_all, t_index * k_cols, k_cols),
            lax.dynamic_slice_in_dim(v_scale_all, t_index * k_cols, k_cols),
        ]
    )
    g_scale = own_ff(g_scale_all)
    u_scale = own_ff(u_scale_all)

    def by_head(codes):
        return codes.reshape(codes.shape[0], 8, -1).transpose(1, 0, 2)

    def by_head_back(blocks):
        return blocks.transpose(1, 0, 2).reshape(blocks.shape[1], -1)

    def by_ff(codes):
        cut = codes.reshape(d_rows, planes * group_count, 8, ff_rows)
        return cut.transpose(2, 0, 1, 3).reshape(8, d_rows, ff_cols)

    def by_ff_back(blocks):
        cut = blocks.reshape(8, d_rows, planes * group_count, ff_rows)
        return cut.transpose(1, 2, 0, 3).reshape(d_rows, 8 * ff_cols)

    def merged(blocks):
        return blocks.reshape(8 * d_rows, blocks.shape[2])

    qkv_blocks = jnp.concatenate(
        [by_head(query_codes), by_head(key_codes), by_head(value_codes)], axis=2
    )
    inputs = tokens.astype(F32)
    qkv_mine = merged(tp_columns(qkv_blocks))
    qkv_codes = gather_rows(qkv_mine)
    gate_mine = merged(tp_columns(by_ff(after(gate_codes, qkv_mine))))
    up_mine = merged(tp_columns(by_ff(after(up_codes, gate_mine))))
    gate_codes_t = gather_rows(gate_mine)
    normed_own, up_mine = lax.optimization_barrier(
        (rms_norm(inputs, pre_attn_gain).astype(BF), up_mine)
    )
    normed = after(tp_gather(normed_own), qkv_scale)

    whole_heads = group_count == 1 and 8 % planes == 0
    heads_per_plane = max(1, 8 // planes)

    def turn(step):
        pairs = []
        for source in range(8):
            plane = (source + step) % planes
            pairs.append((source, plane * heads_per_plane + source // planes))
        return pairs

    def pieces_to_heads(pieces):
        result = jnp.zeros_like(pieces)
        for step in range(planes):
            piece = lax.dynamic_index_in_dim(pieces, (rank + step) % planes, 0, keepdims=False)
            moved = lax.ppermute(piece, "fsdp", turn(step))
            place = (rank // heads_per_plane - step) % planes
            result = lax.dynamic_update_index_in_dim(result, moved, place, 0)
        return result

    def heads_to_pieces(pieces):
        result = jnp.zeros_like(pieces)
        for step in range(planes):
            place = (rank // heads_per_plane - step) % planes
            piece = lax.dynamic_index_in_dim(pieces, place, 0, keepdims=False)
            moved = lax.ppermute(piece, "fsdp", [(b, a) for a, b in turn(step)])
            result = lax.dynamic_update_index_in_dim(result, moved, (rank + step) % planes, 0)
        return result

    output_pieces = gather_rows(output_codes)

    blocks_at = jnp.stack([t_index ^ (c + 2 * x + 4 * y) for c in (0, 1) for y in (0, 1) for x in (0, 1)])
    positions = ((group * 8 + blocks_at) * tok_rows)[:, None] + jnp.arange(tok_rows, dtype=jnp.int32)
    positions = positions.reshape(group_rows)
    far = jnp.int32(1 << 30)
    key_positions = []
    for back in range(group_count):
        earlier = positions - back * group_rows
        key_positions.append(jnp.where(earlier >= 0, earlier, far))
    kpos = jnp.concatenate(key_positions)[None, :]
    qpos = positions[:, None]
    inv_rates = 10000.0 ** (-jnp.arange(HALF, dtype=F32) / HALF)
    angles = positions.astype(F32)[:, None] * inv_rates[None, :]
    cosine, sine = jnp.cos(angles), jnp.sin(angles)
    key_angles = jnp.concatenate(
        [(positions - back * group_rows).astype(F32) for back in range(group_count)]
    )[:, None] * inv_rates[None, :]

    qkv_raw, q, kv_own, qkv_w = project(normed, qkv_codes, qkv_scale, cosine, sine)
    k_near, v_near = whole_heads_of(core, kv_own, swap(kv_own, CORE), cosine, sine)

    if whole_heads:
        head_codes = pieces_to_heads(output_pieces.reshape(planes, o_rows, model)).reshape(HD, model)
    else:
        every = lax.all_gather(output_codes, ALL, axis=0, tiled=True)
        head_codes = lax.dynamic_slice_in_dim(every, t_index * HD, HD, 0)

    def turned(values):
        middle_row = group_rows // 2
        return jnp.concatenate([values[..., middle_row:, :], values[..., :middle_row, :]], axis=-2)

    def back_pairs(back):
        return [(i, i + 8 * back) for i in range(width) if i + 8 * back < width]

    k_parts, v_parts = [k_near], [v_near]
    for back in range(1, group_count):
        k_parts.append(lax.ppermute(k_near, "fsdp", back_pairs(back)))
        v_parts.append(lax.ppermute(v_near, "fsdp", back_pairs(back)))
    k_all = jnp.concatenate(k_parts, axis=1)
    v_all = jnp.concatenate(v_parts, axis=1)
    attended = attend(qpos, kpos, q, k_all, v_all, tok_rows)

    up_codes_t = gather_rows(up_mine)
    down_codes_t = gather_rows(down_codes)

    slot_of, live_of, cot_of = [], [], []
    for w in widths:
        slot = jnp.int32(0)
        for s in range(SLOTS):
            slot = jnp.where(slot_width[0, s] == w, s, slot)
        slot_of.append(slot)
        live = lax.dynamic_index_in_dim(slot_live[0], slot, 0, keepdims=False)
        live_of.append(live.astype(F32).reshape(1, 1))
        cot_of.append(lax.dynamic_index_in_dim(cotangent, slot, 0, keepdims=False))
    kept = [dict() for w in widths]
    for w in widths:
        k = kept[w]
        blocks = attended if w == 0 else after(attended, kept[w - 1]["low"])
        k["low"], high = output_partial(w, blocks, head_codes)
        k["out_raw"], k["middle"], two = output_norm(
            tp_scatter(k["low"], high), tokens, o_scale_all, post_attn_gain, pre_ffw_gain
        )
        k["two_pieces"] = tp_pieces(two)
    for w in widths:
        k = kept[w]
        (
            k["gate_raw"],
            k["up_raw"],
            k["hidden"],
            k["normed_two"],
            k["gate_w"],
            k["up_w"],
        ) = ffn_in(w, k["two_pieces"], gate_codes_t, up_codes_t, g_scale, u_scale)

    hiddens = lax.optimization_barrier(tuple(kept[w]["hidden"] for w in widths))
    for w in widths:
        k = kept[w]
        k["hidden"] = hiddens[w] if w == 0 else after(hiddens[w], kept[w - 1]["down_w"])
        if w == 2:
            k["hidden"], kept[0]["pair"] = lax.optimization_barrier((k["hidden"], kept[0]["pair"]))
        low, high, k["down_w"] = ffn_out(w, k["hidden"], down_codes_t)
        k["pair"] = core_sum(low, high)
    for w in widths:
        kept[w]["down_parts"] = plane_sum(kept[w]["pair"])

    mixed = jnp.zeros((SLOTS, tok_rows, model), BF)
    for w in widths:
        k = kept[w]
        cot = cot_of[w] if w == 0 else after(cot_of[w], kept[w - 1]["gain_four"])
        result, rounded, k["gain_four"], k["down_scale_sum"] = loss_step(
            live_of[w], k["down_parts"], k["middle"], cot, d_scale_all, post_ffw_gain
        )
        mixed = lax.dynamic_update_index_in_dim(mixed, result, slot_of[w], 0)
        k["down_pieces"] = tp_pieces(rounded)
    down_total, *down_rounds = down_gradient(
        [kept[w]["hidden"] for w in widths], [kept[w]["down_pieces"] for w in widths], d_scale_all
    )
    down_sum = scatter_rows(down_total)
    for w in widths:
        k = kept[w]
        low, high, k["gate_round"], k["up_round"], k["gate_sum"], k["up_sum"] = ffn_back(
            down_rounds[w],
            k["gate_raw"],
            k["up_raw"],
            k["down_w"],
            k["gate_w"],
            k["up_w"],
            g_scale,
            u_scale,
            down_total if w == 0 else kept[w - 1]["gate_sum"],
        )
        k["two_parts"] = tp_scatter(low, high)
    normed_two_rows = jnp.concatenate([kept[w]["normed_two"] for w in widths], axis=0)
    gate_rounds = [kept[w]["gate_round"] for w in widths]
    *gate_rounds, down_sum = lax.optimization_barrier((*gate_rounds, down_sum))
    gate_total = dot_tn(normed_two_rows, jnp.concatenate(gate_rounds, axis=0))
    gate_sum = scatter_rows((gate_total / g_scale).astype(BF))
    for w in widths:
        k = kept[w]
        cot = cot_of[w] if w == 0 else after(cot_of[w], kept[w - 1]["gain_two"])
        k["middle_grad"], rounded, k["gain_three"], k["gain_two"], k["out_scale_sum"] = output_back(
            live_of[w],
            k["two_parts"],
            k["middle"],
            k["out_raw"],
            cot,
            o_scale_all,
            post_attn_gain,
            pre_ffw_gain,
        )
        k["out_pieces"] = tp_pieces(rounded)
    up_rounds = [kept[w]["up_round"] for w in widths]
    *up_rounds, _ = lax.optimization_barrier((*up_rounds, kept[2]["gain_two"]))
    up_total = dot_tn(normed_two_rows, jnp.concatenate(up_rounds, axis=0))
    up_total, gate_sum = lax.optimization_barrier(((up_total / u_scale).astype(BF), gate_sum))
    up_sum = scatter_rows(up_total)
    for w in widths:
        k = kept[w]
        codes = head_codes if w == 0 else after(head_codes, kept[w - 1]["o_grad"])
        k["o_grad"], k["out_round"] = head_back(w, k["out_pieces"], codes)

    o_grad = jnp.stack([kept[w]["o_grad"] for w in widths])
    turns = (cosine, sine, jnp.cos(key_angles), jnp.sin(key_angles))
    gate_back = tp_columns(gate_sum.reshape(8, d_rows, ff_cols))
    up_back = tp_columns(up_sum.reshape(8, d_rows, ff_cols))
    q_grad, dk, dv = attend_back(qpos, kpos, turns, q, k_all, v_all, o_grad, tok_rows)
    q_grad, dk, dv, gate_back = lax.optimization_barrier((q_grad, dk, dv, gate_back))
    other = 1 - core

    def half_of(values, which):
        return lax.dynamic_slice_in_dim(values, which * k_cols, k_cols, values.ndim - 1)

    kv_grad = None
    for back in range(group_count):
        part = slice(back * group_rows, (back + 1) * group_rows)
        dkv = jnp.concatenate([half_of(dk[:, part], core), half_of(dv[:, part], core)], axis=-1)
        gone = jnp.concatenate([half_of(dk[:, part], other), half_of(dv[:, part], other)], axis=-1)
        dkv = dkv + turned(swap(gone, CORE))
        if back == 0:
            kv_grad = dkv
        else:
            pairs = [(b, a) for a, b in back_pairs(back)]
            kv_grad = kv_grad + lax.ppermute(dkv, "fsdp", pairs)
    qkv_grad = jnp.concatenate([q_grad, kv_grad], axis=-1)
    qkv_round = (qkv_grad * qkv_scale).astype(BF)
    qkv_scale_acc = jnp.sum(qkv_raw.astype(F32) * qkv_grad, axis=(0, 1))
    qkv_rows = jnp.sum(qkv_round.astype(F32), axis=0).astype(BF)
    qkv_total = (dot_tn(normed, qkv_rows) / qkv_scale).astype(BF)
    qkv_sum = scatter_rows(qkv_total)
    out_total = dot_tn(
        after(attended, qkv_total).reshape(SLOTS * group_rows, HD),
        jnp.concatenate([kept[w]["out_round"] for w in widths], axis=0),
    )
    out_total = (out_total / o_scale_all).astype(BF)
    if whole_heads:
        out_pieces = heads_to_pieces(out_total.reshape(planes, o_rows, model))
        out_pieces = out_pieces.reshape(planes * o_rows, model)
    else:
        whole = jnp.zeros((HEADS * HD, model), BF)
        out_pieces = lax.dynamic_update_slice_in_dim(whole, out_total, t_index * HD, 0)
    low, high = project_back(qkv_round, qkv_w)
    low, up_back = lax.optimization_barrier((low, up_back))
    normed_parts = tp_scatter(low, high)
    gate_grad = by_ff_back(gate_back).astype(F32)
    up_grad = by_ff_back(up_back).astype(F32)
    down_grad = down_sum.reshape(ff_rows, model).astype(F32)
    out_pieces, qkv_sum, gate_grad, up_grad, down_grad = lax.optimization_barrier(
        (out_pieces, qkv_sum, gate_grad, up_grad, down_grad)
    )
    if whole_heads:
        out_sum = scatter_rows(out_pieces)
    else:
        out_sum = lax.psum_scatter(out_pieces, ALL, scatter_dimension=0, tiled=True)
    normed_grad = total(normed_parts)
    _, pull_one = jax.vjp(rms_norm, inputs, pre_attn_gain)
    input_part, gain_one = pull_one(normed_grad)
    input_total = input_part + sum(kept[w]["middle_grad"] for w in widths)

    output_grad = out_sum.reshape(o_rows, model).astype(F32)
    qkv_back = tp_columns(qkv_sum.reshape(8, d_rows, q_cols + 2 * k_cols))
    query_grad = by_head_back(qkv_back[:, :, :q_cols]).astype(F32)
    key_grad = by_head_back(qkv_back[:, :, q_cols : q_cols + k_cols]).astype(F32)
    value_grad = by_head_back(qkv_back[:, :, q_cols + k_cols :]).astype(F32)

    def placed(part, count):
        whole = jnp.zeros((8 * count,), F32)
        return lax.dynamic_update_slice_in_dim(whole, part, t_index * count, 0)

    def placed_ff(part):
        whole = jnp.zeros((planes * group_count, 8, ff_rows), F32)
        block = part.reshape(planes * group_count, 1, ff_rows)
        return lax.dynamic_update_slice(whole, block, (0, t_index, 0)).reshape(-1)

    def over_widths(name):
        return sum(kept[w][name][0] for w in widths)

    vectors = [
        placed(qkv_scale_acc[:q_cols], q_cols),
        placed(qkv_scale_acc[q_cols : q_cols + k_cols], k_cols),
        placed(qkv_scale_acc[q_cols + k_cols :], k_cols),
        over_widths("out_scale_sum"),
        placed_ff(over_widths("gate_sum")),
        placed_ff(over_widths("up_sum")),
        over_widths("down_scale_sum"),
        gain_one,
        over_widths("gain_two"),
        over_widths("gain_three"),
        over_widths("gain_four"),
    ]
    summed = jnp.concatenate([v.reshape(devices, -1) for v in vectors], axis=1)[order]
    for bit in reversed(range(devices.bit_length() - 1)):
        keep = 1 << bit
        summed = summed[:keep] + swap_all(summed[keep:], keep)
    summed = summed[0]
    vector_grads = []
    at = 0
    for v in vectors:
        size = v.shape[0] // devices
        vector_grads.append(summed[at : at + size])
        at += size

    return (
        mixed,
        input_total,
        query_grad,
        key_grad,
        value_grad,
        output_grad,
        gate_grad,
        up_grad,
        down_grad,
        *vector_grads,
    )


def solution(mesh):
    rows = P(ALL, None)
    vector = P(ALL)
    in_specs = (
        (rows,) * 8
        + (vector,) * 7
        + (P(),) * 4
        + (P("dp", None), P("dp", None), P(None, ALL, None))
    )
    out_specs = (P(None, ALL, None),) + (rows,) * 8 + (vector,) * 11
    return jax.shard_map(shards, mesh=mesh, in_specs=in_specs, out_specs=out_specs, check_vma=False)
```

```python
import functools

import jax
import jax.numpy as jnp
from jax import lax
from jax.experimental import pallas as pl
from jax.experimental.pallas import tpu as pltpu
from jax.sharding import PartitionSpec as P

HEADS = 8
KV_HEADS = 4
HD = 256
HALF = HD // 2
SLOTS = 3
EPSILON = 1e-06
SOFT_CAP = 50.0
BF = jnp.bfloat16
F32 = jnp.float32
ALL = ("dp", "fsdp")
STEPS = (1.0, 16.0, 64.0)
VMEM_LIMIT = 60 * 1024 * 1024


def dequantized(codes, width):
    step = STEPS[width]
    if width == 0:
        return codes + BF(0.5)
    return jnp.floor(codes * BF(1.0 / step)) * BF(step) + BF(step / 2)


def rms_norm(values, gain_vector):
    return (
        values
        * lax.rsqrt(jnp.mean(values * values, axis=-1, keepdims=True) + EPSILON)
        * gain_vector
    )


def rotate(values, cosine, sine_part):
    first_half = values[..., :HALF]
    second = values[..., HALF:]
    return jnp.concatenate(
        [first_half * cosine - second * sine_part, second * cosine + first_half * sine_part],
        axis=-1,
    )


def dot(left, right):
    return jnp.dot(left, right, preferred_element_type=F32)


def dot_nt(left, right):
    return lax.dot_general(left, right, (((1,), (1,)), ((), ())), preferred_element_type=F32)


def dot_tn(left, right):
    return lax.dot_general(left, right, (((0,), (0,)), ((), ())), preferred_element_type=F32)


def gated(gate_in, up_in):
    return jax.nn.gelu(gate_in, approximate=True) * up_in


def score_block(qpos_ref, kpos_ref, q, k):
    tanh_part = jnp.tanh(dot_nt(q, k) * (1.0 / SOFT_CAP))
    causal = qpos_ref[...] >= kpos_ref[...]
    exp_scores = jnp.where(causal, jnp.exp(SOFT_CAP * tanh_part), 0.0)
    total = jnp.sum(exp_scores, axis=-1, keepdims=True)
    return tanh_part, exp_scores / total


def attend_kernel(qpos_ref, kpos_ref, q_ref, k_ref, v_ref, o_ref):
    _, probs = score_block(qpos_ref, kpos_ref, q_ref[0], k_ref[0])
    o_ref[0] = dot(probs.astype(BF), v_ref[0]).astype(BF)


def attend_back_kernel(
    qpos_ref,
    kpos_ref,
    qcos_ref,
    qsin_ref,
    kcos_ref,
    ksin_ref,
    q_ref,
    k_ref,
    v_ref,
    do_ref,
    dq_ref,
    dk_ref,
    dv_ref,
):
    q, k, v, do = q_ref[0], k_ref[0], v_ref[0], do_ref[0]

    @pl.when(pl.program_id(1) == 0)
    def _():
        dk_ref[...] = jnp.zeros_like(dk_ref)
        dv_ref[...] = jnp.zeros_like(dv_ref)

    tanh_part, probs = score_block(qpos_ref, kpos_ref, q, k)
    prob_grad = dot_nt(do, v)
    row_dot = jnp.sum(probs * prob_grad, axis=-1, keepdims=True)
    score_grad = (probs * (prob_grad - row_dot) * (1.0 - tanh_part * tanh_part)).astype(BF)
    dq = dot(score_grad, k) * HD ** (-0.5)
    dq_ref[0] = rotate(dq, qcos_ref[...], -qsin_ref[...])
    dk_ref[0] += dot_tn(score_grad, q)
    dv_ref[0] += dot_tn(probs.astype(BF), do)

    @pl.when(pl.program_id(1) == pl.num_programs(1) - 1)
    def _():
        dk_ref[0] = rotate(dk_ref[0], kcos_ref[...], -ksin_ref[...])


def attention_specs(q, keys, tok_rows):
    widths, rows, _ = q.shape
    chunk = 2 * tok_rows
    q_spec = pl.BlockSpec((1, chunk, HD), lambda w, i: (w, i, 0))
    k_spec = pl.BlockSpec((1, keys.shape[1], HD), lambda w, i: (w, 0, 0))
    qpos_spec = pl.BlockSpec((chunk, 1), lambda w, i: (i, 0))
    kpos_spec = pl.BlockSpec((1, keys.shape[1]), lambda w, i: (0, 0))
    turn_specs = [pl.BlockSpec((chunk, HALF), lambda w, i: (i, 0))] * 2
    turn_specs += [pl.BlockSpec((keys.shape[1], HALF), lambda w, i: (0, 0))] * 2
    return (widths, rows // chunk), q_spec, k_spec, qpos_spec, kpos_spec, turn_specs


def attention_cost(q, keys, products):
    pairs = q.shape[0] * q.shape[1] * keys.shape[1]
    return pl.CostEstimate(
        flops=2 * products * pairs * HD,
        bytes_accessed=2 * q.size + 4 * keys.size,
        transcendentals=2 * pairs,
    )


def attend(qpos, kpos, q, k, v, tok_rows):
    grid, q_spec, k_spec, qpos_spec, kpos_spec, _ = attention_specs(q, k, tok_rows)
    return pl.pallas_call(
        attend_kernel,
        grid=grid,
        in_specs=[qpos_spec, kpos_spec, q_spec, k_spec, k_spec],
        out_specs=q_spec,
        out_shape=jax.ShapeDtypeStruct(q.shape, BF),
        compiler_params=pltpu.CompilerParams(vmem_limit_bytes=VMEM_LIMIT),
        cost_estimate=attention_cost(q, k, 2),
        name="attend",
    )(qpos, kpos, q, k, v)


def attend_back(qpos, kpos, turns, q, k, v, do, tok_rows):
    grid, q_spec, k_spec, qpos_spec, kpos_spec, turn_specs = attention_specs(q, k, tok_rows)
    return pl.pallas_call(
        attend_back_kernel,
        grid=grid,
        in_specs=[qpos_spec, kpos_spec, *turn_specs, q_spec, k_spec, k_spec, q_spec],
        out_specs=[q_spec, k_spec, k_spec],
        out_shape=[
            jax.ShapeDtypeStruct(q.shape, F32),
            jax.ShapeDtypeStruct(k.shape, F32),
            jax.ShapeDtypeStruct(k.shape, F32),
        ],
        compiler_params=pltpu.CompilerParams(vmem_limit_bytes=VMEM_LIMIT),
        cost_estimate=attention_cost(q, k, 5),
        name="attend_back",
    )(qpos, kpos, *turns, q, k, v, do)


def project_kernel(
    a_ref, w_hbm, scale_ref, cos_ref, sin_ref, raw_ref, q_ref, kv_ref, kept_hbm, held, sems, out_sems
):
    @pl.when(pl.program_id(0) == 0)
    def _():
        for w in range(SLOTS):
            load_codes(w, (w_hbm,), (held.at[w],), sems)

    copies = keep_copies((held,), (kept_hbm,), out_sems)
    start_on_first(copies)
    a = a_ref[...]
    cosine, sine = cos_ref[...], sin_ref[...]
    for w in range(SLOTS):
        raw = dot(a, held[w])
        raw_ref[w] = raw.astype(BF)
        lin = raw * scale_ref[...]
        q_ref[w] = (rotate(lin[:, :HD], cosine, sine) * HD ** (-0.5)).astype(BF)
        kv_ref[w] = lin[:, HD:]
    wait_on_last(copies)


def project(a, codes, scale, cosine, sine):
    rows, model = a.shape
    cols = codes.shape[1]
    chunk = min(rows, 256)
    turn = pl.BlockSpec((chunk, HALF), lambda i: (i, 0))

    def out(count):
        return pl.BlockSpec((SLOTS, chunk, count), lambda i: (0, i, 0))

    return pl.pallas_call(
        project_kernel,
        grid=(rows // chunk,),
        in_specs=[
            pl.BlockSpec((chunk, model), lambda i: (i, 0)),
            pl.BlockSpec(memory_space=pl.ANY),
            pl.BlockSpec((1, cols), lambda i: (0, 0)),
            turn,
            turn,
        ],
        out_specs=[out(cols), out(HD), out(cols - HD), pl.BlockSpec(memory_space=pl.ANY)],
        out_shape=[
            jax.ShapeDtypeStruct((SLOTS, rows, cols), BF),
            jax.ShapeDtypeStruct((SLOTS, rows, HD), BF),
            jax.ShapeDtypeStruct((SLOTS, rows, cols - HD), F32),
            jax.ShapeDtypeStruct((SLOTS, model, cols), BF),
        ],
        scratch_shapes=[
            pltpu.VMEM((SLOTS, model, cols), BF),
            pltpu.SemaphoreType.DMA((1,)),
            pltpu.SemaphoreType.DMA((1,)),
        ],
        compiler_params=pltpu.CompilerParams(vmem_limit_bytes=VMEM_LIMIT),
        cost_estimate=pl.CostEstimate(
            flops=2 * SLOTS * rows * model * cols,
            bytes_accessed=2 * rows * model + 2 * model * cols + 8 * SLOTS * rows * cols,
            transcendentals=0,
        ),
        name="project",
    )(a, codes, scale[None], cosine, sine)


def heads_kernel(core_ref, own_ref, other_ref, cos_ref, sin_ref, k_ref, v_ref):
    own, other = own_ref[0], other_ref[0]
    cols = own.shape[1] // 2
    first = core_ref[0, 0] == 0
    low = jnp.where(first, own, other)
    high = jnp.where(first, other, own)
    k = jnp.concatenate([low[:, :cols], high[:, :cols]], axis=1)
    k_ref[0] = rotate(k, cos_ref[...], sin_ref[...]).astype(BF)
    v_ref[0] = jnp.concatenate([low[:, cols:], high[:, cols:]], axis=1).astype(BF)


def whole_heads_of(core, own, other, cosine, sine):
    widths, rows, cols = own.shape
    part = rows // 2
    mine = pl.BlockSpec((1, part, cols), lambda w, c: (w, c, 0))
    turn = pl.BlockSpec((part, HALF), lambda w, c: (c, 0))
    return pl.pallas_call(
        heads_kernel,
        grid=(widths, 2),
        in_specs=[
            pl.BlockSpec(memory_space=pltpu.SMEM),
            mine,
            pl.BlockSpec((1, part, cols), lambda w, c: (w, 1 - c, 0)),
            turn,
            turn,
        ],
        out_specs=[mine, mine],
        out_shape=[jax.ShapeDtypeStruct(own.shape, BF)] * 2,
        compiler_params=pltpu.CompilerParams(vmem_limit_bytes=VMEM_LIMIT),
        cost_estimate=pl.CostEstimate(flops=8 * own.size, bytes_accessed=12 * own.size, transcendentals=0),
        name="heads",
    )(core.reshape(1, 1).astype(jnp.int32), own, other, cosine, sine)


def norm_scale(values):
    return lax.rsqrt(jnp.mean(values * values, axis=-1, keepdims=True) + EPSILON)


def norm_back(values, gain, grad):
    r = norm_scale(values)
    weighted = grad * gain
    unit = values * r
    back = r * (weighted - unit * jnp.mean(weighted * unit, axis=-1, keepdims=True))
    return back, jnp.sum(grad * unit, axis=0, keepdims=True)


def output_partial_kernel(width, o_ref, w_ref, low_ref, high_ref, held):
    @pl.when(pl.program_id(0) == 0)
    def _():
        held[...] = dequantized(w_ref[...], width)

    store_halves(low_ref, high_ref, dot(o_ref[0], held[...]).astype(BF))


def output_partial(width, attended, codes):
    rows = attended.shape[1]
    model = codes.shape[1]
    chunk = min(rows // 2, 256)
    specs, shapes = halves_specs(rows, model, chunk)
    return pl.pallas_call(
        functools.partial(output_partial_kernel, width),
        grid=(rows // chunk,),
        in_specs=[
            pl.BlockSpec((1, chunk, HD), lambda i: (width, i, 0)),
            pl.BlockSpec((HD, model), lambda i: (0, 0)),
        ],
        out_specs=specs,
        out_shape=shapes,
        scratch_shapes=[pltpu.VMEM((HD, model), BF)],
        compiler_params=pltpu.CompilerParams(vmem_limit_bytes=VMEM_LIMIT),
        cost_estimate=pl.CostEstimate(
            flops=2 * rows * HD * model, bytes_accessed=2 * rows * model, transcendentals=0
        ),
        name="output_partial",
    )(attended, codes)


def output_norm_kernel(
    part_ref, from_x_ref, from_y_ref, x_ref, scale_ref, post_ref, pre_ref, raw_ref, middle_ref, two_ref
):
    raw = part_ref[...].astype(F32) + from_x_ref[...].astype(F32) + from_y_ref[...].astype(F32)
    raw_ref[...] = raw
    lin = raw * scale_ref[...]
    middle = x_ref[...].astype(F32) + lin * norm_scale(lin) * post_ref[...]
    middle_ref[...] = middle
    two_ref[...] = (middle * norm_scale(middle) * pre_ref[...]).astype(BF)


def output_norm(parts, x, scale, post_gain, pre_gain):
    rows, model = x.shape
    whole = pl.BlockSpec(memory_space=pltpu.VMEM)
    return pl.pallas_call(
        output_norm_kernel,
        in_specs=[whole] * 7,
        out_specs=[whole] * 3,
        out_shape=[
            jax.ShapeDtypeStruct((rows, model), F32),
            jax.ShapeDtypeStruct((rows, model), F32),
            jax.ShapeDtypeStruct((rows, model), BF),
        ],
        compiler_params=pltpu.CompilerParams(vmem_limit_bytes=VMEM_LIMIT),
        cost_estimate=pl.CostEstimate(flops=20 * rows * model, bytes_accessed=18 * rows * model, transcendentals=0),
        name="output_norm",
    )(*parts, x, scale[None], post_gain[None], pre_gain[None])


def loss_kernel(
    live_ref,
    part_ref,
    from_x_ref,
    from_y_ref,
    middle_ref,
    cot_ref,
    scale_ref,
    gain_ref,
    mixed_ref,
    round_ref,
    gain_sum_ref,
    scale_sum_ref,
):
    live = live_ref[0, 0]
    raw = part_ref[...].astype(F32) + from_x_ref[...].astype(F32) + from_y_ref[...].astype(F32)
    scale, gain = scale_ref[...], gain_ref[...]
    lin = raw * scale
    mixed_ref[...] = ((middle_ref[...] + lin * norm_scale(lin) * gain) * live).astype(BF)
    back, gain_sum_ref[...] = norm_back(lin, gain, cot_ref[...].astype(F32) * live)
    round_ref[...] = (back * scale).astype(BF)
    scale_sum_ref[...] = jnp.sum(raw * back, axis=0, keepdims=True)


def loss_step(live, parts, middle, cot, scale, gain):
    rows, model = middle.shape
    whole = pl.BlockSpec(memory_space=pltpu.VMEM)
    return pl.pallas_call(
        loss_kernel,
        in_specs=[pl.BlockSpec(memory_space=pltpu.SMEM)] + [whole] * 7,
        out_specs=[whole] * 4,
        out_shape=[
            jax.ShapeDtypeStruct((rows, model), BF),
            jax.ShapeDtypeStruct((rows, model), BF),
            jax.ShapeDtypeStruct((1, model), F32),
            jax.ShapeDtypeStruct((1, model), F32),
        ],
        compiler_params=pltpu.CompilerParams(vmem_limit_bytes=VMEM_LIMIT),
        cost_estimate=pl.CostEstimate(flops=20 * rows * model, bytes_accessed=16 * rows * model, transcendentals=0),
        name="loss_step",
    )(live, *parts, middle, cot, scale[None], gain[None])


def output_back_kernel(
    live_ref,
    part_ref,
    from_x_ref,
    from_y_ref,
    middle_ref,
    raw_ref,
    cot_ref,
    scale_ref,
    post_ref,
    pre_ref,
    middle_grad_ref,
    round_ref,
    pre_sum_ref,
    post_sum_ref,
    scale_sum_ref,
):
    two_grad = part_ref[...].astype(F32) + from_x_ref[...].astype(F32) + from_y_ref[...].astype(F32)
    back, pre_sum_ref[...] = norm_back(middle_ref[...], pre_ref[...], two_grad)
    middle_grad = cot_ref[...].astype(F32) * live_ref[0, 0] + back
    middle_grad_ref[...] = middle_grad
    raw, scale = raw_ref[...], scale_ref[...]
    lin_grad, post_sum_ref[...] = norm_back(raw * scale, post_ref[...], middle_grad)
    scale_sum_ref[...] = jnp.sum(raw * lin_grad, axis=0, keepdims=True)
    round_ref[...] = (lin_grad * scale).astype(BF)


def output_back(live, parts, middle, raw, cot, scale, post_gain, pre_gain):
    rows, model = middle.shape
    whole = pl.BlockSpec(memory_space=pltpu.VMEM)
    return pl.pallas_call(
        output_back_kernel,
        in_specs=[pl.BlockSpec(memory_space=pltpu.SMEM)] + [whole] * 9,
        out_specs=[whole] * 5,
        out_shape=[
            jax.ShapeDtypeStruct((rows, model), F32),
            jax.ShapeDtypeStruct((rows, model), BF),
            jax.ShapeDtypeStruct((1, model), F32),
            jax.ShapeDtypeStruct((1, model), F32),
            jax.ShapeDtypeStruct((1, model), F32),
        ],
        compiler_params=pltpu.CompilerParams(vmem_limit_bytes=VMEM_LIMIT),
        cost_estimate=pl.CostEstimate(flops=40 * rows * model, bytes_accessed=24 * rows * model, transcendentals=0),
        name="output_back",
    )(live, *parts, middle, raw, cot, scale[None], post_gain[None], pre_gain[None])


def head_back_kernel(width, count, *refs):
    pieces = refs[:count]
    w_ref, do_ref, joined, rows_held, w_held, piece_sems, out_sems = refs[count:]
    gathered = piece_copies(pieces, rows_held, piece_sems)
    start_on_first(gathered)

    @pl.when(pl.program_id(0) == 0)
    def _():
        w_held[...] = dequantized(w_ref[...], width)
        for copy in gathered:
            copy.wait()

    copies = keep_copies((rows_held,), (joined,), out_sems)
    start_on_first(copies)
    chunk = do_ref.shape[0]
    part = rows_held[pl.ds(pl.multiple_of(pl.program_id(0) * chunk, chunk), chunk)]
    do_ref[...] = dot_nt(part, w_held[...]).astype(BF)
    wait_on_last(copies)


def head_back(width, pieces, codes):
    rows = sum(piece.shape[0] for piece in pieces)
    model = codes.shape[1]
    chunk = min(rows, 256)
    whole = pl.BlockSpec(memory_space=pl.ANY)
    return pl.pallas_call(
        functools.partial(head_back_kernel, width, len(pieces)),
        grid=(rows // chunk,),
        in_specs=[whole] * len(pieces) + [pl.BlockSpec((HD, model), lambda i: (0, 0))],
        out_specs=[pl.BlockSpec((chunk, HD), lambda i: (i, 0)), whole],
        out_shape=[
            jax.ShapeDtypeStruct((rows, HD), BF),
            jax.ShapeDtypeStruct((rows, model), BF),
        ],
        scratch_shapes=[
            pltpu.VMEM((rows, model), BF),
            pltpu.VMEM((HD, model), BF),
            pltpu.SemaphoreType.DMA((len(pieces),)),
            pltpu.SemaphoreType.DMA((1,)),
        ],
        compiler_params=pltpu.CompilerParams(vmem_limit_bytes=VMEM_LIMIT),
        cost_estimate=pl.CostEstimate(
            flops=2 * rows * HD * model, bytes_accessed=4 * rows * model, transcendentals=0
        ),
        name="head_back",
    )(*pieces, codes)


def join_kernel(starts, *refs):
    result = refs[-1]
    step = pl.program_id(0)
    for piece, start in zip(refs[:-1], starts):

        @pl.when(step == start // result.shape[0])
        def _(piece=piece, start=start):
            result[pl.ds(start % result.shape[0], piece.shape[0])] = piece[...]


def join(*pieces):
    starts = [0]
    for piece in pieces:
        starts.append(starts[-1] + piece.shape[0])
    total, cols = starts[-1], pieces[0].shape[1]
    rows = pieces[0].shape[0]
    return pl.pallas_call(
        functools.partial(join_kernel, tuple(starts[:-1])),
        grid=(total // rows,),
        in_specs=[pl.BlockSpec(piece.shape, lambda i: (0, 0)) for piece in pieces],
        out_specs=pl.BlockSpec((rows, cols), lambda i: (i, 0)),
        out_shape=jax.ShapeDtypeStruct((total, cols), pieces[0].dtype),
        compiler_params=pltpu.CompilerParams(vmem_limit_bytes=VMEM_LIMIT),
        cost_estimate=pl.CostEstimate(flops=0, bytes_accessed=4 * total * cols, transcendentals=0),
        name="join",
    )(*pieces)


GELU_A = 0.7978845608028654
GELU_B = 0.044715


def load_codes(width, codes, held, sems):
    copies = [
        pltpu.make_async_copy(source, target, sems.at[i])
        for i, (source, target) in enumerate(zip(codes, held))
    ]
    for copy in copies:
        copy.start()
    for copy, target in zip(copies, held):
        copy.wait()
        rows = target.shape[0]
        step = 128 if rows % 128 == 0 else 16

        def turn(i, carry, target=target, step=step):
            part = pl.ds(pl.multiple_of(i * step, step), step)
            target[part] = dequantized(target[part], width)
            return carry

        lax.fori_loop(0, rows // step, turn, 0)


def halves_specs(rows, model, chunk):
    steps = rows // chunk // 2
    low = pl.BlockSpec((chunk, model), lambda i: (jnp.minimum(i, steps - 1), 0))
    high = pl.BlockSpec((chunk, model), lambda i: (jnp.maximum(i - steps, 0), 0))
    return [low, high], [jax.ShapeDtypeStruct((rows // 2, model), BF)] * 2


def store_halves(low_ref, high_ref, value):
    step, steps = pl.program_id(0), pl.num_programs(0)

    @pl.when(step < steps // 2)
    def _():
        low_ref[...] = value

    @pl.when(step >= steps // 2)
    def _():
        high_ref[...] = value


def keep_copies(held, kept, sems):
    return [
        pltpu.make_async_copy(source, target, sems.at[i])
        for i, (source, target) in enumerate(zip(held, kept))
    ]


def start_on_first(copies):
    @pl.when(pl.program_id(0) == 0)
    def _():
        for copy in copies:
            copy.start()


def wait_on_last(copies):
    @pl.when(pl.program_id(0) == pl.num_programs(0) - 1)
    def _():
        for copy in copies:
            copy.wait()


def piece_copies(pieces, held, sems):
    copies = []
    at = 0
    for i, piece in enumerate(pieces):
        rows = piece.shape[0]
        copies.append(pltpu.make_async_copy(piece, held.at[pl.ds(at, rows)], sems.at[i]))
        at += rows
    return copies


def ffn_in_kernel(width, count, *refs):
    pieces = refs[:count]
    (
        g_hbm,
        u_hbm,
        gs_ref,
        us_ref,
        gate_ref,
        up_ref,
        hidden_ref,
        a_hbm,
        gw_hbm,
        uw_hbm,
        a_held,
        g_held,
        u_held,
        piece_sems,
        sems,
        out_sems,
    ) = refs[count:]
    gathered = piece_copies(pieces, a_held, piece_sems)
    start_on_first(gathered)

    @pl.when(pl.program_id(0) == 0)
    def _():
        load_codes(width, (g_hbm, u_hbm), (g_held, u_held), sems)
        for copy in gathered:
            copy.wait()

    copies = keep_copies((a_held, g_held, u_held), (a_hbm, gw_hbm, uw_hbm), out_sems)
    start_on_first(copies)
    chunk = gate_ref.shape[0]
    a = a_held[pl.ds(pl.multiple_of(pl.program_id(0) * chunk, chunk), chunk)]
    gate = dot(a, g_held[...])
    up = dot(a, u_held[...])
    gate_ref[...] = gate.astype(BF)
    up_ref[...] = up.astype(BF)
    gate = gate * gs_ref[...]
    inner = jnp.tanh(GELU_A * (gate + GELU_B * gate * gate * gate))
    hidden_ref[...] = (0.5 * gate * (1.0 + inner) * (up * us_ref[...])).astype(BF)
    wait_on_last(copies)


def ffn_in(width, pieces, gate_codes, up_codes, g_scale, u_scale):
    rows = sum(piece.shape[0] for piece in pieces)
    model, features = gate_codes.shape
    chunk = min(rows, 256)
    whole = pl.BlockSpec(memory_space=pl.ANY)
    vector = pl.BlockSpec((1, features), lambda i: (0, 0))
    block = pl.BlockSpec((chunk, features), lambda i: (i, 0))
    return pl.pallas_call(
        functools.partial(ffn_in_kernel, width, len(pieces)),
        grid=(rows // chunk,),
        in_specs=[whole] * len(pieces) + [whole, whole, vector, vector],
        out_specs=[block] * 3 + [whole] * 3,
        out_shape=[jax.ShapeDtypeStruct((rows, features), BF)] * 3
        + [jax.ShapeDtypeStruct((rows, model), BF)]
        + [jax.ShapeDtypeStruct((model, features), BF)] * 2,
        scratch_shapes=[
            pltpu.VMEM((rows, model), BF),
            pltpu.VMEM((model, features), BF),
            pltpu.VMEM((model, features), BF),
            pltpu.SemaphoreType.DMA((len(pieces),)),
            pltpu.SemaphoreType.DMA((2,)),
            pltpu.SemaphoreType.DMA((3,)),
        ],
        compiler_params=pltpu.CompilerParams(vmem_limit_bytes=VMEM_LIMIT),
        cost_estimate=pl.CostEstimate(
            flops=4 * rows * model * features,
            bytes_accessed=2 * (rows * model + 2 * model * features + 3 * rows * features),
            transcendentals=rows * features,
        ),
        name="ffn_in",
    )(*pieces, gate_codes, up_codes, g_scale[None], u_scale[None])


def down_grad_kernel(counts, *refs):
    pieces, refs = refs[: sum(counts)], refs[sum(counts) :]
    widths = len(counts)
    h_refs, scale_ref, out_ref = refs[:widths], refs[widths], refs[widths + 1]
    joined, held = refs[widths + 2 : 2 * widths + 2], refs[2 * widths + 2]
    piece_sems, out_sems = refs[2 * widths + 3 :]
    groups = []
    at = 0
    for w, count in enumerate(counts):
        groups.append(piece_copies(pieces[at : at + count], held.at[w], piece_sems.at[w]))
        at += count
    for group in groups:
        start_on_first(group)
    copies = keep_copies([held.at[w] for w in range(widths)], joined, out_sems)
    first = pl.program_id(0) == 0
    product = None
    for w in range(widths):

        @pl.when(first)
        def _(w=w):
            for copy in groups[w]:
                copy.wait()
            copies[w].start()

        part = dot_tn(h_refs[w][...], held[w])
        product = part if product is None else product + part
    out_ref[...] = (product / scale_ref[...]).astype(BF)
    wait_on_last(copies)


def down_gradient(hiddens, piece_lists, scale):
    rows, features = hiddens[0].shape
    model = scale.shape[0]
    widths = len(hiddens)
    counts = tuple(len(pieces) for pieces in piece_lists)
    chunk = 128 if features % 128 == 0 else features
    whole = pl.BlockSpec(memory_space=pl.ANY)
    return pl.pallas_call(
        functools.partial(down_grad_kernel, counts),
        grid=(features // chunk,),
        in_specs=[whole] * sum(counts)
        + [pl.BlockSpec((rows, chunk), lambda i: (0, i))] * widths
        + [pl.BlockSpec((1, model), lambda i: (0, 0))],
        out_specs=[pl.BlockSpec((chunk, model), lambda i: (i, 0))] + [whole] * widths,
        out_shape=[jax.ShapeDtypeStruct((features, model), BF)]
        + [jax.ShapeDtypeStruct((rows, model), BF)] * widths,
        scratch_shapes=[
            pltpu.VMEM((widths, rows, model), BF),
            pltpu.SemaphoreType.DMA((widths, max(counts))),
            pltpu.SemaphoreType.DMA((widths,)),
        ],
        compiler_params=pltpu.CompilerParams(vmem_limit_bytes=VMEM_LIMIT),
        cost_estimate=pl.CostEstimate(
            flops=2 * widths * rows * model * features,
            bytes_accessed=2 * (2 * widths * rows * model + features * (model + widths * rows)),
            transcendentals=0,
        ),
        name="down_grad",
    )(*[piece for pieces in piece_lists for piece in pieces], *hiddens, scale[None])


def ffn_out_kernel(width, h_ref, d_hbm, low_ref, high_ref, dw_hbm, d_held, sems, out_sems):
    @pl.when(pl.program_id(0) == 0)
    def _():
        load_codes(width, (d_hbm,), (d_held,), sems)

    copies = keep_copies((d_held,), (dw_hbm,), out_sems)
    start_on_first(copies)
    store_halves(low_ref, high_ref, dot(h_ref[...], d_held[...]).astype(BF))
    wait_on_last(copies)


def ffn_out(width, hidden, down_codes):
    rows, features = hidden.shape
    model = down_codes.shape[1]
    chunk = min(rows // 2, 256)
    whole = pl.BlockSpec(memory_space=pl.ANY)
    specs, shapes = halves_specs(rows, model, chunk)
    return pl.pallas_call(
        functools.partial(ffn_out_kernel, width),
        grid=(rows // chunk,),
        in_specs=[pl.BlockSpec((chunk, features), lambda i: (i, 0)), whole],
        out_specs=specs + [whole],
        out_shape=shapes + [jax.ShapeDtypeStruct((features, model), BF)],
        scratch_shapes=[
            pltpu.VMEM((features, model), BF),
            pltpu.SemaphoreType.DMA((1,)),
            pltpu.SemaphoreType.DMA((1,)),
        ],
        compiler_params=pltpu.CompilerParams(vmem_limit_bytes=VMEM_LIMIT),
        cost_estimate=pl.CostEstimate(
            flops=2 * rows * model * features,
            bytes_accessed=2 * (rows * model + 2 * model * features + rows * features),
            transcendentals=0,
        ),
        name="ffn_out",
    )(hidden, down_codes)


def ffn_back_kernel(
    dr_ref,
    gate_ref,
    up_ref,
    d_hbm,
    g_hbm,
    u_hbm,
    gs_ref,
    us_ref,
    after_hbm,
    low_ref,
    high_ref,
    gr_ref,
    ur_ref,
    gsum_ref,
    usum_ref,
    d_held,
    g_held,
    u_held,
    sems,
):
    del after_hbm
    first = pl.program_id(0) == 0
    copies = keep_copies((d_hbm, g_hbm, u_hbm), (d_held, g_held, u_held), sems)
    start_on_first(copies)

    @pl.when(first)
    def _():
        gsum_ref[...] = jnp.zeros_like(gsum_ref)
        usum_ref[...] = jnp.zeros_like(usum_ref)
        copies[0].wait()

    hidden_grad = dot_nt(dr_ref[...], d_held[...])
    gate_raw = gate_ref[...].astype(F32)
    up_raw = up_ref[...].astype(F32)
    gate = gate_raw * gs_ref[...]
    up = up_raw * us_ref[...]
    square = gate * gate
    inner = jnp.tanh(GELU_A * (gate + GELU_B * gate * square))
    half_sum = 0.5 * (1.0 + inner)
    slope = half_sum + 0.5 * gate * (1.0 - inner * inner) * (
        GELU_A * (1.0 + 3.0 * GELU_B * square)
    )
    gate_grad = hidden_grad * up * slope
    up_grad = hidden_grad * (gate * half_sum)
    gsum_ref[...] += jnp.sum(gate_raw * gate_grad, axis=0, keepdims=True)
    usum_ref[...] += jnp.sum(up_raw * up_grad, axis=0, keepdims=True)
    gate_round = (gate_grad * gs_ref[...]).astype(BF)
    up_round = (up_grad * us_ref[...]).astype(BF)
    gr_ref[...] = gate_round
    ur_ref[...] = up_round

    @pl.when(first)
    def _():
        copies[1].wait()
        copies[2].wait()

    store_halves(
        low_ref,
        high_ref,
        (dot_nt(gate_round, g_held[...]) + dot_nt(up_round, u_held[...])).astype(BF),
    )


def ffn_back(down_round, gate_raw, up_raw, down_w, gate_w, up_w, g_scale, u_scale, after):
    rows, model = down_round.shape
    features = gate_w.shape[1]
    chunk = min(rows // 2, 256)
    whole = pl.BlockSpec(memory_space=pl.ANY)
    vector = pl.BlockSpec((1, features), lambda i: (0, 0))
    block = pl.BlockSpec((chunk, features), lambda i: (i, 0))
    wide = pl.BlockSpec((chunk, model), lambda i: (i, 0))
    specs, shapes = halves_specs(rows, model, chunk)
    return pl.pallas_call(
        ffn_back_kernel,
        grid=(rows // chunk,),
        in_specs=[wide, block, block, whole, whole, whole, vector, vector, whole],
        out_specs=specs + [block, block, vector, vector],
        out_shape=shapes
        + [
            jax.ShapeDtypeStruct((rows, features), BF),
            jax.ShapeDtypeStruct((rows, features), BF),
            jax.ShapeDtypeStruct((1, features), F32),
            jax.ShapeDtypeStruct((1, features), F32),
        ],
        scratch_shapes=[
            pltpu.VMEM((features, model), BF),
            pltpu.VMEM((model, features), BF),
            pltpu.VMEM((model, features), BF),
            pltpu.SemaphoreType.DMA((3,)),
        ],
        compiler_params=pltpu.CompilerParams(vmem_limit_bytes=VMEM_LIMIT),
        cost_estimate=pl.CostEstimate(
            flops=6 * rows * model * features,
            bytes_accessed=2 * (2 * rows * model + 3 * model * features + 4 * rows * features),
            transcendentals=rows * features,
        ),
        name="ffn_back",
    )(down_round, gate_raw, up_raw, down_w, gate_w, up_w, g_scale[None], u_scale[None], after)


def project_back_kernel(round_ref, w_hbm, low_ref, high_ref, held, sems):
    copies = keep_copies((w_hbm,), (held,), sems)
    start_on_first(copies)

    @pl.when(pl.program_id(0) == 0)
    def _():
        copies[0].wait()

    product = dot_nt(round_ref[0], held[0])
    for w in range(1, SLOTS):
        product = product + dot_nt(round_ref[w], held[w])
    store_halves(low_ref, high_ref, product.astype(BF))


def project_back(rounded, weights):
    _, rows, cols = rounded.shape
    model = weights.shape[1]
    chunk = min(rows // 2, 256)
    specs, shapes = halves_specs(rows, model, chunk)
    return pl.pallas_call(
        project_back_kernel,
        grid=(rows // chunk,),
        in_specs=[
            pl.BlockSpec((SLOTS, chunk, cols), lambda i: (0, i, 0)),
            pl.BlockSpec(memory_space=pl.ANY),
        ],
        out_specs=specs,
        out_shape=shapes,
        scratch_shapes=[pltpu.VMEM((SLOTS, model, cols), BF), pltpu.SemaphoreType.DMA((1,))],
        compiler_params=pltpu.CompilerParams(vmem_limit_bytes=VMEM_LIMIT),
        cost_estimate=pl.CostEstimate(
            flops=2 * SLOTS * rows * model * cols,
            bytes_accessed=2 * (rows * model + SLOTS * cols * (model + rows)),
            transcendentals=0,
        ),
        name="project_back",
    )(rounded, weights)


def shards(
    tokens,
    query_codes,
    key_codes,
    value_codes,
    output_codes,
    gate_codes,
    up_codes,
    down_codes,
    query_scale,
    key_scale,
    value_scale,
    output_scale,
    gate_scale,
    up_scale,
    down_scale,
    pre_attn_gain,
    post_attn_gain,
    pre_ffw_gain,
    post_ffw_gain,
    slot_width,
    slot_live,
    cotangent,
):
    planes = lax.axis_size("dp")
    width = lax.axis_size("fsdp")
    devices = planes * width
    group_count = width // 8
    rank = lax.axis_index("fsdp")
    me = lax.axis_index("dp") * width + rank
    t_index, group = rank % 8, rank // 8
    core = rank % 2
    CORE, X, Y = 1, 2, 4
    groups = None
    if group_count > 1:
        groups = [[g * 8 + j for j in range(8)] for g in range(group_count)]
        across = [[g * 8 + j for g in range(group_count)] for j in range(8)]

    def swap(values, mask):
        return lax.ppermute(values, "fsdp", [(i, i ^ mask) for i in range(width)])

    def swap_all(values, mask):
        return lax.ppermute(values, ALL, [(i, i ^ mask) for i in range(devices)])

    tok_rows, model = tokens.shape
    group_rows = 8 * tok_rows
    d_rows = query_codes.shape[0]
    o_rows = output_codes.shape[0]
    ff_rows = down_codes.shape[0]
    q_cols = query_codes.shape[1] // 8
    k_cols = key_codes.shape[1] // 8
    ff_cols = ff_rows * planes * group_count
    widths = range(SLOTS)

    def tp_pieces(block):
        from_x = swap(block, X)
        from_y = swap(block, Y)
        cut = block.shape[0] // 2
        first = swap(from_y[:cut], X)
        second = swap(from_x[cut:], Y)
        same = [block, from_x, from_y, first, second]
        return same + [swap(piece, CORE) for piece in same]

    def tp_gather(block):
        return join(*tp_pieces(block))

    def after(values, *others):
        return lax.optimization_barrier((values, *others))[0]

    def core_sum(low, high):
        return (low.astype(F32) + swap(high, CORE).astype(F32)).astype(BF)

    def tp_scatter(low, high):
        return plane_sum(core_sum(low, high))

    def plane_sum(pair):
        rows = pair.shape[0] // 4
        cut = rows // 2
        pair = pair.reshape(2, 2, rows, model)
        got_x = swap(pair[1, 1, :cut], X)
        got_y = swap(pair[1, 1, cut:], Y)
        for_x = jnp.concatenate(
            [pair[0, 1, :cut], (pair[0, 1, cut:].astype(F32) + got_y.astype(F32)).astype(BF)]
        )
        for_y = jnp.concatenate(
            [(pair[1, 0, :cut].astype(F32) + got_x.astype(F32)).astype(BF), pair[1, 0, cut:]]
        )
        return pair[0, 0], swap(for_x, X), swap(for_y, Y)

    def total(parts):
        return sum(part.astype(F32) for part in parts)

    def tp_columns(blocks):
        return lax.all_to_all(blocks, "fsdp", 0, 0, tiled=True, axis_index_groups=groups)

    def gather_rows(rows):
        if group_count > 1:
            rows = lax.all_gather(rows, "fsdp", axis=0, tiled=True, axis_index_groups=across)
        return lax.all_gather(rows, "dp", axis=0, tiled=True)

    def scatter_rows(grad):
        rows = lax.psum_scatter(grad, "dp", scatter_dimension=0, tiled=True)
        if group_count > 1:
            rows = lax.psum_scatter(
                rows, "fsdp", scatter_dimension=0, tiled=True, axis_index_groups=across
            )
        return rows

    small = jnp.concatenate(
        [query_scale, key_scale, value_scale, output_scale, gate_scale, up_scale, down_scale]
    )
    all_small = small[None]
    for bit in range(devices.bit_length() - 1):
        all_small = jnp.concatenate([all_small, swap_all(all_small, 1 << bit)], axis=0)
    order = jnp.arange(devices, dtype=jnp.int32) ^ me
    all_small = all_small[order]
    cuts = []
    at = 0
    for vector in (
        query_scale,
        key_scale,
        value_scale,
        output_scale,
        gate_scale,
        up_scale,
        down_scale,
    ):
        cuts.append(all_small[:, at : at + vector.shape[0]].reshape(-1))
        at += vector.shape[0]
    q_scale_all, k_scale_all, v_scale_all, o_scale_all, g_scale_all, u_scale_all, d_scale_all = cuts

    def own_ff(vector):
        cut = vector.reshape(planes * group_count, 8, ff_rows)
        return lax.dynamic_index_in_dim(cut, t_index, 1, keepdims=False).reshape(ff_cols)

    qkv_scale = jnp.concatenate(
        [
            lax.dynamic_slice_in_dim(q_scale_all, t_index * q_cols, q_cols),
            lax.dynamic_slice_in_dim(k_scale_all, t_index * k_cols, k_cols),
            lax.dynamic_slice_in_dim(v_scale_all, t_index * k_cols, k_cols),
        ]
    )
    g_scale = own_ff(g_scale_all)
    u_scale = own_ff(u_scale_all)

    def by_head(codes):
        return codes.reshape(codes.shape[0], 8, -1).transpose(1, 0, 2)

    def by_head_back(blocks):
        return blocks.transpose(1, 0, 2).reshape(blocks.shape[1], -1)

    def by_ff(codes):
        cut = codes.reshape(d_rows, planes * group_count, 8, ff_rows)
        return cut.transpose(2, 0, 1, 3).reshape(8, d_rows, ff_cols)

    def by_ff_back(blocks):
        cut = blocks.reshape(8, d_rows, planes * group_count, ff_rows)
        return cut.transpose(1, 2, 0, 3).reshape(d_rows, 8 * ff_cols)

    def merged(blocks):
        return blocks.reshape(8 * d_rows, blocks.shape[2])

    qkv_blocks = jnp.concatenate(
        [by_head(query_codes), by_head(key_codes), by_head(value_codes)], axis=2
    )
    inputs = tokens.astype(F32)
    qkv_mine = merged(tp_columns(qkv_blocks))
    qkv_codes = gather_rows(qkv_mine)
    gate_mine = merged(tp_columns(by_ff(after(gate_codes, qkv_mine))))
    up_mine = merged(tp_columns(by_ff(after(up_codes, gate_mine))))
    gate_codes_t = gather_rows(gate_mine)
    normed_own, up_mine = lax.optimization_barrier(
        (rms_norm(inputs, pre_attn_gain).astype(BF), up_mine)
    )
    normed = after(tp_gather(normed_own), qkv_scale)

    whole_heads = group_count == 1 and 8 % planes == 0
    heads_per_plane = max(1, 8 // planes)

    def turn(step):
        pairs = []
        for source in range(8):
            plane = (source + step) % planes
            pairs.append((source, plane * heads_per_plane + source // planes))
        return pairs

    def pieces_to_heads(pieces):
        result = jnp.zeros_like(pieces)
        for step in range(planes):
            piece = lax.dynamic_index_in_dim(pieces, (rank + step) % planes, 0, keepdims=False)
            moved = lax.ppermute(piece, "fsdp", turn(step))
            place = (rank // heads_per_plane - step) % planes
            result = lax.dynamic_update_index_in_dim(result, moved, place, 0)
        return result

    def heads_to_pieces(pieces):
        result = jnp.zeros_like(pieces)
        for step in range(planes):
            place = (rank // heads_per_plane - step) % planes
            piece = lax.dynamic_index_in_dim(pieces, place, 0, keepdims=False)
            moved = lax.ppermute(piece, "fsdp", [(b, a) for a, b in turn(step)])
            result = lax.dynamic_update_index_in_dim(result, moved, (rank + step) % planes, 0)
        return result

    output_pieces = gather_rows(output_codes)

    blocks_at = jnp.stack([t_index ^ (c + 2 * x + 4 * y) for c in (0, 1) for y in (0, 1) for x in (0, 1)])
    positions = ((group * 8 + blocks_at) * tok_rows)[:, None] + jnp.arange(tok_rows, dtype=jnp.int32)
    positions = positions.reshape(group_rows)
    far = jnp.int32(1 << 30)
    key_positions = []
    for back in range(group_count):
        earlier = positions - back * group_rows
        key_positions.append(jnp.where(earlier >= 0, earlier, far))
    kpos = jnp.concatenate(key_positions)[None, :]
    qpos = positions[:, None]
    inv_rates = 10000.0 ** (-jnp.arange(HALF, dtype=F32) / HALF)
    angles = positions.astype(F32)[:, None] * inv_rates[None, :]
    cosine, sine = jnp.cos(angles), jnp.sin(angles)
    key_angles = jnp.concatenate(
        [(positions - back * group_rows).astype(F32) for back in range(group_count)]
    )[:, None] * inv_rates[None, :]

    qkv_raw, q, kv_own, qkv_w = project(normed, qkv_codes, qkv_scale, cosine, sine)
    k_near, v_near = whole_heads_of(core, kv_own, swap(kv_own, CORE), cosine, sine)

    if whole_heads:
        head_codes = pieces_to_heads(output_pieces.reshape(planes, o_rows, model)).reshape(HD, model)
    else:
        every = lax.all_gather(output_codes, ALL, axis=0, tiled=True)
        head_codes = lax.dynamic_slice_in_dim(every, t_index * HD, HD, 0)

    def turned(values):
        middle_row = group_rows // 2
        return jnp.concatenate([values[..., middle_row:, :], values[..., :middle_row, :]], axis=-2)

    def back_pairs(back):
        return [(i, i + 8 * back) for i in range(width) if i + 8 * back < width]

    k_parts, v_parts = [k_near], [v_near]
    for back in range(1, group_count):
        k_parts.append(lax.ppermute(k_near, "fsdp", back_pairs(back)))
        v_parts.append(lax.ppermute(v_near, "fsdp", back_pairs(back)))
    k_all = jnp.concatenate(k_parts, axis=1)
    v_all = jnp.concatenate(v_parts, axis=1)
    attended = attend(qpos, kpos, q, k_all, v_all, tok_rows)

    up_codes_t = gather_rows(up_mine)
    down_codes_t = gather_rows(down_codes)

    slot_of, live_of, cot_of = [], [], []
    for w in widths:
        slot = jnp.int32(0)
        for s in range(SLOTS):
            slot = jnp.where(slot_width[0, s] == w, s, slot)
        slot_of.append(slot)
        live = lax.dynamic_index_in_dim(slot_live[0], slot, 0, keepdims=False)
        live_of.append(live.astype(F32).reshape(1, 1))
        cot_of.append(lax.dynamic_index_in_dim(cotangent, slot, 0, keepdims=False))
    kept = [dict() for w in widths]
    for w in widths:
        k = kept[w]
        blocks = attended if w == 0 else after(attended, kept[w - 1]["low"])
        k["low"], high = output_partial(w, blocks, head_codes)
        k["out_raw"], k["middle"], two = output_norm(
            tp_scatter(k["low"], high), tokens, o_scale_all, post_attn_gain, pre_ffw_gain
        )
        k["two_pieces"] = tp_pieces(two)
    for w in widths:
        k = kept[w]
        (
            k["gate_raw"],
            k["up_raw"],
            k["hidden"],
            k["normed_two"],
            k["gate_w"],
            k["up_w"],
        ) = ffn_in(w, k["two_pieces"], gate_codes_t, up_codes_t, g_scale, u_scale)

    hiddens = lax.optimization_barrier(tuple(kept[w]["hidden"] for w in widths))
    for w in widths:
        k = kept[w]
        k["hidden"] = hiddens[w] if w == 0 else after(hiddens[w], kept[w - 1]["down_w"])
        if w == 2:
            k["hidden"], kept[0]["pair"] = lax.optimization_barrier((k["hidden"], kept[0]["pair"]))
        low, high, k["down_w"] = ffn_out(w, k["hidden"], down_codes_t)
        k["pair"] = core_sum(low, high)
    for w in widths:
        kept[w]["down_parts"] = plane_sum(kept[w]["pair"])

    mixed = jnp.zeros((SLOTS, tok_rows, model), BF)
    for w in widths:
        k = kept[w]
        cot = cot_of[w] if w == 0 else after(cot_of[w], kept[w - 1]["gain_four"])
        result, rounded, k["gain_four"], k["down_scale_sum"] = loss_step(
            live_of[w], k["down_parts"], k["middle"], cot, d_scale_all, post_ffw_gain
        )
        mixed = lax.dynamic_update_index_in_dim(mixed, result, slot_of[w], 0)
        k["down_pieces"] = tp_pieces(rounded)
    down_total, *down_rounds = down_gradient(
        [kept[w]["hidden"] for w in widths], [kept[w]["down_pieces"] for w in widths], d_scale_all
    )
    down_sum = scatter_rows(down_total)
    for w in widths:
        k = kept[w]
        low, high, k["gate_round"], k["up_round"], k["gate_sum"], k["up_sum"] = ffn_back(
            down_rounds[w],
            k["gate_raw"],
            k["up_raw"],
            k["down_w"],
            k["gate_w"],
            k["up_w"],
            g_scale,
            u_scale,
            down_total if w == 0 else kept[w - 1]["gate_sum"],
        )
        k["two_parts"] = tp_scatter(low, high)
    normed_two_rows = jnp.concatenate([kept[w]["normed_two"] for w in widths], axis=0)
    gate_rounds = [kept[w]["gate_round"] for w in widths]
    *gate_rounds, down_sum = lax.optimization_barrier((*gate_rounds, down_sum))
    gate_total = dot_tn(normed_two_rows, jnp.concatenate(gate_rounds, axis=0))
    gate_sum = scatter_rows((gate_total / g_scale).astype(BF))
    for w in widths:
        k = kept[w]
        cot = cot_of[w] if w == 0 else after(cot_of[w], kept[w - 1]["gain_two"])
        k["middle_grad"], rounded, k["gain_three"], k["gain_two"], k["out_scale_sum"] = output_back(
            live_of[w],
            k["two_parts"],
            k["middle"],
            k["out_raw"],
            cot,
            o_scale_all,
            post_attn_gain,
            pre_ffw_gain,
        )
        k["out_pieces"] = tp_pieces(rounded)
    up_rounds = [kept[w]["up_round"] for w in widths]
    *up_rounds, _ = lax.optimization_barrier((*up_rounds, kept[2]["gain_two"]))
    up_total = dot_tn(normed_two_rows, jnp.concatenate(up_rounds, axis=0))
    up_total, gate_sum = lax.optimization_barrier(((up_total / u_scale).astype(BF), gate_sum))
    up_sum = scatter_rows(up_total)
    for w in widths:
        k = kept[w]
        codes = head_codes if w == 0 else after(head_codes, kept[w - 1]["o_grad"])
        k["o_grad"], k["out_round"] = head_back(w, k["out_pieces"], codes)

    o_grad = jnp.stack([kept[w]["o_grad"] for w in widths])
    turns = (cosine, sine, jnp.cos(key_angles), jnp.sin(key_angles))
    gate_back = tp_columns(gate_sum.reshape(8, d_rows, ff_cols))
    up_back = tp_columns(up_sum.reshape(8, d_rows, ff_cols))
    q_grad, dk, dv = attend_back(qpos, kpos, turns, q, k_all, v_all, o_grad, tok_rows)
    other = 1 - core

    def half_of(values, which):
        return lax.dynamic_slice_in_dim(values, which * k_cols, k_cols, values.ndim - 1)

    kv_grad = None
    for back in range(group_count):
        part = slice(back * group_rows, (back + 1) * group_rows)
        dkv = jnp.concatenate([half_of(dk[:, part], core), half_of(dv[:, part], core)], axis=-1)
        gone = jnp.concatenate([half_of(dk[:, part], other), half_of(dv[:, part], other)], axis=-1)
        dkv = dkv + turned(swap(gone, CORE))
        if back == 0:
            kv_grad = dkv
        else:
            pairs = [(b, a) for a, b in back_pairs(back)]
            kv_grad = kv_grad + lax.ppermute(dkv, "fsdp", pairs)
    qkv_grad = jnp.concatenate([q_grad, kv_grad], axis=-1)
    qkv_round = (qkv_grad * qkv_scale).astype(BF)
    qkv_scale_acc = jnp.sum(qkv_raw.astype(F32) * qkv_grad, axis=(0, 1))
    qkv_rows = jnp.sum(qkv_round.astype(F32), axis=0).astype(BF)
    qkv_total = (dot_tn(normed, qkv_rows) / qkv_scale).astype(BF)
    qkv_sum = scatter_rows(qkv_total)
    low, high = project_back(after(qkv_round, qkv_total), qkv_w)
    normed_parts = tp_scatter(low, high)
    out_total = dot_tn(
        after(attended, low).reshape(SLOTS * group_rows, HD),
        jnp.concatenate([kept[w]["out_round"] for w in widths], axis=0),
    )
    out_total = (out_total / o_scale_all).astype(BF)
    if whole_heads:
        out_pieces = heads_to_pieces(out_total.reshape(planes, o_rows, model))
        out_pieces = out_pieces.reshape(planes * o_rows, model)
    else:
        whole = jnp.zeros((HEADS * HD, model), BF)
        out_pieces = lax.dynamic_update_slice_in_dim(whole, out_total, t_index * HD, 0)
    gate_grad = by_ff_back(gate_back).astype(F32)
    up_grad = by_ff_back(up_back).astype(F32)
    down_grad = down_sum.reshape(ff_rows, model).astype(F32)
    normed_parts, qkv_sum, gate_grad = lax.optimization_barrier((normed_parts, qkv_sum, gate_grad))
    out_pieces, up_grad, down_grad = lax.optimization_barrier((out_pieces, up_grad, down_grad))
    if whole_heads:
        out_sum = scatter_rows(out_pieces)
    else:
        out_sum = lax.psum_scatter(out_pieces, ALL, scatter_dimension=0, tiled=True)
    normed_grad = total(normed_parts)
    _, pull_one = jax.vjp(rms_norm, inputs, pre_attn_gain)
    input_part, gain_one = pull_one(normed_grad)
    input_total = input_part + sum(kept[w]["middle_grad"] for w in widths)

    output_grad = out_sum.reshape(o_rows, model).astype(F32)
    qkv_back = tp_columns(qkv_sum.reshape(8, d_rows, q_cols + 2 * k_cols))
    query_grad = by_head_back(qkv_back[:, :, :q_cols]).astype(F32)
    key_grad = by_head_back(qkv_back[:, :, q_cols : q_cols + k_cols]).astype(F32)
    value_grad = by_head_back(qkv_back[:, :, q_cols + k_cols :]).astype(F32)

    def placed(part, count):
        whole = jnp.zeros((8 * count,), F32)
        return lax.dynamic_update_slice_in_dim(whole, part, t_index * count, 0)

    def placed_ff(part):
        whole = jnp.zeros((planes * group_count, 8, ff_rows), F32)
        block = part.reshape(planes * group_count, 1, ff_rows)
        return lax.dynamic_update_slice(whole, block, (0, t_index, 0)).reshape(-1)

    def over_widths(name):
        return sum(kept[w][name][0] for w in widths)

    vectors = [
        placed(qkv_scale_acc[:q_cols], q_cols),
        placed(qkv_scale_acc[q_cols : q_cols + k_cols], k_cols),
        placed(qkv_scale_acc[q_cols + k_cols :], k_cols),
        over_widths("out_scale_sum"),
        placed_ff(over_widths("gate_sum")),
        placed_ff(over_widths("up_sum")),
        over_widths("down_scale_sum"),
        gain_one,
        over_widths("gain_two"),
        over_widths("gain_three"),
        over_widths("gain_four"),
    ]
    summed = jnp.concatenate([v.reshape(devices, -1) for v in vectors], axis=1)[order]
    for bit in reversed(range(devices.bit_length() - 1)):
        keep = 1 << bit
        summed = summed[:keep] + swap_all(summed[keep:], keep)
    summed = summed[0]
    vector_grads = []
    at = 0
    for v in vectors:
        size = v.shape[0] // devices
        vector_grads.append(summed[at : at + size])
        at += size

    return (
        mixed,
        input_total,
        query_grad,
        key_grad,
        value_grad,
        output_grad,
        gate_grad,
        up_grad,
        down_grad,
        *vector_grads,
    )


def solution(mesh):
    rows = P(ALL, None)
    vector = P(ALL)
    in_specs = (
        (rows,) * 8
        + (vector,) * 7
        + (P(),) * 4
        + (P("dp", None), P("dp", None), P(None, ALL, None))
    )
    out_specs = (P(None, ALL, None),) + (rows,) * 8 + (vector,) * 11
    return jax.shard_map(shards, mesh=mesh, in_specs=in_specs, out_specs=out_specs, check_vma=False)
```
